32 devices in a mesh: groups: 2 (over x), dp: 16 (over z, y, core).
Axes of the slice: x: 2, y: 2, z: 4, core: 2. Of those that a mesh axis runs over, the one named last changes fastest.
Arguments:
- query: bfloat16 [8192, 4096], P(('groups', 'dp')), parts along dimension 0, may hold values from -400 to 400
- leaf_key_value: bfloat16 [8192, 1024], P(('groups', 'dp')), parts along dimension 0, may hold values from -6 to 6
- prefix_key_value: bfloat16 [4096, 1024], P(('groups', 'dp')), parts along dimension 0, may hold values from -6 to 6
- d_out: bfloat16 [8192, 4096], P(('groups', 'dp')), parts along dimension 0, may hold values from -6 to 6
- block_owner: int32 [32], P('groups'), parts along dimension 0, may hold values from 0 to 15, each once
- subtree_tokens: int32 [8], P('groups'), parts along dimension 0, may hold values from 256 to 1792, as said below
- leaf_id: int32 [32, 256], P(('groups', 'dp')), parts along dimension 0, may hold values from 0 to 63, never falling along the last dimension, each value on 1 to 128 neighbouring positions
- loss_mask: int32 [8192], P(('groups', 'dp')), parts along dimension 0, may hold values 0 or 1
Outputs:
- attended: bfloat16 [8192, 4096], P(('groups', 'dp')), parts along dimension 0
- d_query: bfloat16 [8192, 4096], P(('groups', 'dp')), parts along dimension 0
- d_leaf_kv: bfloat16 [8192, 1024], P(('groups', 'dp')), parts along dimension 0
- d_prefix_kv: bfloat16 [4096, 1024], P(('groups', 'dp')), parts along dimension 0
The draws below stay inside these ranges and needn't reach their ends.
There are 2 independent parts, one for each index of `groups`. The reference program is written for one: setup_inputs(seed, part) draws one part's arguments, and reference() takes and returns one part's arrays. A program takes and returns all parts, laid end to end along the dimension named above; each array names one. Nothing has to cross between parts.
Inputs may be any that keep to these rules, and one draw needn't show every extreme that they name: `subtree_tokens`: sums to 4096; the smallest is 256 and the largest 7 * 256.
All inputs are finite; a program needn't handle non-finite values. No bound on the sum of `loss_mask` on one device may be relied on, other than what follows from the above.
Results may differ from the reference program's by a relative error of at most 0.029.
Values may be sent and summed in bfloat16 or wider, within the bound.
No kernel may reach another device: no remote copies, remote signals or barrier semaphores. Data moves between devices by JAX's collectives and lax.ppermute only.
A program may use at most 192 MiB of HBM per device.

```python
import math
import jax
import jax.numpy as jnp
import numpy as np
from jax import lax

HEAD_SIZE = 128
HQ = 32
KEY_VALUE_HEADS = 4
GQ = 8
PREFIX_BLOCK_LEN = 128
BLOCKS_PER_PREFIX = 4
TOK_DEV = 256
NPRE = 4
LEAF_TOKEN_COUNT = 4096
N_DP = 16


def draw_query(key, part):
    key = jax.random.fold_in(key, 5)
    first_key = jax.random.fold_in(key, 0)
    values = jax.random.normal(first_key, (LEAF_TOKEN_COUNT, HQ * HEAD_SIZE), jnp.float32)
    return jnp.clip(values, -6.0, 6.0).astype(jnp.bfloat16)


def draw_subtree_tokens(key, part):
    key = jax.random.fold_in(key, 11)
    first_key, second_key = jax.random.split(key)
    half = NPRE // 2
    offsets = jax.random.randint(first_key, (half,), 0, 3 * TOK_DEV + 1).astype(jnp.int32)
    offsets = offsets.at[0].set(3 * TOK_DEV)
    sizes = jnp.concatenate([4 * TOK_DEV + offsets, 4 * TOK_DEV - offsets]).astype(jnp.int32)
    order = jax.random.permutation(second_key, NPRE)
    return sizes[order].astype(jnp.int32)


def place_ends(result, own_key, least, largest):
    extent = result.shape
    place = [jax.random.randint(jax.random.fold_in(own_key, axis), (), 0, extent[axis]) for axis in range(len(extent))]
    result = result.at[tuple(place)].set(least)
    longest = extent.index(max(extent))
    place[longest] = (place[longest] + 1) % extent[longest]
    return result.at[tuple(place)].set(largest)


def level_of(key, dims, pieces, smallest, top_value):
    loudness, own = 1.0, jax.random.fold_in(key, 6)
    for position, shards_of in pieces:
        steps = jnp.exp(jax.random.uniform(jax.random.fold_in(own, position), (shards_of,), jnp.float32, smallest / len(pieces), top_value / len(pieces)))
        loudness = loudness * jnp.repeat(steps, dims[position] // shards_of).reshape([-1 if axis == position else 1 for axis in range(len(dims))])
    return loudness


def length_profile(count, total, reach, skew):
    weights = [(1 << 20) // math.isqrt(standing ** skew) + 1 for standing in range(2, count + 1)]
    surplus, counts = total - reach - (count - 1), [1] * (count - 1)
    while surplus > 0:
        free = [i for i in range(count - 1) if counts[i] < reach]
        whole, left = sum([weights[i] for i in free]), surplus
        for i in free:
            more = min(reach - counts[i], max(1, left * weights[i] // whole), surplus)
            counts[i] = counts[i] + more
            surplus = surplus - more
    return np.array([reach] + counts)


def ragged_sizes(rng, count, total, limit, skew):
    if count == 2:
        one = jax.random.randint(rng, (), max(1, total - limit), min(limit, total - 1) + 1)
        return jnp.stack([one, total - one])
    tallies = jnp.asarray(length_profile(count, total, limit, skew), jnp.int32)
    twos = (count - 1) // 2
    giver, taker = tallies[1:1 + 2 * twos:2], tallies[2:2 + 2 * twos:2]
    room = jnp.minimum(giver - 1, limit - taker)
    moved = jax.random.randint(jax.random.fold_in(rng, 1), (twos,), 0, 1 << 20) % (room + 1)
    tallies = tallies.at[1:1 + 2 * twos:2].set(giver - moved).at[2:2 + 2 * twos:2].set(taker + moved)
    return tallies[jax.random.permutation(jax.random.fold_in(rng, 2), count)]


def centred(own_key, dims, scale, most, cuts=(), held_as=jnp.bfloat16):
    result = jax.random.normal(own_key, dims, jnp.float32) * scale
    if len(cuts) > 0:
        result = level_of(own_key, dims, cuts, -0.22, 0.18) * result
    return jnp.clip(result, min=-most, max=most).astype(held_as)


def setup_inputs(seed: int = 0, part: int = 0) -> dict:
    arg_keys = jax.random.split(jax.random.key(seed), 9)
    part_keys = jax.random.split(jax.random.fold_in(arg_keys[8], part), 9)
    query = draw_query(jax.random.fold_in(jax.random.fold_in(arg_keys[8], part), 71), part)
    leaf_key_value = centred(part_keys[1], (LEAF_TOKEN_COUNT, 2 * KEY_VALUE_HEADS * HEAD_SIZE), 1.0, 6.0, ((0, 16),))
    prefix_key_value = centred(part_keys[2], (N_DP * PREFIX_BLOCK_LEN, 2 * KEY_VALUE_HEADS * HEAD_SIZE), 1.0, 6.0, ((0, 16),))
    d_out = centred(part_keys[3], (LEAF_TOKEN_COUNT, HQ * HEAD_SIZE), 1.0, 6.0, ((0, 16),))
    block_owner = jax.random.permutation(part_keys[4], N_DP).astype(jnp.int32)
    subtree_tokens = draw_subtree_tokens(jax.random.fold_in(jax.random.fold_in(arg_keys[8], part), 71), part)
    leaf_id = jax.vmap(lambda own: jnp.searchsorted(jnp.cumsum(ragged_sizes(own, TOK_DEV // 4, TOK_DEV, TOK_DEV // 2, 2)), jnp.arange(TOK_DEV), side="right"))(jax.random.split(part_keys[6], N_DP)).reshape((N_DP, TOK_DEV)).astype(jnp.int32)
    loss_mask = place_ends((jax.random.randint(part_keys[7], (LEAF_TOKEN_COUNT,), 0, 4) < 3).astype(jnp.int32), jax.random.fold_in(part_keys[7], 1), 0, 1)
    return {"query": query, "leaf_key_value": leaf_key_value, "prefix_key_value": prefix_key_value, "d_out": d_out, "block_owner": block_owner, "subtree_tokens": subtree_tokens, "leaf_id": leaf_id, "loss_mask": loss_mask}


def token_prefix(subtree_tokens, first, count):
    ends = jnp.cumsum(subtree_tokens).astype(jnp.int32)
    positions = first + jnp.arange(count, dtype=jnp.int32)
    return jnp.sum((ends[None, :] <= positions[:, None]).astype(jnp.int32), axis=1).astype(jnp.int32)


def device_pass(query, leaf_key_value, picked_blocks, d_out, loss_mask, prefixes, prefix_pair, leaf):
    count = query.shape[0]
    key_value_width = KEY_VALUE_HEADS * HEAD_SIZE
    scale = HEAD_SIZE ** -0.5
    keys_all = jnp.concatenate([picked_blocks, leaf_key_value], axis=0)
    span = BLOCKS_PER_PREFIX * PREFIX_BLOCK_LEN
    block_set = jnp.arange(2 * span, dtype=jnp.int32) // span
    pre_ok = (prefixes[:, None] == prefix_pair[block_set][None, :]) & ((block_set[None, :] == 0) | (prefix_pair[1] != prefix_pair[0]))
    positions = jnp.arange(count, dtype=jnp.int32)
    loc_ok = (leaf[:, None] == leaf[None, :]) & (prefixes[:, None] == prefixes[None, :]) & (positions[None, :] <= positions[:, None])
    allowed = jnp.concatenate([pre_ok, loc_ok], axis=1)
    gradient = d_out * loss_mask[:, None].astype(jnp.bfloat16)
    outs, d_queries, d_keys, d_values = [], [], [], []
    for head_group in range(KEY_VALUE_HEADS):
        head_query = query[:, head_group * GQ * HEAD_SIZE:(head_group + 1) * GQ * HEAD_SIZE].reshape(count, GQ, HEAD_SIZE).astype(jnp.float32)
        head_keys = keys_all[:, head_group * HEAD_SIZE:(head_group + 1) * HEAD_SIZE].astype(jnp.float32)
        head_values = keys_all[:, key_value_width + head_group * HEAD_SIZE:key_value_width + (head_group + 1) * HEAD_SIZE].astype(jnp.float32)
        head_grad = gradient[:, head_group * GQ * HEAD_SIZE:(head_group + 1) * GQ * HEAD_SIZE].reshape(count, GQ, HEAD_SIZE).astype(jnp.float32)
        scores = jnp.einsum('tjd,kd->jtk', head_query, head_keys) * scale
        scores = jnp.where(allowed[None], scores, jnp.float32(-1e30))
        row_max = jnp.max(scores, axis=-1, keepdims=True)
        weights = jnp.exp(scores - row_max)
        probs = weights / jnp.sum(weights, axis=-1, keepdims=True)
        probs_b = probs.astype(jnp.bfloat16).astype(jnp.float32)
        head_out = jnp.einsum('jtk,kd->tjd', probs_b, head_values).astype(jnp.bfloat16)
        dprob = jnp.einsum('tjd,kd->jtk', head_grad, head_values)
        delta = jnp.sum(head_grad * head_out.astype(jnp.float32), axis=-1).T[:, :, None]
        dscore = (probs * (dprob - delta)).astype(jnp.bfloat16).astype(jnp.float32)
        d_head = (jnp.einsum('jtk,kd->tjd', dscore, head_keys) * scale).astype(jnp.bfloat16)
        d_keys.append(jnp.einsum('jtk,tjd->kd', dscore, head_query) * scale)
        d_values.append(jnp.einsum('jtk,tjd->kd', probs_b, head_grad))
        outs.append(head_out.reshape(count, GQ * HEAD_SIZE))
        d_queries.append(d_head.reshape(count, GQ * HEAD_SIZE))
    d_all = jnp.concatenate(d_keys + d_values, axis=1)
    return (jnp.concatenate(outs, axis=1), jnp.concatenate(d_queries, axis=1),
            d_all[2 * span:].astype(jnp.bfloat16), d_all[:2 * span])


def reference(query, leaf_key_value, prefix_key_value, d_out, block_owner, subtree_tokens, leaf_id, loss_mask):
    table = block_owner.reshape(NPRE, BLOCKS_PER_PREFIX)
    block_list = prefix_key_value.reshape(N_DP, PREFIX_BLOCK_LEN, 2 * KEY_VALUE_HEADS * HEAD_SIZE)

    def per_device(loop_carry, device):
        first = (device * TOK_DEV).astype(jnp.int32)

        def piece(array):
            return lax.dynamic_slice_in_dim(array, first, TOK_DEV, 0)

        prefixes = token_prefix(subtree_tokens, first, TOK_DEV)
        prefix_pair = jnp.stack([prefixes[0], prefixes[-1]]).astype(jnp.int32)
        rows_of_block = table[prefix_pair].reshape(-1).astype(jnp.int32)
        picked_blocks = block_list[rows_of_block].reshape(2 * BLOCKS_PER_PREFIX * PREFIX_BLOCK_LEN, 2 * KEY_VALUE_HEADS * HEAD_SIZE)
        out, d_query, d_leaf, picked_gradient = device_pass(piece(query), piece(leaf_key_value), picked_blocks, piece(d_out),
                                                     piece(loss_mask), prefixes, prefix_pair, leaf_id[device])
        loop_carry = loop_carry.at[rows_of_block].add(picked_gradient.reshape(2 * BLOCKS_PER_PREFIX, PREFIX_BLOCK_LEN, 2 * KEY_VALUE_HEADS * HEAD_SIZE))
        return loop_carry, (out, d_query, d_leaf)

    start_row = jnp.zeros((N_DP, PREFIX_BLOCK_LEN, 2 * KEY_VALUE_HEADS * HEAD_SIZE), jnp.float32)
    total_count, (outs, d_queries, leaf_gradient) = lax.scan(per_device, start_row, jnp.arange(N_DP, dtype=jnp.int32))
    return (outs.reshape(LEAF_TOKEN_COUNT, HQ * HEAD_SIZE), d_queries.reshape(LEAF_TOKEN_COUNT, HQ * HEAD_SIZE),
            leaf_gradient.reshape(LEAF_TOKEN_COUNT, 2 * KEY_VALUE_HEADS * HEAD_SIZE), total_count.reshape(N_DP * PREFIX_BLOCK_LEN, 2 * KEY_VALUE_HEADS * HEAD_SIZE).astype(jnp.bfloat16))
```

```python
import functools

import jax
import jax.numpy as jnp
from jax import lax
from jax.experimental import pallas as pl
from jax.experimental.pallas import tpu as pltpu
from jax.sharding import PartitionSpec as P

HEAD_SIZE = 128
KEY_VALUE_HEADS = 4
GQ = 8
SCALE = HEAD_SIZE ** (-0.5)
LOG2E = 1.4426950408889634


def dot(a, b, contract):
    return lax.dot_general(a, b, (contract, ((), ())), preferred_element_type=jnp.float32)


def attention_kernel(
    owner_ref, tokens_ref, device_ref,
    q_ref, g_ref, leaf_kv_ref, leaf_ref, mask_ref, whole_ref,
    out_ref, dq_ref, dleaf_ref, dpre_ref,
    kv, kcat, vcat, kcat_t, vcat_t, bias, q_pick, g_pick, dk_sum, dv_sum, sems,
    *, prompts, per_prefix, block_len,
):
    head = pl.program_id(0)
    group = head // GQ
    within = lax.rem(head, GQ)
    count = q_ref.shape[0]
    span = per_prefix * block_len
    width = KEY_VALUE_HEADS * HEAD_SIZE

    first = device_ref[0] * count
    last = first + (count - 1)
    end = jnp.int32(0)
    pair_first = jnp.int32(0)
    pair_last = jnp.int32(0)
    border = jnp.int32(2**30)
    for p in range(prompts):
        end = end + tokens_ref[p]
        pair_first = pair_first + (end <= first).astype(jnp.int32)
        pair_last = pair_last + (end <= last).astype(jnp.int32)
        border = jnp.where(end > first, jnp.minimum(border, end), border)
    border = border - first

    def block_row(side, j):
        prefix = pair_first if side == 0 else pair_last
        return owner_ref[prefix * per_prefix + j]

    @pl.when(head == 0)
    def _():
        copies = []
        for side in range(2):
            for j in range(per_prefix):
                n = side * per_prefix + j
                rows = pl.ds(pl.multiple_of(block_row(side, j) * block_len, block_len), block_len)
                copy = pltpu.make_async_copy(
                    whole_ref.at[rows, :], kv.at[pl.ds(n * block_len, block_len), :], sems.at[n]
                )
                copy.start()
                copies.append(copy)
        leaf_row = jnp.broadcast_to(leaf_ref[...], (count, count))
        leaf_col = leaf_row.T
        key_at = lax.broadcasted_iota(jnp.int32, (count, count), 0)
        token_at = lax.broadcasted_iota(jnp.int32, (count, count), 1)
        same = (leaf_row == leaf_col) & (key_at <= token_at)
        same = same & ((key_at < border) == (token_at < border))
        bias[...] = jnp.where(same, 0.0, -1e30).astype(jnp.float32)
        mask_col = jnp.broadcast_to(mask_ref[...], (count, count)).T.astype(jnp.float32)
        in_first = key_at < border
        left = token_at < HEAD_SIZE
        pick = (in_first == left).astype(jnp.float32)
        q_pick[...] = pick.astype(jnp.bfloat16)
        g_pick[...] = (pick * mask_col).astype(jnp.bfloat16)
        dpre_ref[...] = jnp.zeros_like(dpre_ref)
        for copy in copies:
            copy.wait()

    key_cols = pl.ds(pl.multiple_of(group * HEAD_SIZE, HEAD_SIZE), HEAD_SIZE)
    value_cols = pl.ds(pl.multiple_of(width + group * HEAD_SIZE, HEAD_SIZE), HEAD_SIZE)

    @pl.when(within == 0)
    def _():
        for cat, cat_t, cols in ((kcat, kcat_t, key_cols), (vcat, vcat_t, value_cols)):
            for side in range(2):
                lanes = slice(side * HEAD_SIZE, (side + 1) * HEAD_SIZE)
                cat[0:span, lanes] = kv[side * span:(side + 1) * span, cols]
                cat[span:, lanes] = leaf_kv_ref[:, cols]
            cat_t[...] = cat[...].T
        dk_sum[...] = jnp.zeros_like(dk_sum)
        dv_sum[...] = jnp.zeros_like(dv_sum)

    q = q_ref[...]
    g = g_ref[...]
    q2 = jnp.concatenate([q, q], axis=1) * q_pick[...]
    g2 = jnp.concatenate([g, g], axis=1) * g_pick[...]
    first_side = lax.broadcasted_iota(jnp.int32, (HEAD_SIZE, count), 1) < border

    scores = dot(kcat[...], q2, ((1,), (1,))) * (SCALE * LOG2E)
    dprob = dot(vcat[...], g2, ((1,), (1,)))
    s_pre = scores[:span]
    s_leaf = scores[span:] + bias[...]
    top = jnp.maximum(
        jnp.max(s_pre, axis=0, keepdims=True), jnp.max(s_leaf, axis=0, keepdims=True)
    )
    weights = jnp.concatenate([jnp.exp2(s_pre - top), jnp.exp2(s_leaf - top)], axis=0)
    total = jnp.sum(weights, axis=0, keepdims=True)
    probs = weights * (1.0 / total)
    probs_b = probs.astype(jnp.bfloat16)
    delta = jnp.sum(probs * dprob, axis=0, keepdims=True)
    dscore = (probs * (dprob - delta)).astype(jnp.bfloat16)

    out_t = dot(vcat_t[...], probs_b, ((1,), (0,)))
    out_t = jnp.where(first_side, out_t[:HEAD_SIZE], out_t[HEAD_SIZE:])
    out_ref[...] = out_t.T.astype(jnp.bfloat16)
    dq_t = dot(kcat_t[...], dscore, ((1,), (0,)))
    dq_t = jnp.where(first_side, dq_t[:HEAD_SIZE], dq_t[HEAD_SIZE:]) * SCALE
    dq_ref[...] = dq_t.T.astype(jnp.bfloat16)
    dk_sum[...] += dot(dscore, q2, ((1,), (0,)))
    dv_sum[...] += dot(probs_b, g2, ((1,), (0,)))

    @pl.when(within == GQ - 1)
    def _():
        for total_ref, cols, factor in ((dk_sum, key_cols, SCALE), (dv_sum, value_cols, 1.0)):
            leaf = (total_ref[span:, :HEAD_SIZE] + total_ref[span:, HEAD_SIZE:]) * factor
            dleaf_ref[:, cols] = leaf.astype(jnp.bfloat16)
            for side in range(2):
                lanes = slice(side * HEAD_SIZE, (side + 1) * HEAD_SIZE)
                for j in range(per_prefix):
                    value = total_ref[j * block_len:(j + 1) * block_len, lanes] * factor
                    value = value.astype(dpre_ref.dtype)
                    where = block_row(side, j)
                    if side == 1:
                        value = value + dpre_ref[where, :, cols]
                    dpre_ref[where, :, cols] = value


def attention(owner, tokens, device, q, g, leaf_kv, leaf, mask, whole, devices):
    count = q.shape[0]
    block_len = whole.shape[0] // devices
    prompts = tokens.shape[0]
    per_prefix = owner.shape[0] // prompts
    span = per_prefix * block_len
    keys = span + count
    heads = KEY_VALUE_HEADS * GQ
    bf16, f32 = jnp.bfloat16, jnp.float32
    slab = pl.BlockSpec((count, HEAD_SIZE), lambda h, *_: (0, h))

    def full(shape):
        return pl.BlockSpec(shape, lambda h, *_: (0,) * len(shape))

    dpre_shape = (devices, block_len, whole.shape[1])
    return pl.pallas_call(
        functools.partial(
            attention_kernel, prompts=prompts, per_prefix=per_prefix, block_len=block_len
        ),
        grid_spec=pltpu.PrefetchScalarGridSpec(
            num_scalar_prefetch=3,
            grid=(heads,),
            in_specs=[
                slab, slab, full(leaf_kv.shape), full(leaf.shape), full(mask.shape),
                pl.BlockSpec(memory_space=pl.ANY),
            ],
            out_specs=[slab, slab, full(leaf_kv.shape), full(dpre_shape)],
            scratch_shapes=[
                pltpu.VMEM((2 * span, whole.shape[1]), bf16),
                pltpu.VMEM((keys, 2 * HEAD_SIZE), bf16),
                pltpu.VMEM((keys, 2 * HEAD_SIZE), bf16),
                pltpu.VMEM((2 * HEAD_SIZE, keys), bf16),
                pltpu.VMEM((2 * HEAD_SIZE, keys), bf16),
                pltpu.VMEM((count, count), f32),
                pltpu.VMEM((count, 2 * HEAD_SIZE), bf16),
                pltpu.VMEM((count, 2 * HEAD_SIZE), bf16),
                pltpu.VMEM((keys, 2 * HEAD_SIZE), f32),
                pltpu.VMEM((keys, 2 * HEAD_SIZE), f32),
                pltpu.SemaphoreType.DMA((2 * per_prefix,)),
            ],
        ),
        out_shape=[
            jax.ShapeDtypeStruct(q.shape, bf16),
            jax.ShapeDtypeStruct(q.shape, bf16),
            jax.ShapeDtypeStruct(leaf_kv.shape, bf16),
            jax.ShapeDtypeStruct(dpre_shape, bf16),
        ],
        compiler_params=pltpu.CompilerParams(
            vmem_limit_bytes=48 * 2**20, dimension_semantics=("arbitrary",)
        ),
        cost_estimate=pl.CostEstimate(
            flops=heads * 6 * 2 * keys * 256 * 256, bytes_accessed=16 * 2**20,
            transcendentals=heads * keys * count,
        ),
    )(owner, tokens, device, q, g, leaf_kv, leaf, mask, whole)


def shards(
    query, leaf_key_value, prefix_key_value, d_out, block_owner, subtree_tokens, leaf_id, loss_mask
):
    devices = lax.axis_size("dp")
    device = lax.axis_index("dp").astype(jnp.int32).reshape(1)
    whole = lax.all_gather(prefix_key_value, "dp", axis=0, tiled=True)
    attended, d_query, d_leaf, partial = attention(
        block_owner, subtree_tokens, device, query, d_out, leaf_key_value,
        leaf_id, loss_mask.reshape(1, -1), whole, devices,
    )
    mine = lax.psum_scatter(partial, "dp", scatter_dimension=0, tiled=True)
    return attended, d_query, d_leaf, mine.reshape(prefix_key_value.shape)


def solution(mesh):
    rows = P(("groups", "dp"), None)
    in_specs = (rows, rows, rows, rows, P("groups"), P("groups"), rows, P(("groups", "dp")))
    return jax.shard_map(
        shards, mesh=mesh, in_specs=in_specs, out_specs=(rows,) * 4, check_vma=False
    )
```

```python
import functools

import jax
import jax.numpy as jnp
from jax import lax
from jax.experimental import pallas as pl
from jax.experimental.pallas import tpu as pltpu
from jax.sharding import PartitionSpec as P

HEAD_SIZE = 128
KEY_VALUE_HEADS = 4
GQ = 8
SCALE = HEAD_SIZE ** (-0.5)
LOG2E = 1.4426950408889634


def dot(a, b, contract):
    return lax.dot_general(a, b, (contract, ((), ())), preferred_element_type=jnp.float32)

CHUNKS = 1


def attention_kernel(
    owner_ref, tokens_ref, place_ref,
    q_ref, g_ref, leaf_k_ref, leaf_v_ref, leaf_ref, mask_ref, own_ref, far_ref, *rest,
    prompts, per_prefix, block_len, planes, ranks, chained,
):
    (out_ref, dq_ref, dleaf_ref, own_sum_ref, far_sum_ref,
     kv, kcat, vcat, kcat_t, vcat_t, bias, q_pick, g_pick, dk_sum, dv_sum, sems) = rest[2 * chained:]
    head = pl.program_id(0)
    group = head // GQ
    within = lax.rem(head, GQ)
    count = q_ref.shape[0]
    span = per_prefix * block_len
    half = own_ref.shape[1] // 2

    place = place_ref[0]
    first = place * count
    last = first + (count - 1)
    end = jnp.int32(0)
    pair_first = jnp.int32(0)
    pair_last = jnp.int32(0)
    border = jnp.int32(2**30)
    for p in range(prompts):
        end = end + tokens_ref[p]
        pair_first = pair_first + (end <= first).astype(jnp.int32)
        pair_last = pair_last + (end <= last).astype(jnp.int32)
        border = jnp.where(end > first, jnp.minimum(border, end), border)
    border = border - first

    def block_place(side, j):
        prefix = pair_first if side == 0 else pair_last
        owner = owner_ref[prefix * per_prefix + j]
        same_core = lax.rem(owner, 2) == lax.rem(place, 2)
        row = lax.rem(owner // 2 + place // 2, ranks)
        ahead = lax.rem(owner // (2 * ranks) + planes - place // (2 * ranks), planes)
        return same_core, row, ahead

    @pl.when(head == 0)
    def _():
        for side in range(2):
            for j in range(per_prefix):
                n = side * per_prefix + j
                same_core, row, ahead = block_place(side, j)
                slot = row * planes + lax.rem(planes - ahead, planes)
                rows = pl.ds(pl.multiple_of(slot * block_len, block_len), block_len)
                target = kv.at[pl.ds(n * block_len, block_len), :]

                @pl.when(same_core)
                def _():
                    pltpu.make_async_copy(own_ref.at[rows, :], target, sems.at[n]).start()

                @pl.when(jnp.logical_not(same_core))
                def _():
                    pltpu.make_async_copy(far_ref.at[rows, :], target, sems.at[n]).start()

        leaf_row = jnp.broadcast_to(leaf_ref[...], (count, count))
        leaf_col = leaf_row.T
        key_at = lax.broadcasted_iota(jnp.int32, (count, count), 0)
        token_at = lax.broadcasted_iota(jnp.int32, (count, count), 1)
        same = (leaf_row == leaf_col) & (key_at <= token_at)
        same = same & ((key_at < border) == (token_at < border))
        bias[...] = jnp.where(same, 0.0, -1e30).astype(jnp.float32)
        mask_col = jnp.broadcast_to(mask_ref[...], (count, count)).T.astype(jnp.float32)
        in_first = key_at < border
        left = token_at < HEAD_SIZE
        pick = (in_first == left).astype(jnp.float32)
        q_pick[...] = pick.astype(jnp.bfloat16)
        g_pick[...] = (pick * mask_col).astype(jnp.bfloat16)
        own_sum_ref[...] = jnp.zeros_like(own_sum_ref)
        far_sum_ref[...] = jnp.zeros_like(far_sum_ref)
        for n in range(2 * per_prefix):
            target = kv.at[pl.ds(n * block_len, block_len), :]
            pltpu.make_async_copy(own_ref.at[pl.ds(0, block_len), :], target, sems.at[n]).wait()

    key_cols = pl.ds(pl.multiple_of(group * HEAD_SIZE, HEAD_SIZE), HEAD_SIZE)
    value_cols = pl.ds(pl.multiple_of(half + group * HEAD_SIZE, HEAD_SIZE), HEAD_SIZE)

    @pl.when(within == 0)
    def _():
        for cat, cat_t, cols, leaf in (
            (kcat, kcat_t, key_cols, leaf_k_ref), (vcat, vcat_t, value_cols, leaf_v_ref)
        ):
            for side in range(2):
                lanes = slice(side * HEAD_SIZE, (side + 1) * HEAD_SIZE)
                cat[0:span, lanes] = kv[side * span:(side + 1) * span, cols]
                cat[span:, lanes] = leaf[...]
            cat_t[...] = cat[...].T
        dk_sum[...] = jnp.zeros_like(dk_sum)
        dv_sum[...] = jnp.zeros_like(dv_sum)

    q = q_ref[...]
    g = g_ref[...]
    q2 = jnp.concatenate([q, q], axis=1) * q_pick[...]
    g2 = jnp.concatenate([g, g], axis=1) * g_pick[...]
    first_side = lax.broadcasted_iota(jnp.int32, (HEAD_SIZE, count), 1) < border

    scores = dot(kcat[...], q2, ((1,), (1,))) * (SCALE * LOG2E)
    dprob = dot(vcat[...], g2, ((1,), (1,)))
    s_pre = scores[:span]
    s_leaf = scores[span:] + bias[...]
    top = jnp.maximum(
        jnp.max(s_pre, axis=0, keepdims=True), jnp.max(s_leaf, axis=0, keepdims=True)
    )
    weights = jnp.concatenate([jnp.exp2(s_pre - top), jnp.exp2(s_leaf - top)], axis=0)
    total = jnp.sum(weights, axis=0, keepdims=True)
    probs = weights * (1.0 / total)
    probs_b = probs.astype(jnp.bfloat16)
    delta = jnp.sum(probs * dprob, axis=0, keepdims=True)
    dscore = (probs * (dprob - delta)).astype(jnp.bfloat16)

    out_t = dot(vcat_t[...], probs_b, ((1,), (0,)))
    out_t = jnp.where(first_side, out_t[:HEAD_SIZE], out_t[HEAD_SIZE:])
    out_ref[...] = out_t.T.astype(jnp.bfloat16)
    dq_t = dot(kcat_t[...], dscore, ((1,), (0,)))
    dq_t = jnp.where(first_side, dq_t[:HEAD_SIZE], dq_t[HEAD_SIZE:]) * SCALE
    dq_ref[...] = dq_t.T.astype(jnp.bfloat16)
    dk_sum[...] += dot(dscore, q2, ((1,), (0,)))
    dv_sum[...] += dot(probs_b, g2, ((1,), (0,)))

    @pl.when(within == GQ - 1)
    def _():
        for total_ref, cols, factor in ((dk_sum, key_cols, SCALE), (dv_sum, value_cols, 1.0)):
            leaf = (total_ref[span:, :HEAD_SIZE] + total_ref[span:, HEAD_SIZE:]) * factor
            dleaf_ref[:, cols] = leaf.astype(jnp.bfloat16)
            for side in range(2):
                lanes = slice(side * HEAD_SIZE, (side + 1) * HEAD_SIZE)
                for j in range(per_prefix):
                    value = total_ref[j * block_len:(j + 1) * block_len, lanes] * factor
                    value = value.astype(jnp.bfloat16)
                    same_core, row, ahead = block_place(side, j)
                    slot = row * planes + ahead

                    @pl.when(same_core)
                    def _():
                        own_sum_ref[slot, :, cols] += value

                    @pl.when(jnp.logical_not(same_core))
                    def _():
                        far_sum_ref[slot, :, cols] += value


def attention(
    chunk, owner, tokens, place, q, g, leaf_kv, leaf, mask, own, far, earlier, planes, ranks
):
    count = q.shape[0]
    slots = planes * ranks
    block_len = own.shape[0] // slots
    prompts = tokens.shape[0]
    per_prefix = owner.shape[0] // prompts
    span = per_prefix * block_len
    keys = span + count
    width = own.shape[1]
    groups = width // (2 * HEAD_SIZE)
    heads = groups * GQ
    bf16, f32 = jnp.bfloat16, jnp.float32
    slab = pl.BlockSpec((count, HEAD_SIZE), lambda h, *_: (0, chunk * heads + h))
    leaf_k = pl.BlockSpec((count, HEAD_SIZE), lambda h, *_: (0, chunk * groups + h // GQ))
    leaf_v = pl.BlockSpec(
        (count, HEAD_SIZE), lambda h, *_: (0, KEY_VALUE_HEADS + chunk * groups + h // GQ)
    )
    anywhere = pl.BlockSpec(memory_space=pl.ANY)

    def full(shape):
        return pl.BlockSpec(shape, lambda h, *_: (0,) * len(shape))

    sum_shape = (slots, block_len, width)
    chained = len(earlier) > 0
    return pl.pallas_call(
        functools.partial(
            attention_kernel, prompts=prompts, per_prefix=per_prefix, block_len=block_len,
            planes=planes, ranks=ranks, chained=chained,
        ),
        grid_spec=pltpu.PrefetchScalarGridSpec(
            num_scalar_prefetch=3,
            grid=(heads,),
            in_specs=[
                slab, slab, leaf_k, leaf_v, full(leaf.shape), full(mask.shape), anywhere, anywhere,
            ] + [anywhere] * len(earlier),
            out_specs=[slab, slab, full((count, width)), full(sum_shape), full(sum_shape)],
            scratch_shapes=[
                pltpu.VMEM((2 * span, width), bf16),
                pltpu.VMEM((keys, 2 * HEAD_SIZE), bf16),
                pltpu.VMEM((keys, 2 * HEAD_SIZE), bf16),
                pltpu.VMEM((2 * HEAD_SIZE, keys), bf16),
                pltpu.VMEM((2 * HEAD_SIZE, keys), bf16),
                pltpu.VMEM((count, count), f32),
                pltpu.VMEM((count, 2 * HEAD_SIZE), bf16),
                pltpu.VMEM((count, 2 * HEAD_SIZE), bf16),
                pltpu.VMEM((keys, 2 * HEAD_SIZE), f32),
                pltpu.VMEM((keys, 2 * HEAD_SIZE), f32),
                pltpu.SemaphoreType.DMA((2 * per_prefix,)),
            ],
        ),
        out_shape=[
            jax.ShapeDtypeStruct(q.shape, bf16),
            jax.ShapeDtypeStruct(q.shape, bf16),
            jax.ShapeDtypeStruct((count, width), bf16),
            jax.ShapeDtypeStruct(sum_shape, bf16),
            jax.ShapeDtypeStruct(sum_shape, bf16),
        ],
        input_output_aliases={11: 0, 12: 1} if chained else {},
        compiler_params=pltpu.CompilerParams(
            vmem_limit_bytes=60 * 2**20, dimension_semantics=("arbitrary",)
        ),
        cost_estimate=pl.CostEstimate(
            flops=heads * 6 * 2 * keys * 256 * 256, bytes_accessed=16 * 2**20 // CHUNKS,
            transcendentals=heads * keys * count,
        ),
    )(owner, tokens, place, q, g, leaf_kv, leaf_kv, leaf, mask, own, far, *earlier)


def shards(
    query, leaf_key_value, prefix_key_value, d_out, block_owner, subtree_tokens, leaf_id, loss_mask
):
    devices = lax.axis_size("dp")
    ranks = 2 if devices == 16 else 1
    planes = devices // (2 * ranks)
    place = lax.axis_index("dp").astype(jnp.int32).reshape(1)
    mask = loss_mask.reshape(1, -1)
    f32 = jnp.float32

    def index(plane, rank, core):
        return (plane % planes * ranks + rank % ranks) * 2 + core % 2

    def send(array, plane_step, rank_step, core_step):
        pairs = [
            (index(p, r, c), index(p + plane_step, r + rank_step, c + core_step))
            for p in range(planes) for r in range(ranks) for c in range(2)
        ]
        return lax.ppermute(array, "dp", pairs)

    groups = KEY_VALUE_HEADS // CHUNKS
    step = groups * HEAD_SIZE
    middle = KEY_VALUE_HEADS * HEAD_SIZE

    def gather(chunk):
        mine = jnp.concatenate(
            [prefix_key_value[:, chunk * step:(chunk + 1) * step],
             prefix_key_value[:, middle + chunk * step:middle + (chunk + 1) * step]], axis=1
        ) if CHUNKS > 1 else prefix_key_value
        near = [mine] + [send(mine, k, 0, 0) for k in range(1, planes)]
        near = jnp.concatenate(near, axis=0)
        if ranks == 2:
            near = jnp.concatenate([near, send(near, 0, 1, 0)], axis=0)
        return near, send(near, 0, 0, 1)

    def reduce(own, far):
        total = own.astype(f32) + send(far, 0, 0, 1).astype(f32)
        if ranks == 2:
            away = send(total[planes:].astype(jnp.bfloat16), 0, 1, 0)
            total = total[:planes] + away.astype(f32)
        mine = total[0]
        for k in range(1, planes):
            mine = mine + send(total[k].astype(jnp.bfloat16), k, 0, 0).astype(f32)
        return mine.astype(jnp.bfloat16)

    blocks = [gather(chunk) for chunk in range(CHUNKS)]
    d_leaf, d_prefix, earlier = [], [], ()
    for chunk in range(CHUNKS):
        own, far = blocks[chunk]
        attended, d_query, leaf_part, own_sum, far_sum = attention(
            chunk, block_owner, subtree_tokens, place, query, d_out, leaf_key_value, leaf_id, mask,
            own, far, earlier, planes, ranks,
        )
        earlier = (attended, d_query)
        d_leaf.append(leaf_part)
        d_prefix.append(reduce(own_sum, far_sum))

    def join(parts):
        if CHUNKS == 1:
            return parts[0]
        return jnp.concatenate([p[:, :step] for p in parts] + [p[:, step:] for p in parts], axis=1)

    return attended, d_query, join(d_leaf), join(d_prefix)


def solution(mesh):
    rows = P(("groups", "dp"), None)
    in_specs = (rows, rows, rows, rows, P("groups"), P("groups"), rows, P(("groups", "dp")))
    return jax.shard_map(
        shards, mesh=mesh, in_specs=in_specs, out_specs=(rows,) * 4, check_vma=False
    )
```

```python
import functools

import jax
import jax.numpy as jnp
from jax import lax
from jax.experimental import pallas as pl
from jax.experimental.pallas import tpu as pltpu
from jax.sharding import PartitionSpec as P

HEAD_SIZE = 128
KEY_VALUE_HEADS = 4
GQ = 8
SCALE = HEAD_SIZE ** (-0.5)
LOG2E = 1.4426950408889634


def dot(a, b, contract):
    return lax.dot_general(a, b, (contract, ((), ())), preferred_element_type=jnp.float32)

CHUNKS = 2
PAIR = 2
PIECE = 32


def attention_kernel(
    owner_ref, tokens_ref, place_ref,
    q_ref, g_ref, leaf_k_ref, leaf_v_ref, leaf_ref, mask_ref, own_ref, far_ref, *rest,
    prompts, per_prefix, block_len, planes, ranks, chained, steps,
):
    (out_ref, dq_ref, dleaf_ref, own_sum_ref, far_sum_ref,
     kv, kcat, vcat, kcat_t, vcat_t, bias, q_pick, g_pick, q2, g2, scores, dprob, probs_b, dscore,
     dk_sum, dv_sum, sems) = rest[2 * chained:]
    step = pl.program_id(0)
    per_group = GQ // PAIR
    count = q_ref.shape[0]
    columns = PAIR * count
    span = per_prefix * block_len
    keys = span + count
    half = own_ref.shape[1] // 2

    place = place_ref[0]
    first = place * count
    last = first + (count - 1)
    end = jnp.int32(0)
    pair_first = jnp.int32(0)
    pair_last = jnp.int32(0)
    border = jnp.int32(2**30)
    for p in range(prompts):
        end = end + tokens_ref[p]
        pair_first = pair_first + (end <= first).astype(jnp.int32)
        pair_last = pair_last + (end <= last).astype(jnp.int32)
        border = jnp.where(end > first, jnp.minimum(border, end), border)
    border = border - first

    def block_place(side, j):
        prefix = pair_first if side == 0 else pair_last
        owner = owner_ref[prefix * per_prefix + j]
        same_core = lax.rem(owner, 2) == lax.rem(place, 2)
        row = lax.rem(owner // 2 + place // 2, ranks)
        ahead = lax.rem(owner // (2 * ranks) + planes - place // (2 * ranks), planes)
        return same_core, row, ahead

    def key_columns(group):
        return pl.ds(pl.multiple_of(group * HEAD_SIZE, HEAD_SIZE), HEAD_SIZE)

    def value_columns(group):
        return pl.ds(pl.multiple_of(half + group * HEAD_SIZE, HEAD_SIZE), HEAD_SIZE)

    @pl.when(step == 0)
    def _():
        for side in range(2):
            for j in range(per_prefix):
                n = side * per_prefix + j
                same_core, row, ahead = block_place(side, j)
                slot = row * planes + lax.rem(planes - ahead, planes)
                rows = pl.ds(pl.multiple_of(slot * block_len, block_len), block_len)
                target = kv.at[pl.ds(n * block_len, block_len), :]

                @pl.when(same_core)
                def _():
                    pltpu.make_async_copy(own_ref.at[rows, :], target, sems.at[n]).start()

                @pl.when(jnp.logical_not(same_core))
                def _():
                    pltpu.make_async_copy(far_ref.at[rows, :], target, sems.at[n]).start()

        leaf_row = jnp.broadcast_to(leaf_ref[...], (count, count))
        leaf_col = leaf_row.T
        key_at = lax.broadcasted_iota(jnp.int32, (count, count), 0)
        token_at = lax.broadcasted_iota(jnp.int32, (count, count), 1)
        same = (leaf_row == leaf_col) & (key_at <= token_at)
        same = same & ((key_at < border) == (token_at < border))
        allowed_bias = jnp.where(same, 0.0, -1e30).astype(jnp.float32)
        mask_col = jnp.broadcast_to(mask_ref[...], (count, count)).T.astype(jnp.float32)
        in_first = key_at < border
        left = token_at < HEAD_SIZE
        pick = (in_first == left).astype(jnp.float32)
        q_pick[...] = pick.astype(jnp.bfloat16)
        g_pick[...] = (pick * mask_col).astype(jnp.bfloat16)
        for n in range(PAIR):
            bias[:, n * count:(n + 1) * count] = allowed_bias
        own_sum_ref[...] = jnp.zeros_like(own_sum_ref)
        far_sum_ref[...] = jnp.zeros_like(far_sum_ref)
        dk_sum[...] = jnp.zeros_like(dk_sum)
        dv_sum[...] = jnp.zeros_like(dv_sum)
        for n in range(2 * per_prefix):
            target = kv.at[pl.ds(n * block_len, block_len), :]
            pltpu.make_async_copy(own_ref.at[pl.ds(0, block_len), :], target, sems.at[n]).wait()

    new_group = lax.rem(step, per_group) == 0

    @pl.when(new_group & (step < steps))
    def _():
        group = step // per_group
        for cat, cols, leaf in (
            (kcat, key_columns(group), leaf_k_ref), (vcat, value_columns(group), leaf_v_ref)
        ):
            for side in range(2):
                lanes = slice(side * HEAD_SIZE, (side + 1) * HEAD_SIZE)
                cat[0:span, lanes] = kv[side * span:(side + 1) * span, cols]
                cat[span:, lanes] = leaf[...]

    def later_products():
        token_at = lax.rem(lax.broadcasted_iota(jnp.int32, (HEAD_SIZE, columns), 1), count)
        first_side = token_at < border
        for source, cat_t, factor, target in (
            (probs_b, vcat_t, 1.0, out_ref), (dscore, kcat_t, SCALE, dq_ref)
        ):
            both = dot(cat_t[...], source[...], ((1,), (0,)))
            mine = jnp.where(first_side, both[:HEAD_SIZE], both[HEAD_SIZE:])
            if factor != 1.0:
                mine = mine * factor
            for n in range(PAIR):
                lanes = slice(n * HEAD_SIZE, (n + 1) * HEAD_SIZE)
                target[:, lanes] = mine[:, n * count:(n + 1) * count].T.astype(jnp.bfloat16)
        dk_sum[...] += dot(dscore[...], q2[...], ((1,), (0,)))
        dv_sum[...] += dot(probs_b[...], g2[...], ((1,), (0,)))

    def first_products():
        new_q, new_g = [], []
        for n in range(PAIR):
            q = q_ref[:, n * HEAD_SIZE:(n + 1) * HEAD_SIZE]
            g = g_ref[:, n * HEAD_SIZE:(n + 1) * HEAD_SIZE]
            new_q.append(jnp.concatenate([q, q], axis=1) * q_pick[...])
            new_g.append(jnp.concatenate([g, g], axis=1) * g_pick[...])
        new_q = jnp.concatenate(new_q, axis=0)
        new_g = jnp.concatenate(new_g, axis=0)
        scores[...] = dot(kcat[...], new_q, ((1,), (1,)))
        dprob[...] = dot(vcat[...], new_g, ((1,), (1,)))
        return new_q, new_g

    def softmax(new_q, new_g):
        def fold(value, op):
            value = value.reshape(PIECE // 8, 8, columns)
            total = value[0]
            for n in range(1, PIECE // 8):
                total = op(total, value[n])
            return total

        def score_piece(at):
            value = scores[at:at + PIECE, :]
            if at >= span:
                value = value + bias[at - span:at - span + PIECE, :]
            return value

        top = None
        for at in range(0, keys, PIECE):
            piece = fold(score_piece(at), jnp.maximum)
            top = piece if top is None else jnp.maximum(top, piece)
        top = jnp.max(top, axis=0, keepdims=True)
        total = jnp.zeros((8, columns), jnp.float32)
        delta = jnp.zeros((8, columns), jnp.float32)
        for at in range(0, keys, PIECE):
            weight = jnp.exp2((score_piece(at) - top) * (SCALE * LOG2E))
            scores[at:at + PIECE, :] = weight
            total = total + fold(weight, jnp.add)
            delta = delta + fold(weight * dprob[at:at + PIECE, :], jnp.add)
        inverse = 1.0 / jnp.sum(total, axis=0, keepdims=True)
        delta = jnp.sum(delta, axis=0, keepdims=True) * inverse
        for at in range(0, keys, PIECE):
            probs = scores[at:at + PIECE, :] * inverse
            probs_b[at:at + PIECE, :] = probs.astype(jnp.bfloat16)
            dscore[at:at + PIECE, :] = (probs * (dprob[at:at + PIECE, :] - delta)).astype(jnp.bfloat16)
        q2[...] = new_q
        g2[...] = new_g

    @pl.when(step == 0)
    def _():
        softmax(*first_products())

    @pl.when((step > 0) & (step < steps))
    def _():
        new = first_products()
        later_products()
        softmax(*new)

    @pl.when(step == steps)
    def _():
        later_products()

    @pl.when(new_group & (step > 0))
    def _():
        group = step // per_group - 1
        for total_ref, cols, factor in (
            (dk_sum, key_columns(group), SCALE), (dv_sum, value_columns(group), 1.0)
        ):
            leaf = (total_ref[span:, :HEAD_SIZE] + total_ref[span:, HEAD_SIZE:]) * factor
            dleaf_ref[:, cols] = leaf.astype(jnp.bfloat16)
            for side in range(2):
                lanes = slice(side * HEAD_SIZE, (side + 1) * HEAD_SIZE)
                for j in range(per_prefix):
                    value = total_ref[j * block_len:(j + 1) * block_len, lanes] * factor
                    value = value.astype(jnp.bfloat16)
                    same_core, row, ahead = block_place(side, j)
                    slot = row * planes + ahead

                    @pl.when(same_core)
                    def _():
                        own_sum_ref[slot, :, cols] += value

                    @pl.when(jnp.logical_not(same_core))
                    def _():
                        far_sum_ref[slot, :, cols] += value
        dk_sum[...] = jnp.zeros_like(dk_sum)
        dv_sum[...] = jnp.zeros_like(dv_sum)

    @pl.when(new_group & (step < steps))
    def _():
        kcat_t[...] = kcat[...].T
        vcat_t[...] = vcat[...].T


def attention(
    chunk, owner, tokens, place, q, g, leaf_kv, leaf, mask, own, far, earlier, planes, ranks
):
    count = q.shape[0]
    slots = planes * ranks
    block_len = own.shape[0] // slots
    prompts = tokens.shape[0]
    per_prefix = owner.shape[0] // prompts
    span = per_prefix * block_len
    keys = span + count
    width = own.shape[1]
    groups = width // (2 * HEAD_SIZE)
    heads = groups * GQ
    steps = heads // PAIR
    per_group = GQ // PAIR
    bf16, f32 = jnp.bfloat16, jnp.float32

    def now(i):
        return jnp.minimum(i, steps - 1)

    ahead = pl.BlockSpec((count, PAIR * HEAD_SIZE), lambda i, *_: (0, chunk * steps + now(i)))
    behind = pl.BlockSpec(
        (count, PAIR * HEAD_SIZE), lambda i, *_: (0, chunk * steps + jnp.maximum(i - 1, 0))
    )
    leaf_k = pl.BlockSpec(
        (count, HEAD_SIZE), lambda i, *_: (0, chunk * groups + now(i) // per_group)
    )
    leaf_v = pl.BlockSpec(
        (count, HEAD_SIZE),
        lambda i, *_: (0, KEY_VALUE_HEADS + chunk * groups + now(i) // per_group),
    )
    anywhere = pl.BlockSpec(memory_space=pl.ANY)

    def full(shape):
        return pl.BlockSpec(shape, lambda h, *_: (0,) * len(shape))

    sum_shape = (slots, block_len, width)
    chained = len(earlier) > 0
    return pl.pallas_call(
        functools.partial(
            attention_kernel, prompts=prompts, per_prefix=per_prefix, block_len=block_len,
            planes=planes, ranks=ranks, chained=chained, steps=steps,
        ),
        grid_spec=pltpu.PrefetchScalarGridSpec(
            num_scalar_prefetch=3,
            grid=(steps + 1,),
            in_specs=[
                ahead, ahead, leaf_k, leaf_v, full(leaf.shape), full(mask.shape), anywhere, anywhere,
            ] + [anywhere] * len(earlier),
            out_specs=[behind, behind, full((count, width)), full(sum_shape), full(sum_shape)],
            scratch_shapes=[
                pltpu.VMEM((2 * span, width), bf16),
                pltpu.VMEM((keys, 2 * HEAD_SIZE), bf16),
                pltpu.VMEM((keys, 2 * HEAD_SIZE), bf16),
                pltpu.VMEM((2 * HEAD_SIZE, keys), bf16),
                pltpu.VMEM((2 * HEAD_SIZE, keys), bf16),
                pltpu.VMEM((count, PAIR * count), f32),
                pltpu.VMEM((count, 2 * HEAD_SIZE), bf16),
                pltpu.VMEM((count, 2 * HEAD_SIZE), bf16),
                pltpu.VMEM((PAIR * count, 2 * HEAD_SIZE), bf16),
                pltpu.VMEM((PAIR * count, 2 * HEAD_SIZE), bf16),
                pltpu.VMEM((keys, PAIR * count), f32),
                pltpu.VMEM((keys, PAIR * count), f32),
                pltpu.VMEM((keys, PAIR * count), bf16),
                pltpu.VMEM((keys, PAIR * count), bf16),
                pltpu.VMEM((keys, 2 * HEAD_SIZE), f32),
                pltpu.VMEM((keys, 2 * HEAD_SIZE), f32),
                pltpu.SemaphoreType.DMA((2 * per_prefix,)),
            ],
        ),
        out_shape=[
            jax.ShapeDtypeStruct(q.shape, bf16),
            jax.ShapeDtypeStruct(q.shape, bf16),
            jax.ShapeDtypeStruct((count, width), bf16),
            jax.ShapeDtypeStruct(sum_shape, bf16),
            jax.ShapeDtypeStruct(sum_shape, bf16),
        ],
        input_output_aliases={11: 0, 12: 1} if chained else {},
        compiler_params=pltpu.CompilerParams(
            vmem_limit_bytes=60 * 2**20, dimension_semantics=("arbitrary",)
        ),
        cost_estimate=pl.CostEstimate(
            flops=heads * 6 * 2 * keys * 256 * 256, bytes_accessed=16 * 2**20 // CHUNKS,
            transcendentals=heads * keys * count,
        ),
    )(owner, tokens, place, q, g, leaf_kv, leaf_kv, leaf, mask, own, far, *earlier)


def shards(
    query, leaf_key_value, prefix_key_value, d_out, block_owner, subtree_tokens, leaf_id, loss_mask
):
    devices = lax.axis_size("dp")
    ranks = 2 if devices == 16 else 1
    planes = devices // (2 * ranks)
    place = lax.axis_index("dp").astype(jnp.int32).reshape(1)
    mask = loss_mask.reshape(1, -1)
    f32 = jnp.float32

    def index(plane, rank, core):
        return (plane % planes * ranks + rank % ranks) * 2 + core % 2

    def send(array, plane_step, rank_step, core_step):
        pairs = [
            (index(p, r, c), index(p + plane_step, r + rank_step, c + core_step))
            for p in range(planes) for r in range(ranks) for c in range(2)
        ]
        return lax.ppermute(array, "dp", pairs)

    groups = KEY_VALUE_HEADS // CHUNKS
    step = groups * HEAD_SIZE
    middle = KEY_VALUE_HEADS * HEAD_SIZE

    def tie(value, *others):
        return lax.optimization_barrier((value, *others))[0]

    def by_planes(chunk):
        mine = jnp.concatenate(
            [prefix_key_value[:, chunk * step:(chunk + 1) * step],
             prefix_key_value[:, middle + chunk * step:middle + (chunk + 1) * step]], axis=1
        ) if CHUNKS > 1 else prefix_key_value
        near = [mine] + [send(mine, k, 0, 0) for k in range(1, planes)]
        return jnp.concatenate(near, axis=0)

    def by_ranks(near):
        return jnp.concatenate([near, send(near, 0, 1, 0)], axis=0) if ranks == 2 else near

    def reduce_cores(own, far):
        return own.astype(f32) + send(far, 0, 0, 1).astype(f32)

    def reduce_planes(total, away):
        if ranks == 2:
            total = total[:planes] + send(away, 0, 1, 0).astype(f32)
        mine = total[0]
        for k in range(1, planes):
            mine = mine + send(total[k].astype(jnp.bfloat16), k, 0, 0).astype(f32)
        return mine.astype(jnp.bfloat16)

    near = [by_planes(chunk) for chunk in range(CHUNKS)]
    own = [by_ranks(n) for n in near]
    d_leaf, d_prefix, earlier, done = [], [], (), []
    for chunk in range(CHUNKS):
        mine = tie(own[chunk], d_leaf[-1] if chunk else near[-1])
        far = send(mine, 0, 0, 1)
        attended, d_query, leaf_part, own_sum, far_sum = attention(
            chunk, block_owner, subtree_tokens, tie(place, *done), query, d_out, leaf_key_value,
            leaf_id, mask, mine, far, earlier, planes, ranks,
        )
        earlier = (attended, d_query)
        d_leaf.append(leaf_part)
        total = reduce_cores(own_sum, far_sum)
        away = total[planes:].astype(jnp.bfloat16)
        done = [away]
        d_prefix.append(reduce_planes(total, away))

    def join(parts):
        if CHUNKS == 1:
            return parts[0]
        return jnp.concatenate([p[:, :step] for p in parts] + [p[:, step:] for p in parts], axis=1)

    return attended, d_query, join(d_leaf), join(d_prefix)


def solution(mesh):
    rows = P(("groups", "dp"), None)
    in_specs = (rows, rows, rows, rows, P("groups"), P("groups"), rows, P(("groups", "dp")))
    return jax.shard_map(
        shards, mesh=mesh, in_specs=in_specs, out_specs=(rows,) * 4, check_vma=False
    )
```

```python
import functools

import jax
import jax.numpy as jnp
from jax import lax
from jax.experimental import pallas as pl
from jax.experimental.pallas import tpu as pltpu
from jax.sharding import PartitionSpec as P

HEAD_SIZE = 128
KEY_VALUE_HEADS = 4
GQ = 8
SCALE = HEAD_SIZE ** (-0.5)
LOG2E = 1.4426950408889634


def dot(a, b, contract):
    return lax.dot_general(a, b, (contract, ((), ())), preferred_element_type=jnp.float32)

CHUNKS = (1, 2, 1)
PAIR = 2
PIECE = 32


def attention_kernel(
    owner_ref, tokens_ref, place_ref,
    q_ref, g_ref, leaf_k_ref, leaf_v_ref, leaf_ref, mask_ref, *rest,
    prompts, per_prefix, block_len, planes, ranks, chained, steps,
):
    sources = rest[:2 * ranks]
    (out_ref, dq_ref, dleaf_ref, own_sum_ref, far_sum_ref,
     kv, kcat, vcat, kcat_t, vcat_t, bias, q_pick, g_pick, q2, g2, scores, dprob, probs_b, dscore,
     dk_sum, dv_sum, sems) = rest[2 * ranks + 2 * chained:]
    step = pl.program_id(0)
    per_group = GQ // PAIR
    count = q_ref.shape[0]
    columns = PAIR * count
    span = per_prefix * block_len
    keys = span + count
    half = sources[0].shape[1] // 2

    place = place_ref[0]
    first = place * count
    last = first + (count - 1)
    end = jnp.int32(0)
    pair_first = jnp.int32(0)
    pair_last = jnp.int32(0)
    border = jnp.int32(2**30)
    for p in range(prompts):
        end = end + tokens_ref[p]
        pair_first = pair_first + (end <= first).astype(jnp.int32)
        pair_last = pair_last + (end <= last).astype(jnp.int32)
        border = jnp.where(end > first, jnp.minimum(border, end), border)
    border = border - first

    def block_place(side, j):
        prefix = pair_first if side == 0 else pair_last
        owner = owner_ref[prefix * per_prefix + j]
        same_core = lax.rem(owner, 2) == lax.rem(place, 2)
        row = lax.rem(owner // 2 + place // 2, ranks)
        ahead = lax.rem(owner // (2 * ranks) + planes - place // (2 * ranks), planes)
        return same_core, row, ahead

    def key_columns(group):
        return pl.ds(pl.multiple_of(group * HEAD_SIZE, HEAD_SIZE), HEAD_SIZE)

    def value_columns(group):
        return pl.ds(pl.multiple_of(half + group * HEAD_SIZE, HEAD_SIZE), HEAD_SIZE)

    @pl.when(step == 0)
    def _():
        for side in range(2):
            for j in range(per_prefix):
                n = side * per_prefix + j
                same_core, row, ahead = block_place(side, j)
                slot = lax.rem(planes - ahead, planes)
                rows = pl.ds(pl.multiple_of(slot * block_len, block_len), block_len)
                target = kv.at[pl.ds(n * block_len, block_len), :]
                for at, source in enumerate(sources):
                    @pl.when((same_core == (at % 2 == 0)) & (row == at // 2))
                    def _():
                        pltpu.make_async_copy(source.at[rows, :], target, sems.at[n]).start()

        leaf_row = jnp.broadcast_to(leaf_ref[...], (count, count))
        leaf_col = leaf_row.T
        key_at = lax.broadcasted_iota(jnp.int32, (count, count), 0)
        token_at = lax.broadcasted_iota(jnp.int32, (count, count), 1)
        same = (leaf_row == leaf_col) & (key_at <= token_at)
        same = same & ((key_at < border) == (token_at < border))
        allowed_bias = jnp.where(same, 0.0, -1e30).astype(jnp.float32)
        mask_col = jnp.broadcast_to(mask_ref[...], (count, count)).T.astype(jnp.float32)
        in_first = key_at < border
        left = token_at < HEAD_SIZE
        pick = (in_first == left).astype(jnp.float32)
        q_pick[...] = pick.astype(jnp.bfloat16)
        g_pick[...] = (pick * mask_col).astype(jnp.bfloat16)
        for n in range(PAIR):
            bias[:, n * count:(n + 1) * count] = allowed_bias
        own_sum_ref[...] = jnp.zeros_like(own_sum_ref)
        far_sum_ref[...] = jnp.zeros_like(far_sum_ref)
        dk_sum[...] = jnp.zeros_like(dk_sum)
        dv_sum[...] = jnp.zeros_like(dv_sum)
        for n in range(2 * per_prefix):
            target = kv.at[pl.ds(n * block_len, block_len), :]
            pltpu.make_async_copy(
                sources[0].at[pl.ds(0, block_len), :], target, sems.at[n]
            ).wait()

    new_group = lax.rem(step, per_group) == 0

    @pl.when(new_group & (step < steps))
    def _():
        group = step // per_group
        for cat, cols, leaf in (
            (kcat, key_columns(group), leaf_k_ref), (vcat, value_columns(group), leaf_v_ref)
        ):
            for side in range(2):
                lanes = slice(side * HEAD_SIZE, (side + 1) * HEAD_SIZE)
                cat[0:span, lanes] = kv[side * span:(side + 1) * span, cols]
                cat[span:, lanes] = leaf[...]

    def later_products():
        token_at = lax.rem(lax.broadcasted_iota(jnp.int32, (HEAD_SIZE, columns), 1), count)
        first_side = token_at < border
        for source, cat_t, factor, target in (
            (probs_b, vcat_t, 1.0, out_ref), (dscore, kcat_t, SCALE, dq_ref)
        ):
            both = dot(cat_t[...], source[...], ((1,), (0,)))
            mine = jnp.where(first_side, both[:HEAD_SIZE], both[HEAD_SIZE:])
            if factor != 1.0:
                mine = mine * factor
            for n in range(PAIR):
                lanes = slice(n * HEAD_SIZE, (n + 1) * HEAD_SIZE)
                target[:, lanes] = mine[:, n * count:(n + 1) * count].T.astype(jnp.bfloat16)
        dk_sum[...] += dot(dscore[...], q2[...], ((1,), (0,)))
        dv_sum[...] += dot(probs_b[...], g2[...], ((1,), (0,)))

    def first_products():
        new_q, new_g = [], []
        for n in range(PAIR):
            q = q_ref[:, n * HEAD_SIZE:(n + 1) * HEAD_SIZE]
            g = g_ref[:, n * HEAD_SIZE:(n + 1) * HEAD_SIZE]
            new_q.append(jnp.concatenate([q, q], axis=1) * q_pick[...])
            new_g.append(jnp.concatenate([g, g], axis=1) * g_pick[...])
        new_q = jnp.concatenate(new_q, axis=0)
        new_g = jnp.concatenate(new_g, axis=0)
        product = dot(kcat[...], new_q, ((1,), (1,)))
        top = None
        for at in range(0, keys, PIECE):
            piece = product[at:at + PIECE]
            if at >= span:
                piece = piece + bias[at - span:at - span + PIECE, :]
            scores[at:at + PIECE, :] = piece
            piece = fold(piece, jnp.maximum)
            top = piece if top is None else jnp.maximum(top, piece)
        dprob[...] = dot(vcat[...], new_g, ((1,), (1,)))
        return new_q, new_g, top

    def fold(value, op):
        value = value.reshape(PIECE // 8, 8, columns)
        total = value[0]
        for n in range(1, PIECE // 8):
            total = op(total, value[n])
        return total

    def softmax(new_q, new_g, top):
        top = jnp.max(top, axis=0, keepdims=True)
        total = jnp.zeros((8, columns), jnp.float32)
        delta = jnp.zeros((8, columns), jnp.float32)
        for at in range(0, keys, PIECE):
            weight = jnp.exp2((scores[at:at + PIECE, :] - top) * (SCALE * LOG2E))
            scores[at:at + PIECE, :] = weight
            total = total + fold(weight, jnp.add)
            delta = delta + fold(weight * dprob[at:at + PIECE, :], jnp.add)
        inverse = 1.0 / jnp.sum(total, axis=0, keepdims=True)
        delta = jnp.sum(delta, axis=0, keepdims=True) * inverse
        for at in range(0, keys, PIECE):
            probs = scores[at:at + PIECE, :] * inverse
            probs_b[at:at + PIECE, :] = probs.astype(jnp.bfloat16)
            dscore[at:at + PIECE, :] = (probs * (dprob[at:at + PIECE, :] - delta)).astype(jnp.bfloat16)
        q2[...] = new_q
        g2[...] = new_g

    @pl.when(step == 0)
    def _():
        softmax(*first_products())

    @pl.when((step > 0) & (step < steps))
    def _():
        new = first_products()
        later_products()
        softmax(*new)

    @pl.when(step == steps)
    def _():
        later_products()

    @pl.when(new_group & (step > 0))
    def _():
        group = step // per_group - 1
        for total_ref, cols, factor in (
            (dk_sum, key_columns(group), SCALE), (dv_sum, value_columns(group), 1.0)
        ):
            leaf = (total_ref[span:, :HEAD_SIZE] + total_ref[span:, HEAD_SIZE:]) * factor
            dleaf_ref[:, cols] = leaf.astype(jnp.bfloat16)
            for side in range(2):
                lanes = slice(side * HEAD_SIZE, (side + 1) * HEAD_SIZE)
                for j in range(per_prefix):
                    value = total_ref[j * block_len:(j + 1) * block_len, lanes] * factor
                    value = value.astype(jnp.bfloat16)
                    same_core, row, ahead = block_place(side, j)
                    slot = row * planes + ahead

                    @pl.when(same_core)
                    def _():
                        own_sum_ref[slot, :, cols] += value

                    @pl.when(jnp.logical_not(same_core))
                    def _():
                        far_sum_ref[slot, :, cols] += value
        dk_sum[...] = jnp.zeros_like(dk_sum)
        dv_sum[...] = jnp.zeros_like(dv_sum)

    @pl.when(new_group & (step < steps))
    def _():
        kcat_t[...] = kcat[...].T
        vcat_t[...] = vcat[...].T


def attention(
    chunk, owner, tokens, place, q, g, leaf_kv, leaf, mask, sources, earlier, planes, ranks
):
    count = q.shape[0]
    slots = planes * ranks
    block_len = sources[0].shape[0] // planes
    prompts = tokens.shape[0]
    per_prefix = owner.shape[0] // prompts
    span = per_prefix * block_len
    keys = span + count
    width = sources[0].shape[1]
    groups = CHUNKS[chunk]
    skipped = sum(CHUNKS[:chunk])
    heads = groups * GQ
    steps = heads // PAIR
    per_group = GQ // PAIR
    skipped_steps = skipped * per_group
    bf16, f32 = jnp.bfloat16, jnp.float32

    def now(i):
        return jnp.minimum(i, steps - 1)

    ahead = pl.BlockSpec((count, PAIR * HEAD_SIZE), lambda i, *_: (0, skipped_steps + now(i)))
    behind = pl.BlockSpec(
        (count, PAIR * HEAD_SIZE), lambda i, *_: (0, skipped_steps + jnp.maximum(i - 1, 0))
    )
    leaf_k = pl.BlockSpec(
        (count, HEAD_SIZE), lambda i, *_: (0, skipped + now(i) // per_group)
    )
    leaf_v = pl.BlockSpec(
        (count, HEAD_SIZE),
        lambda i, *_: (0, KEY_VALUE_HEADS + skipped + now(i) // per_group),
    )
    anywhere = pl.BlockSpec(memory_space=pl.ANY)

    def full(shape):
        return pl.BlockSpec(shape, lambda h, *_: (0,) * len(shape))

    sum_shape = (slots, block_len, width)
    chained = len(earlier) > 0
    return pl.pallas_call(
        functools.partial(
            attention_kernel, prompts=prompts, per_prefix=per_prefix, block_len=block_len,
            planes=planes, ranks=ranks, chained=chained, steps=steps,
        ),
        grid_spec=pltpu.PrefetchScalarGridSpec(
            num_scalar_prefetch=3,
            grid=(steps + 1,),
            in_specs=[
                ahead, ahead, leaf_k, leaf_v, full(leaf.shape), full(mask.shape),
            ] + [anywhere] * (2 * ranks + len(earlier)),
            out_specs=[behind, behind, full((count, width)), full(sum_shape), full(sum_shape)],
            scratch_shapes=[
                pltpu.VMEM((2 * span, width), bf16),
                pltpu.VMEM((keys, 2 * HEAD_SIZE), bf16),
                pltpu.VMEM((keys, 2 * HEAD_SIZE), bf16),
                pltpu.VMEM((2 * HEAD_SIZE, keys), bf16),
                pltpu.VMEM((2 * HEAD_SIZE, keys), bf16),
                pltpu.VMEM((count, PAIR * count), f32),
                pltpu.VMEM((count, 2 * HEAD_SIZE), bf16),
                pltpu.VMEM((count, 2 * HEAD_SIZE), bf16),
                pltpu.VMEM((PAIR * count, 2 * HEAD_SIZE), bf16),
                pltpu.VMEM((PAIR * count, 2 * HEAD_SIZE), bf16),
                pltpu.VMEM((keys, PAIR * count), f32),
                pltpu.VMEM((keys, PAIR * count), f32),
                pltpu.VMEM((keys, PAIR * count), bf16),
                pltpu.VMEM((keys, PAIR * count), bf16),
                pltpu.VMEM((keys, 2 * HEAD_SIZE), f32),
                pltpu.VMEM((keys, 2 * HEAD_SIZE), f32),
                pltpu.SemaphoreType.DMA((2 * per_prefix,)),
            ],
        ),
        out_shape=[
            jax.ShapeDtypeStruct(q.shape, bf16),
            jax.ShapeDtypeStruct(q.shape, bf16),
            jax.ShapeDtypeStruct((count, width), bf16),
            jax.ShapeDtypeStruct(sum_shape, bf16),
            jax.ShapeDtypeStruct(sum_shape, bf16),
        ],
        input_output_aliases={9 + 2 * ranks: 0, 10 + 2 * ranks: 1} if chained else {},
        compiler_params=pltpu.CompilerParams(
            vmem_limit_bytes=32 * 2**20, dimension_semantics=("arbitrary",)
        ),
        cost_estimate=pl.CostEstimate(
            flops=heads * 6 * 2 * keys * 256 * 256, bytes_accessed=groups * 4 * 2**20,
            transcendentals=heads * keys * count,
        ),
    )(owner, tokens, place, q, g, leaf_kv, leaf_kv, leaf, mask, *sources, *earlier)


def shards(
    query, leaf_key_value, prefix_key_value, d_out, block_owner, subtree_tokens, leaf_id, loss_mask
):
    devices = lax.axis_size("dp")
    ranks = 2 if devices == 16 else 1
    planes = devices // (2 * ranks)
    place = lax.axis_index("dp").astype(jnp.int32).reshape(1)
    mask = loss_mask.reshape(1, -1)
    f32 = jnp.float32

    def index(plane, rank, core):
        return (plane % planes * ranks + rank % ranks) * 2 + core % 2

    def send(array, plane_step, rank_step, core_step):
        pairs = [
            (index(p, r, c), index(p + plane_step, r + rank_step, c + core_step))
            for p in range(planes) for r in range(ranks) for c in range(2)
        ]
        return lax.ppermute(array, "dp", pairs)

    middle = KEY_VALUE_HEADS * HEAD_SIZE

    def tie(value, *others):
        return lax.optimization_barrier((value, *others))[0]

    def by_planes(chunk):
        low = sum(CHUNKS[:chunk]) * HEAD_SIZE
        high = low + CHUNKS[chunk] * HEAD_SIZE
        mine = jnp.concatenate(
            [prefix_key_value[:, low:high], prefix_key_value[:, middle + low:middle + high]], axis=1
        )
        return jnp.concatenate([mine] + [send(mine, k, 0, 0) for k in range(1, planes)], axis=0)

    def reduce_cores(own, far):
        return own.astype(f32) + send(far, 0, 0, 1).astype(f32)

    def reduce_ranks(total, away):
        return total[:planes] + send(away, 0, 1, 0).astype(f32) if ranks == 2 else total

    def reduce_planes(total, away):
        mine = total[0]
        for k in range(1, planes):
            mine = mine + send(away[k - 1], k, 0, 0).astype(f32)
        return mine.astype(jnp.bfloat16)

    chunks = len(CHUNKS)
    near = [by_planes(chunk) for chunk in range(chunks)]
    other = [send(n, 0, 1, 0) for n in near] if ranks == 2 else []
    d_leaf, d_prefix, earlier = [], [], ()
    by_cores, by_ranks = [], []
    for chunk in range(chunks):
        first = [place] + near[chunk + 1:chunk + 2]
        if chunk >= 1:
            first.append(by_cores[chunk - 1][1])
        if chunk >= 2:
            total, away = by_cores[chunk - 2]
            total = reduce_ranks(total, away)
            away = [total[k].astype(jnp.bfloat16) for k in range(1, planes)]
            by_ranks.append((total, away))
            first.extend(away)
        sources = [near[chunk], send(near[chunk], 0, 0, 1)]
        if ranks == 2:
            row = tie(other[chunk], d_leaf[-1] if chunk else near[1])
            sources += [row, send(row, 0, 0, 1)]
        attended, d_query, leaf_part, own_sum, far_sum = attention(
            chunk, block_owner, subtree_tokens, tie(*first), query, d_out, leaf_key_value,
            leaf_id, mask, sources, earlier, planes, ranks,
        )
        earlier = (attended, d_query)
        d_leaf.append(leaf_part)
        total = reduce_cores(own_sum, far_sum)
        by_cores.append((total, total[planes:].astype(jnp.bfloat16)))
    for chunk in range(chunks):
        if chunk >= len(by_ranks):
            total = reduce_ranks(*by_cores[chunk])
            by_ranks.append((total, [total[k].astype(jnp.bfloat16) for k in range(1, planes)]))
        d_prefix.append(reduce_planes(*by_ranks[chunk]))

    def join(parts):
        halves = [jnp.split(p, 2, axis=1) for p in parts]
        return jnp.concatenate([h[0] for h in halves] + [h[1] for h in halves], axis=1)

    return attended, d_query, join(d_leaf), join(d_prefix)


def solution(mesh):
    rows = P(("groups", "dp"), None)
    in_specs = (rows, rows, rows, rows, P("groups"), P("groups"), rows, P(("groups", "dp")))
    return jax.shard_map(
        shards, mesh=mesh, in_specs=in_specs, out_specs=(rows,) * 4, check_vma=False
    )
```

```python
import functools

import jax
import jax.numpy as jnp
from jax import lax
from jax.experimental import pallas as pl
from jax.experimental.pallas import tpu as pltpu
from jax.sharding import PartitionSpec as P

HEAD_SIZE = 128
KEY_VALUE_HEADS = 4
GQ = 8
SCALE = HEAD_SIZE ** (-0.5)
LOG2E = 1.4426950408889634


def dot(a, b, contract):
    return lax.dot_general(a, b, (contract, ((), ())), preferred_element_type=jnp.float32)

CHUNKS = (2, 2)
STEP_HEADS = (4, 2)
PIECE = 32


def attention_kernel(
    owner_ref, tokens_ref, place_ref,
    q_ref, g_ref, leaf_k_ref, leaf_v_ref, leaf_ref, mask_ref, *rest,
    prompts, per_prefix, block_len, planes, ranks, chained, steps, step_heads,
):
    sources = rest[:2 * ranks]
    rest = rest[2 * ranks + 2 * chained:]
    out_ref, dq_ref, dleaf_ref = rest[:3]
    totals = rest[3:3 + 2 * ranks]
    (kv, kcat, vcat, kcat_t, vcat_t, bias, q_pick, g_pick, q2, g2, scores, dprob, probs_b, dscore,
     dk_sum, dv_sum, sems) = rest[3 + 2 * ranks:]
    step = pl.program_id(0)
    per_group = GQ // step_heads
    count = q_ref.shape[0]
    columns = step_heads * count
    span = per_prefix * block_len
    keys = span + count
    half = sources[0].shape[1] // 2

    place = place_ref[0]
    first = place * count
    last = first + (count - 1)
    end = jnp.int32(0)
    pair_first = jnp.int32(0)
    pair_last = jnp.int32(0)
    border = jnp.int32(2**30)
    for p in range(prompts):
        end = end + tokens_ref[p]
        pair_first = pair_first + (end <= first).astype(jnp.int32)
        pair_last = pair_last + (end <= last).astype(jnp.int32)
        border = jnp.where(end > first, jnp.minimum(border, end), border)
    border = border - first

    def block_place(side, j):
        prefix = pair_first if side == 0 else pair_last
        owner = owner_ref[prefix * per_prefix + j]
        same_core = lax.rem(owner, 2) == lax.rem(place, 2)
        row = lax.rem(owner // 2 + place // 2, ranks)
        ahead = lax.rem(owner // (2 * ranks) + planes - place // (2 * ranks), planes)
        return same_core, row, ahead

    def key_columns(group):
        return pl.ds(pl.multiple_of(group * HEAD_SIZE, HEAD_SIZE), HEAD_SIZE)

    def value_columns(group):
        return pl.ds(pl.multiple_of(half + group * HEAD_SIZE, HEAD_SIZE), HEAD_SIZE)

    @pl.when(step == 0)
    def _():
        for side in range(2):
            for j in range(per_prefix):
                n = side * per_prefix + j
                same_core, row, ahead = block_place(side, j)
                slot = lax.rem(planes - ahead, planes)
                rows = pl.ds(pl.multiple_of(slot * block_len, block_len), block_len)
                target = kv.at[pl.ds(n * block_len, block_len), :]
                for at, source in enumerate(sources):
                    @pl.when((same_core == (at % 2 == 0)) & (row == at // 2))
                    def _():
                        pltpu.make_async_copy(source.at[rows, :], target, sems.at[n]).start()

        leaf_row = jnp.broadcast_to(leaf_ref[...], (count, count))
        leaf_col = leaf_row.T
        key_at = lax.broadcasted_iota(jnp.int32, (count, count), 0)
        token_at = lax.broadcasted_iota(jnp.int32, (count, count), 1)
        same = (leaf_row == leaf_col) & (key_at <= token_at)
        same = same & ((key_at < border) == (token_at < border))
        allowed_bias = jnp.where(same, 0.0, -1e30).astype(jnp.float32)
        mask_col = jnp.broadcast_to(mask_ref[...], (count, count)).T.astype(jnp.float32)
        in_first = key_at < border
        left = token_at < HEAD_SIZE
        pick = (in_first == left).astype(jnp.float32)
        q_pick[...] = pick.astype(jnp.bfloat16)
        g_pick[...] = (pick * mask_col).astype(jnp.bfloat16)
        for n in range(step_heads):
            bias[:, n * count:(n + 1) * count] = allowed_bias
        for ref in totals:
            ref[...] = jnp.zeros_like(ref)
        dk_sum[...] = jnp.zeros_like(dk_sum)
        dv_sum[...] = jnp.zeros_like(dv_sum)
        for n in range(2 * per_prefix):
            target = kv.at[pl.ds(n * block_len, block_len), :]
            pltpu.make_async_copy(
                sources[0].at[pl.ds(0, block_len), :], target, sems.at[n]
            ).wait()

    new_group = lax.rem(step, per_group) == 0

    @pl.when(new_group & (step < steps))
    def _():
        group = step // per_group
        for cat, cols, leaf in (
            (kcat, key_columns(group), leaf_k_ref), (vcat, value_columns(group), leaf_v_ref)
        ):
            for side in range(2):
                lanes = slice(side * HEAD_SIZE, (side + 1) * HEAD_SIZE)
                cat[0:span, lanes] = kv[side * span:(side + 1) * span, cols]
                cat[span:, lanes] = leaf[...]


    def later_rows():
        dk_sum[...] += dot(dscore[...], q2[...], ((1,), (0,)))
        dv_sum[...] += dot(probs_b[...], g2[...], ((1,), (0,)))

    def later_columns():
        token_at = lax.rem(lax.broadcasted_iota(jnp.int32, (HEAD_SIZE, columns), 1), count)
        first_side = token_at < border
        for source, cat_t, factor, target in (
            (probs_b, vcat_t, 1.0, out_ref), (dscore, kcat_t, SCALE, dq_ref)
        ):
            both = dot(cat_t[...], source[...], ((1,), (0,)))
            mine = jnp.where(first_side, both[:HEAD_SIZE], both[HEAD_SIZE:])
            if factor != 1.0:
                mine = mine * factor
            for n in range(step_heads):
                lanes = slice(n * HEAD_SIZE, (n + 1) * HEAD_SIZE)
                target[:, lanes] = mine[:, n * count:(n + 1) * count].T.astype(jnp.bfloat16)


    def pick(source, chosen):
        parts = []
        for n in range(step_heads):
            part = source[:, n * HEAD_SIZE:(n + 1) * HEAD_SIZE]
            parts.append(jnp.concatenate([part, part], axis=1) * chosen[...])
        return jnp.concatenate(parts, axis=0)

    def fold(value, op):
        value = value.reshape(PIECE // 8, 8, columns)
        total = value[0]
        for n in range(1, PIECE // 8):
            total = op(total, value[n])
        return total

    def score(new_q):
        product = dot(kcat[...], new_q, ((1,), (1,)))
        top = None
        for at in range(0, keys, PIECE):
            piece = product[at:at + PIECE]
            if at >= span:
                piece = piece + bias[at - span:at - span + PIECE, :]
            scores[at:at + PIECE, :] = piece
            piece = fold(piece, jnp.maximum)
            top = piece if top is None else jnp.maximum(top, piece)
        return jnp.max(top, axis=0, keepdims=True)

    def sums(top):
        total = jnp.zeros((8, columns), jnp.float32)
        delta = jnp.zeros((8, columns), jnp.float32)
        for at in range(0, keys, PIECE):
            weight = jnp.exp2((scores[at:at + PIECE, :] - top) * (SCALE * LOG2E))
            total = total + fold(weight, jnp.add)
            delta = delta + fold(weight * dprob[at:at + PIECE, :], jnp.add)
        total = jnp.sum(total, axis=0, keepdims=True)
        return total, jnp.sum(delta, axis=0, keepdims=True) / total

    def finish(top, total, delta):
        shift = jnp.log2(total)
        for at in range(0, keys, PIECE):
            power = (scores[at:at + PIECE, :] - top) * (SCALE * LOG2E)
            probs = jnp.exp2(power - shift)
            probs_b[at:at + PIECE, :] = probs.astype(jnp.bfloat16)
            dscore[at:at + PIECE, :] = (probs * (dprob[at:at + PIECE, :] - delta)).astype(jnp.bfloat16)

    def work(later):
        new_q = pick(q_ref, q_pick)
        new_g = pick(g_ref, g_pick)
        top = score(new_q)
        if later:
            later_rows()
        dprob[...] = dot(vcat[...], new_g, ((1,), (1,)))
        total, delta = sums(top)
        if later:
            later_columns()
        finish(top, total, delta)
        q2[...] = new_q
        g2[...] = new_g

    @pl.when(step == 0)
    def _():
        work(False)

    @pl.when((step > 0) & (step < steps))
    def _():
        work(True)

    @pl.when(step == steps)
    def _():
        later_rows()
        later_columns()

    @pl.when(new_group & (step > 0))
    def _():
        group = step // per_group - 1
        for total_ref, cols, factor in (
            (dk_sum, key_columns(group), SCALE), (dv_sum, value_columns(group), 1.0)
        ):
            leaf = (total_ref[span:, :HEAD_SIZE] + total_ref[span:, HEAD_SIZE:]) * factor
            dleaf_ref[:, cols] = leaf.astype(jnp.bfloat16)
            for side in range(2):
                lanes = slice(side * HEAD_SIZE, (side + 1) * HEAD_SIZE)
                for j in range(per_prefix):
                    value = total_ref[j * block_len:(j + 1) * block_len, lanes] * factor
                    value = value.astype(jnp.bfloat16)
                    same_core, row, ahead = block_place(side, j)
                    for at, ref in enumerate(totals):
                        @pl.when((same_core == (at % 2 == 0)) & (row == at // 2))
                        def _():
                            ref[ahead, :, cols] += value

        dk_sum[...] = jnp.zeros_like(dk_sum)
        dv_sum[...] = jnp.zeros_like(dv_sum)

    @pl.when(new_group & (step < steps))
    def _():
        kcat_t[...] = kcat[...].T
        vcat_t[...] = vcat[...].T


def attention(
    chunk, owner, tokens, place, q, g, leaf_kv, leaf, mask, sources, earlier, planes, ranks
):
    count = q.shape[0]
    block_len = sources[0].shape[0] // planes
    prompts = tokens.shape[0]
    per_prefix = owner.shape[0] // prompts
    span = per_prefix * block_len
    keys = span + count
    width = sources[0].shape[1]
    groups = CHUNKS[chunk]
    step_heads = STEP_HEADS[chunk]
    skipped = sum(CHUNKS[:chunk])
    heads = groups * GQ
    steps = heads // step_heads
    per_group = GQ // step_heads
    skipped_steps = skipped * per_group
    bf16, f32 = jnp.bfloat16, jnp.float32

    def now(i):
        return jnp.minimum(i, steps - 1)

    ahead = pl.BlockSpec((count, step_heads * HEAD_SIZE), lambda i, *_: (0, skipped_steps + now(i)))
    behind = pl.BlockSpec(
        (count, step_heads * HEAD_SIZE), lambda i, *_: (0, skipped_steps + jnp.maximum(i - 1, 0))
    )
    leaf_k = pl.BlockSpec(
        (count, HEAD_SIZE), lambda i, *_: (0, skipped + now(i) // per_group)
    )
    leaf_v = pl.BlockSpec(
        (count, HEAD_SIZE),
        lambda i, *_: (0, KEY_VALUE_HEADS + skipped + now(i) // per_group),
    )
    anywhere = pl.BlockSpec(memory_space=pl.ANY)

    def full(shape):
        return pl.BlockSpec(shape, lambda h, *_: (0,) * len(shape))

    sum_shape = (planes, block_len, width)
    chained = len(earlier) > 0
    return pl.pallas_call(
        functools.partial(
            attention_kernel, prompts=prompts, per_prefix=per_prefix, block_len=block_len,
            planes=planes, ranks=ranks, chained=chained, steps=steps, step_heads=step_heads,
        ),
        grid_spec=pltpu.PrefetchScalarGridSpec(
            num_scalar_prefetch=3,
            grid=(steps + 1,),
            in_specs=[
                ahead, ahead, leaf_k, leaf_v, full(leaf.shape), full(mask.shape),
            ] + [anywhere] * (2 * ranks + len(earlier)),
            out_specs=[behind, behind, full((count, width))] + [full(sum_shape)] * (2 * ranks),
            scratch_shapes=[
                pltpu.VMEM((2 * span, width), bf16),
                pltpu.VMEM((keys, 2 * HEAD_SIZE), bf16),
                pltpu.VMEM((keys, 2 * HEAD_SIZE), bf16),
                pltpu.VMEM((2 * HEAD_SIZE, keys), bf16),
                pltpu.VMEM((2 * HEAD_SIZE, keys), bf16),
                pltpu.VMEM((count, step_heads * count), f32),
                pltpu.VMEM((count, 2 * HEAD_SIZE), bf16),
                pltpu.VMEM((count, 2 * HEAD_SIZE), bf16),
                pltpu.VMEM((step_heads * count, 2 * HEAD_SIZE), bf16),
                pltpu.VMEM((step_heads * count, 2 * HEAD_SIZE), bf16),
                pltpu.VMEM((keys, step_heads * count), f32),
                pltpu.VMEM((keys, step_heads * count), f32),
                pltpu.VMEM((keys, step_heads * count), bf16),
                pltpu.VMEM((keys, step_heads * count), bf16),
                pltpu.VMEM((keys, 2 * HEAD_SIZE), f32),
                pltpu.VMEM((keys, 2 * HEAD_SIZE), f32),
                pltpu.SemaphoreType.DMA((2 * per_prefix,)),
            ],
        ),
        out_shape=[
            jax.ShapeDtypeStruct(q.shape, bf16),
            jax.ShapeDtypeStruct(q.shape, bf16),
            jax.ShapeDtypeStruct((count, width), bf16),
        ] + [jax.ShapeDtypeStruct(sum_shape, bf16)] * (2 * ranks),
        input_output_aliases={9 + 2 * ranks: 0, 10 + 2 * ranks: 1} if chained else {},
        compiler_params=pltpu.CompilerParams(
            vmem_limit_bytes=54 * 2**20, dimension_semantics=("arbitrary",)
        ),
        cost_estimate=pl.CostEstimate(
            flops=heads * 6 * 2 * keys * 256 * 256, bytes_accessed=groups * 4 * 2**20,
            transcendentals=heads * keys * count,
        ),
    )(owner, tokens, place, q, g, leaf_kv, leaf_kv, leaf, mask, *sources, *earlier)


def shards(
    query, leaf_key_value, prefix_key_value, d_out, block_owner, subtree_tokens, leaf_id, loss_mask
):
    devices = lax.axis_size("dp")
    ranks = 2 if devices == 16 else 1
    planes = devices // (2 * ranks)
    place = lax.axis_index("dp").astype(jnp.int32).reshape(1)
    mask = loss_mask.reshape(1, -1)
    f32 = jnp.float32

    def index(plane, rank, core):
        return (plane % planes * ranks + rank % ranks) * 2 + core % 2

    def send(array, plane_step, rank_step, core_step):
        pairs = [
            (index(p, r, c), index(p + plane_step, r + rank_step, c + core_step))
            for p in range(planes) for r in range(ranks) for c in range(2)
        ]
        return lax.ppermute(array, "dp", pairs)

    middle = KEY_VALUE_HEADS * HEAD_SIZE

    def tie(value, *others):
        return lax.optimization_barrier((value, *others))[0]

    def by_planes(chunk):
        low = sum(CHUNKS[:chunk]) * HEAD_SIZE
        high = low + CHUNKS[chunk] * HEAD_SIZE
        mine = jnp.concatenate(
            [prefix_key_value[:, low:high], prefix_key_value[:, middle + low:middle + high]], axis=1
        )
        return jnp.concatenate([mine] + [send(mine, k, 0, 0) for k in range(1, planes)], axis=0)

    def add(own, received):
        return own.astype(f32) + received.astype(f32)

    def reduce_ranks(totals, away):
        total = add(totals[0], send(totals[1], 0, 0, 1))
        return add(total, send(away, 0, 1, 0)) if ranks == 2 else total

    def reduce_planes(total):
        mine = total[0]
        for k in range(1, planes):
            mine = add(mine, send(total[k].astype(jnp.bfloat16), k, 0, 0))
        return mine.astype(jnp.bfloat16)

    chunks = len(CHUNKS)
    near = [by_planes(chunk) for chunk in range(chunks)]
    near_far = [send(n, 0, 0, 1) for n in near]
    other = [send(n, 0, 1, 0) for n in near] if ranks == 2 else []
    d_leaf, d_prefix, earlier = [], [], ()
    parts = []
    for chunk in range(chunks):
        first = [place] + near[chunk + 1:chunk + 2] + near_far[chunk + 1:chunk + 2]
        if chunk and ranks == 2:
            first.append(parts[-1][1])
        sources = [near[chunk], near_far[chunk]]
        if ranks == 2:
            row = tie(other[chunk], d_leaf[-1] if chunk else near[1])
            sources += [row, send(row, 0, 0, 1)]
        attended, d_query, leaf_part, *totals = attention(
            chunk, block_owner, subtree_tokens, tie(*first), query, d_out, leaf_key_value,
            leaf_id, mask, sources, earlier, planes, ranks,
        )
        earlier = (attended, d_query)
        d_leaf.append(leaf_part)
        away = add(totals[2], send(totals[3], 0, 0, 1)).astype(jnp.bfloat16) if ranks == 2 else None
        parts.append((totals, away))
    d_prefix = [reduce_planes(reduce_ranks(*part)) for part in parts]

    def join(parts):
        halves = [jnp.split(p, 2, axis=1) for p in parts]
        return jnp.concatenate([h[0] for h in halves] + [h[1] for h in halves], axis=1)

    return attended, d_query, join(d_leaf), join(d_prefix)


def solution(mesh):
    rows = P(("groups", "dp"), None)
    in_specs = (rows, rows, rows, rows, P("groups"), P("groups"), rows, P(("groups", "dp")))
    return jax.shard_map(
        shards, mesh=mesh, in_specs=in_specs, out_specs=(rows,) * 4, check_vma=False
    )
```

```python
import functools

import jax
import jax.numpy as jnp
from jax import lax
from jax.experimental import pallas as pl
from jax.experimental.pallas import tpu as pltpu
from jax.sharding import PartitionSpec as P

HEAD_SIZE = 128
KEY_VALUE_HEADS = 4
GQ = 8
SCALE = HEAD_SIZE ** (-0.5)
LOG2E = 1.4426950408889634


def dot(a, b, contract):
    return lax.dot_general(a, b, (contract, ((), ())), preferred_element_type=jnp.float32)

CHUNKS = (2, 2)
STEP_HEADS = (4, 2)
PIECE = 32


def prefixes_here(tokens_ref, place, count, prompts):
    first = place * count
    last = first + (count - 1)
    end = jnp.int32(0)
    pair_first = jnp.int32(0)
    pair_last = jnp.int32(0)
    border = jnp.int32(2**30)
    for p in range(prompts):
        end = end + tokens_ref[p]
        pair_first = pair_first + (end <= first).astype(jnp.int32)
        pair_last = pair_last + (end <= last).astype(jnp.int32)
        border = jnp.where(end > first, jnp.minimum(border, end), border)
    return pair_first, pair_last, border - first


def gradient_kernel(
    owner_ref, tokens_ref, place_ref,
    q_ref, g_ref, leaf_k_ref, leaf_v_ref, leaf_ref, mask_ref, *rest,
    prompts, per_prefix, block_len, planes, ranks, steps, step_heads,
):
    sources = rest[:2 * ranks]
    dleaf_ref, probs_out, dscore_out, kcat_t, vcat_t = rest[2 * ranks:2 * ranks + 5]
    totals = rest[2 * ranks + 5:4 * ranks + 5]
    (kv, kcat, vcat, bias, q_pick, g_pick, q2, g2, scores, dprob, probs_b, dscore,
     dk_sum, dv_sum, sems, out_sems) = rest[4 * ranks + 5:]
    step = pl.program_id(0)
    per_group = GQ // step_heads
    count = q_ref.shape[0]
    columns = step_heads * count
    span = per_prefix * block_len
    keys = span + count
    half = sources[0].shape[1] // 2

    place = place_ref[0]
    pair_first, pair_last, border = prefixes_here(tokens_ref, place, count, prompts)

    def block_place(side, j):
        prefix = pair_first if side == 0 else pair_last
        owner = owner_ref[prefix * per_prefix + j]
        same_core = lax.rem(owner, 2) == lax.rem(place, 2)
        row = lax.rem(owner // 2 + place // 2, ranks)
        ahead = lax.rem(owner // (2 * ranks) + planes - place // (2 * ranks), planes)
        return same_core, row, ahead

    def key_columns(group):
        return pl.ds(pl.multiple_of(group * HEAD_SIZE, HEAD_SIZE), HEAD_SIZE)

    def value_columns(group):
        return pl.ds(pl.multiple_of(half + group * HEAD_SIZE, HEAD_SIZE), HEAD_SIZE)

    @pl.when(step == 0)
    def _():
        for side in range(2):
            for j in range(per_prefix):
                n = side * per_prefix + j
                same_core, row, ahead = block_place(side, j)
                slot = lax.rem(planes - ahead, planes)
                rows = pl.ds(pl.multiple_of(slot * block_len, block_len), block_len)
                target = kv.at[pl.ds(n * block_len, block_len), :]
                for at, source in enumerate(sources):
                    @pl.when((same_core == (at % 2 == 0)) & (row == at // 2))
                    def _():
                        pltpu.make_async_copy(source.at[rows, :], target, sems.at[n]).start()

        leaf_row = jnp.broadcast_to(leaf_ref[...], (count, count))
        leaf_col = leaf_row.T
        key_at = lax.broadcasted_iota(jnp.int32, (count, count), 0)
        token_at = lax.broadcasted_iota(jnp.int32, (count, count), 1)
        same = (leaf_row == leaf_col) & (key_at <= token_at)
        same = same & ((key_at < border) == (token_at < border))
        allowed_bias = jnp.where(same, 0.0, -1e30).astype(jnp.float32)
        mask_col = jnp.broadcast_to(mask_ref[...], (count, count)).T.astype(jnp.float32)
        in_first = key_at < border
        left = token_at < HEAD_SIZE
        pick = (in_first == left).astype(jnp.float32)
        q_pick[...] = pick.astype(jnp.bfloat16)
        g_pick[...] = (pick * mask_col).astype(jnp.bfloat16)
        for n in range(step_heads):
            bias[:, n * count:(n + 1) * count] = allowed_bias
        for ref in totals:
            ref[...] = jnp.zeros_like(ref)
        dk_sum[...] = jnp.zeros_like(dk_sum)
        dv_sum[...] = jnp.zeros_like(dv_sum)
        for n in range(2 * per_prefix):
            target = kv.at[pl.ds(n * block_len, block_len), :]
            pltpu.make_async_copy(
                sources[0].at[pl.ds(0, block_len), :], target, sems.at[n]
            ).wait()

    new_group = lax.rem(step, per_group) == 0

    @pl.when(new_group & (step < steps))
    def _():
        group = step // per_group
        for cat, cat_t, cols, leaf in (
            (kcat, kcat_t, key_columns(group), leaf_k_ref),
            (vcat, vcat_t, value_columns(group), leaf_v_ref),
        ):
            for side in range(2):
                lanes = slice(side * HEAD_SIZE, (side + 1) * HEAD_SIZE)
                cat[0:span, lanes] = kv[side * span:(side + 1) * span, cols]
                cat[span:, lanes] = leaf[...]
            cat_t[0] = cat[...].T

    slot = lax.rem(step, 2)
    before = 1 - slot

    def copies_out(at, slot):
        return [
            pltpu.make_async_copy(probs_b.at[slot], probs_out.at[at], out_sems.at[0, slot]),
            pltpu.make_async_copy(dscore.at[slot], dscore_out.at[at], out_sems.at[1, slot]),
        ]

    def later_rows():
        dk_sum[...] += dot(dscore[before], q2[...], ((1,), (0,)))
        dv_sum[...] += dot(probs_b[before], g2[...], ((1,), (0,)))


    def pick(source, chosen):
        parts = []
        for n in range(step_heads):
            part = source[:, n * HEAD_SIZE:(n + 1) * HEAD_SIZE]
            parts.append(jnp.concatenate([part, part], axis=1) * chosen[...])
        return jnp.concatenate(parts, axis=0)

    def fold(value, op):
        value = value.reshape(PIECE // 8, 8, columns)
        total = value[0]
        for n in range(1, PIECE // 8):
            total = op(total, value[n])
        return total

    def score(new_q):
        product = dot(kcat[...], new_q, ((1,), (1,)))
        top = None
        for at in range(0, keys, PIECE):
            piece = product[at:at + PIECE]
            if at >= span:
                piece = piece + bias[at - span:at - span + PIECE, :]
            scores[at:at + PIECE, :] = piece
            piece = fold(piece, jnp.maximum)
            top = piece if top is None else jnp.maximum(top, piece)
        return jnp.max(top, axis=0, keepdims=True)

    def sums(top):
        total = jnp.zeros((8, columns), jnp.float32)
        delta = jnp.zeros((8, columns), jnp.float32)
        for at in range(0, keys, PIECE):
            weight = jnp.exp2((scores[at:at + PIECE, :] - top) * (SCALE * LOG2E))
            total = total + fold(weight, jnp.add)
            delta = delta + fold(weight * dprob[at:at + PIECE, :], jnp.add)
        total = jnp.sum(total, axis=0, keepdims=True)
        return total, jnp.sum(delta, axis=0, keepdims=True) / total

    def finish(top, total, delta):
        shift = jnp.log2(total)
        for at in range(0, keys, PIECE):
            power = (scores[at:at + PIECE, :] - top) * (SCALE * LOG2E)
            probs = jnp.exp2(power - shift)
            probs_b[slot, at:at + PIECE, :] = probs.astype(jnp.bfloat16)
            dscore[slot, at:at + PIECE, :] = (probs * (dprob[at:at + PIECE, :] - delta)).astype(jnp.bfloat16)

    def work(later):
        new_q = pick(q_ref, q_pick)
        new_g = pick(g_ref, g_pick)
        top = score(new_q)
        if later:
            later_rows()
        dprob[...] = dot(vcat[...], new_g, ((1,), (1,)))
        total, delta = sums(top)
        finish(top, total, delta)
        q2[...] = new_q
        g2[...] = new_g

    @pl.when((step >= 2) & (step < steps))
    def _():
        for copy in copies_out(step - 2, slot):
            copy.wait()

    @pl.when(step == 0)
    def _():
        work(False)

    @pl.when((step > 0) & (step < steps))
    def _():
        work(True)

    @pl.when(step < steps)
    def _():
        for copy in copies_out(step, slot):
            copy.start()

    @pl.when(step == steps)
    def _():
        later_rows()
        for at in range(max(steps - 2, 0), steps):
            for copy in copies_out(at, at % 2):
                copy.wait()

    @pl.when(new_group & (step > 0))
    def _():
        group = step // per_group - 1
        for total_ref, cols, factor in (
            (dk_sum, key_columns(group), SCALE), (dv_sum, value_columns(group), 1.0)
        ):
            leaf = (total_ref[span:, :HEAD_SIZE] + total_ref[span:, HEAD_SIZE:]) * factor
            dleaf_ref[:, cols] = leaf.astype(jnp.bfloat16)
            for side in range(2):
                lanes = slice(side * HEAD_SIZE, (side + 1) * HEAD_SIZE)
                for j in range(per_prefix):
                    value = total_ref[j * block_len:(j + 1) * block_len, lanes] * factor
                    value = value.astype(jnp.bfloat16)
                    same_core, row, ahead = block_place(side, j)
                    for at, ref in enumerate(totals):
                        @pl.when((same_core == (at % 2 == 0)) & (row == at // 2))
                        def _():
                            ref[ahead, :, cols] += value

        dk_sum[...] = jnp.zeros_like(dk_sum)
        dv_sum[...] = jnp.zeros_like(dv_sum)


def query_kernel(
    tokens_ref, place_ref, probs_ref, dscore_ref, vcat_t, kcat_t, *rest, prompts, step_heads, chained
):
    out_ref, dq_ref = rest[2 * chained:]
    count = out_ref.shape[0]
    border = prefixes_here(tokens_ref, place_ref[0], count, prompts)[2]
    columns = step_heads * count
    token_at = lax.rem(lax.broadcasted_iota(jnp.int32, (HEAD_SIZE, columns), 1), count)
    first_side = token_at < border
    for source, cat_t, factor, target in (
        (probs_ref, vcat_t, 1.0, out_ref), (dscore_ref, kcat_t, SCALE, dq_ref)
    ):
        both = dot(cat_t[0], source[0], ((1,), (0,)))
        mine = jnp.where(first_side, both[:HEAD_SIZE], both[HEAD_SIZE:])
        if factor != 1.0:
            mine = mine * factor
        for n in range(step_heads):
            lanes = slice(n * HEAD_SIZE, (n + 1) * HEAD_SIZE)
            target[:, lanes] = mine[:, n * count:(n + 1) * count].T.astype(jnp.bfloat16)


def full(shape):
    return pl.BlockSpec(shape, lambda i, *_: (0,) * len(shape))


def gradients(chunk, owner, tokens, place, q, g, leaf_kv, leaf, mask, sources, planes, ranks):
    count = q.shape[0]
    block_len = sources[0].shape[0] // planes
    prompts = tokens.shape[0]
    per_prefix = owner.shape[0] // prompts
    span = per_prefix * block_len
    keys = span + count
    width = sources[0].shape[1]
    groups = CHUNKS[chunk]
    step_heads = STEP_HEADS[chunk]
    skipped = sum(CHUNKS[:chunk])
    heads = groups * GQ
    steps = heads // step_heads
    per_group = GQ // step_heads
    skipped_steps = skipped * per_group
    columns = step_heads * count
    bf16, f32 = jnp.bfloat16, jnp.float32

    def now(i):
        return jnp.minimum(i, steps - 1)

    slab = pl.BlockSpec(
        (count, step_heads * HEAD_SIZE), lambda i, *_: (0, skipped_steps + now(i))
    )
    leaf_k = pl.BlockSpec(
        (count, HEAD_SIZE), lambda i, *_: (0, skipped + now(i) // per_group)
    )
    leaf_v = pl.BlockSpec(
        (count, HEAD_SIZE),
        lambda i, *_: (0, KEY_VALUE_HEADS + skipped + now(i) // per_group),
    )
    cat_t = pl.BlockSpec((1, 2 * HEAD_SIZE, keys), lambda i, *_: (now(i) // per_group, 0, 0))
    anywhere = pl.BlockSpec(memory_space=pl.ANY)
    sum_shape = (planes, block_len, width)
    probs_shape = jax.ShapeDtypeStruct((steps, keys, columns), bf16)
    cat_t_shape = jax.ShapeDtypeStruct((groups, 2 * HEAD_SIZE, keys), bf16)
    return pl.pallas_call(
        functools.partial(
            gradient_kernel, prompts=prompts, per_prefix=per_prefix, block_len=block_len,
            planes=planes, ranks=ranks, steps=steps, step_heads=step_heads,
        ),
        grid_spec=pltpu.PrefetchScalarGridSpec(
            num_scalar_prefetch=3,
            grid=(steps + 1,),
            in_specs=[
                slab, slab, leaf_k, leaf_v, full(leaf.shape), full(mask.shape),
            ] + [anywhere] * (2 * ranks),
            out_specs=[full((count, width)), anywhere, anywhere, cat_t, cat_t]
            + [full(sum_shape)] * (2 * ranks),
            scratch_shapes=[
                pltpu.VMEM((2 * span, width), bf16),
                pltpu.VMEM((keys, 2 * HEAD_SIZE), bf16),
                pltpu.VMEM((keys, 2 * HEAD_SIZE), bf16),
                pltpu.VMEM((count, columns), f32),
                pltpu.VMEM((count, 2 * HEAD_SIZE), bf16),
                pltpu.VMEM((count, 2 * HEAD_SIZE), bf16),
                pltpu.VMEM((columns, 2 * HEAD_SIZE), bf16),
                pltpu.VMEM((columns, 2 * HEAD_SIZE), bf16),
                pltpu.VMEM((keys, columns), f32),
                pltpu.VMEM((keys, columns), f32),
                pltpu.VMEM((2, keys, columns), bf16),
                pltpu.VMEM((2, keys, columns), bf16),
                pltpu.VMEM((keys, 2 * HEAD_SIZE), f32),
                pltpu.VMEM((keys, 2 * HEAD_SIZE), f32),
                pltpu.SemaphoreType.DMA((2 * per_prefix,)),
                pltpu.SemaphoreType.DMA((2, 2)),
            ],
        ),
        out_shape=[
            jax.ShapeDtypeStruct((count, width), bf16), probs_shape, probs_shape, cat_t_shape,
            cat_t_shape,
        ] + [jax.ShapeDtypeStruct(sum_shape, bf16)] * (2 * ranks),
        compiler_params=pltpu.CompilerParams(
            vmem_limit_bytes=54 * 2**20, dimension_semantics=("arbitrary",)
        ),
        cost_estimate=pl.CostEstimate(
            flops=heads * 4 * 2 * keys * 256 * 256, bytes_accessed=groups * 8 * 2**20,
            transcendentals=2 * heads * keys * count,
        ),
    )(owner, tokens, place, q, g, leaf_kv, leaf_kv, leaf, mask, *sources)


def queries(chunk, part, tokens, place, probs, dscore, kcat_t, vcat_t, like, earlier):
    step_heads = STEP_HEADS[chunk]
    per_group = GQ // step_heads
    count, keys = like.shape[0], probs.shape[1]
    first = (sum(CHUNKS[:chunk]) + part) * per_group
    chained = len(earlier) > 0
    block = pl.BlockSpec(
        (1, keys, step_heads * count), lambda i, *_: (part * per_group + i, 0, 0)
    )
    cat_t = pl.BlockSpec((1, 2 * HEAD_SIZE, keys), lambda i, *_: (part, 0, 0))
    slab = pl.BlockSpec((count, step_heads * HEAD_SIZE), lambda i, *_: (0, first + i))
    anywhere = pl.BlockSpec(memory_space=pl.ANY)
    return pl.pallas_call(
        functools.partial(
            query_kernel, prompts=tokens.shape[0], step_heads=step_heads, chained=chained
        ),
        grid_spec=pltpu.PrefetchScalarGridSpec(
            num_scalar_prefetch=2,
            grid=(per_group,),
            in_specs=[block, block, cat_t, cat_t] + [anywhere] * len(earlier),
            out_specs=[slab, slab],
        ),
        out_shape=[jax.ShapeDtypeStruct(like.shape, jnp.bfloat16)] * 2,
        input_output_aliases={6: 0, 7: 1} if chained else {},
        compiler_params=pltpu.CompilerParams(
            vmem_limit_bytes=54 * 2**20, dimension_semantics=("arbitrary",)
        ),
        cost_estimate=pl.CostEstimate(
            flops=GQ * 2 * 2 * keys * 256 * 256, bytes_accessed=8 * 2**20, transcendentals=0,
        ),
    )(tokens, place, probs, dscore, vcat_t, kcat_t, *earlier)


def shards(
    query, leaf_key_value, prefix_key_value, d_out, block_owner, subtree_tokens, leaf_id, loss_mask
):
    devices = lax.axis_size("dp")
    ranks = 2 if devices == 16 else 1
    planes = devices // (2 * ranks)
    place = lax.axis_index("dp").astype(jnp.int32).reshape(1)
    mask = loss_mask.reshape(1, -1)
    f32 = jnp.float32

    def index(plane, rank, core):
        return (plane % planes * ranks + rank % ranks) * 2 + core % 2

    def send(array, plane_step, rank_step, core_step):
        pairs = [
            (index(p, r, c), index(p + plane_step, r + rank_step, c + core_step))
            for p in range(planes) for r in range(ranks) for c in range(2)
        ]
        return lax.ppermute(array, "dp", pairs)

    middle = KEY_VALUE_HEADS * HEAD_SIZE

    def tie(value, *others):
        return lax.optimization_barrier((value, *others))[0]

    def by_planes(chunk):
        low = sum(CHUNKS[:chunk]) * HEAD_SIZE
        high = low + CHUNKS[chunk] * HEAD_SIZE
        mine = jnp.concatenate(
            [prefix_key_value[:, low:high], prefix_key_value[:, middle + low:middle + high]], axis=1
        )
        return jnp.concatenate([mine] + [send(mine, k, 0, 0) for k in range(1, planes)], axis=0)

    def add(own, received):
        return own.astype(f32) + received.astype(f32)

    def reduce_ranks(totals, away):
        total = add(totals[0], send(totals[1], 0, 0, 1))
        return add(total, send(away, 0, 1, 0)) if ranks == 2 else total

    def for_planes(total):
        return total[0], [total[k].astype(jnp.bfloat16) for k in range(1, planes)]

    def reduce_planes(mine, away):
        for k in range(1, planes):
            mine = add(mine, send(away[k - 1], k, 0, 0))
        return mine.astype(jnp.bfloat16)

    chunks = len(CHUNKS)
    near = [by_planes(chunk) for chunk in range(chunks)]
    near_far = [send(n, 0, 0, 1) for n in near]
    other = [send(n, 0, 1, 0) for n in near] if ranks == 2 else []
    d_leaf, parts, left = [], [], []
    for chunk in range(chunks):
        first = [place] + near[chunk + 1:chunk + 2] + near_far[chunk + 1:chunk + 2]
        if chunk and ranks == 2:
            first.append(parts[-1][1])
        sources = [near[chunk], near_far[chunk]]
        if ranks == 2:
            row = tie(other[chunk], d_leaf[-1] if chunk else near[1])
            sources += [row, send(row, 0, 0, 1)]
        leaf_part, probs, dscore, kcat_t, vcat_t, *totals = gradients(
            chunk, block_owner, subtree_tokens, tie(*first), query, d_out, leaf_key_value,
            leaf_id, mask, sources, planes, ranks,
        )
        left.append((probs, dscore, kcat_t, vcat_t))
        d_leaf.append(leaf_part)
        away = add(totals[2], send(totals[3], 0, 0, 1)).astype(jnp.bfloat16) if ranks == 2 else None
        parts.append((totals, away))
    totals = [for_planes(reduce_ranks(*part)) for part in parts]
    d_prefix = [reduce_planes(*total) for total in totals]
    earlier = ()
    work = [(chunk, part) for chunk in range(chunks) for part in range(CHUNKS[chunk])]
    for at, (chunk, part) in enumerate(work):
        if at < len(work) - 1:
            begun = [away for total in totals[:-1] for away in total[1]]
            begun += [parts[-1][1]] if ranks == 2 else []
        else:
            begun = totals[-1][1]
        after = tie(place, d_leaf[-1], *begun)
        earlier = queries(chunk, part, subtree_tokens, after, *left[chunk], query, earlier)
    attended, d_query = earlier

    def join(parts):
        halves = [jnp.split(p, 2, axis=1) for p in parts]
        return jnp.concatenate([h[0] for h in halves] + [h[1] for h in halves], axis=1)

    return attended, d_query, join(d_leaf), join(d_prefix)


def solution(mesh):
    rows = P(("groups", "dp"), None)
    in_specs = (rows, rows, rows, rows, P("groups"), P("groups"), rows, P(("groups", "dp")))
    return jax.shard_map(
        shards, mesh=mesh, in_specs=in_specs, out_specs=(rows,) * 4, check_vma=False
    )
```

```python
import functools

import jax
import jax.numpy as jnp
from jax import lax
from jax.experimental import pallas as pl
from jax.experimental.pallas import tpu as pltpu
from jax.sharding import PartitionSpec as P

HEAD_SIZE = 128
KEY_VALUE_HEADS = 4
GQ = 8
SCALE = HEAD_SIZE ** (-0.5)
LOG2E = 1.4426950408889634


def dot(a, b, contract):
    return lax.dot_general(a, b, (contract, ((), ())), preferred_element_type=jnp.float32)

CHUNKS = (2, 2)
PAIR = 2
PIECE = 32


def prefixes_here(tokens_ref, place, count, prompts):
    first = place * count
    last = first + (count - 1)
    end = jnp.int32(0)
    pair_first = jnp.int32(0)
    pair_last = jnp.int32(0)
    border = jnp.int32(2**30)
    for p in range(prompts):
        end = end + tokens_ref[p]
        pair_first = pair_first + (end <= first).astype(jnp.int32)
        pair_last = pair_last + (end <= last).astype(jnp.int32)
        border = jnp.where(end > first, jnp.minimum(border, end), border)
    return pair_first, pair_last, border - first


def gradient_kernel(
    owner_ref, tokens_ref, place_ref,
    q_next, g_next, q_here, g_here, leaf_k_ref, leaf_v_ref, leaf_ref, mask_ref, *rest,
    prompts, per_prefix, block_len, planes, ranks, steps,
):
    sources = rest[:2 * ranks]
    dleaf_ref, probs_out, dscore_out, kcat_t, vcat_t = rest[2 * ranks:2 * ranks + 5]
    totals = rest[2 * ranks + 5:4 * ranks + 5]
    (kv, kcat, vcat, bias, q_pick, g_pick, q2, g2, tops, scores, dprob, probs_b, dscore,
     dk_sum, dv_sum, sems, out_sems) = rest[4 * ranks + 5:]
    step = pl.program_id(0)
    per_group = GQ // PAIR
    count = q_next.shape[0]
    columns = PAIR * count
    span = per_prefix * block_len
    keys = span + count
    half = sources[0].shape[1] // 2

    place = place_ref[0]
    pair_first, pair_last, border = prefixes_here(tokens_ref, place, count, prompts)

    def block_place(side, j):
        prefix = pair_first if side == 0 else pair_last
        owner = owner_ref[prefix * per_prefix + j]
        same_core = lax.rem(owner, 2) == lax.rem(place, 2)
        row = lax.rem(owner // 2 + place // 2, ranks)
        ahead = lax.rem(owner // (2 * ranks) + planes - place // (2 * ranks), planes)
        return same_core, row, ahead

    def key_columns(group):
        return pl.ds(pl.multiple_of(group * HEAD_SIZE, HEAD_SIZE), HEAD_SIZE)

    def value_columns(group):
        return pl.ds(pl.multiple_of(half + group * HEAD_SIZE, HEAD_SIZE), HEAD_SIZE)

    @pl.when(step == 0)
    def _():
        for side in range(2):
            for j in range(per_prefix):
                n = side * per_prefix + j
                same_core, row, ahead = block_place(side, j)
                slot = lax.rem(planes - ahead, planes)
                rows = pl.ds(pl.multiple_of(slot * block_len, block_len), block_len)
                target = kv.at[pl.ds(n * block_len, block_len), :]
                for at, source in enumerate(sources):
                    @pl.when((same_core == (at % 2 == 0)) & (row == at // 2))
                    def _():
                        pltpu.make_async_copy(source.at[rows, :], target, sems.at[n]).start()

        leaf_row = jnp.broadcast_to(leaf_ref[...], (count, count))
        leaf_col = leaf_row.T
        key_at = lax.broadcasted_iota(jnp.int32, (count, count), 0)
        token_at = lax.broadcasted_iota(jnp.int32, (count, count), 1)
        same = (leaf_row == leaf_col) & (key_at <= token_at)
        same = same & ((key_at < border) == (token_at < border))
        allowed_bias = jnp.where(same, 0.0, -1e30).astype(jnp.float32)
        mask_col = jnp.broadcast_to(mask_ref[...], (count, count)).T.astype(jnp.float32)
        in_first = key_at < border
        left = token_at < HEAD_SIZE
        pick = (in_first == left).astype(jnp.float32)
        q_pick[...] = pick.astype(jnp.bfloat16)
        g_pick[...] = (pick * mask_col).astype(jnp.bfloat16)
        for n in range(PAIR):
            bias[:, n * count:(n + 1) * count] = allowed_bias
        for ref in totals:
            ref[...] = jnp.zeros_like(ref)
        for ref in (dk_sum, dv_sum, q2, g2):
            ref[...] = jnp.zeros_like(ref)
        probs_b[0, 1] = jnp.zeros((keys, columns), jnp.bfloat16)
        dscore[0, 1] = jnp.zeros((keys, columns), jnp.bfloat16)
        for n in range(2 * per_prefix):
            target = kv.at[pl.ds(n * block_len, block_len), :]
            pltpu.make_async_copy(
                sources[0].at[pl.ds(0, block_len), :], target, sems.at[n]
            ).wait()

    @pl.when((lax.rem(2 * step, per_group) == 0) & (step < steps))
    def _():
        group = 2 * step // per_group
        for cat, cat_t, cols, leaf in (
            (kcat, kcat_t, key_columns(group), leaf_k_ref),
            (vcat, vcat_t, value_columns(group), leaf_v_ref),
        ):
            for side in range(2):
                lanes = slice(side * HEAD_SIZE, (side + 1) * HEAD_SIZE)
                cat[lax.rem(group, 2), 0:span, lanes] = kv[side * span:(side + 1) * span, cols]
                cat[lax.rem(group, 2), span:, lanes] = leaf[...]
            cat_t[0] = cat[lax.rem(group, 2)].T

    slot = lax.rem(step, 2)
    before = 1 - slot

    def copies_out(step):
        slot = lax.rem(step, 2)
        return [
            pltpu.make_async_copy(held.at[slot], out.at[pl.ds(2 * (step - 1), 2)], out_sems.at[n, slot])
            for n, (held, out) in enumerate(((probs_b, probs_out), (dscore, dscore_out)))
        ]

    def group_slot(pair):
        return lax.rem(pair // per_group, 2)

    def rows(slot, side, pair):
        into = group_slot(pair)
        dk_sum[into] += dot(dscore[slot, side], q2[side], ((1,), (0,)))
        dv_sum[into] += dot(probs_b[slot, side], g2[side], ((1,), (0,)))

    def fold(value, op):
        value = value.reshape(PIECE // 8, 8, columns)
        total = value[0]
        for n in range(1, PIECE // 8):
            total = op(total, value[n])
        return total

    def pick_side(source, chosen):
        parts = []
        for n in range(PAIR):
            part = source[:, n * HEAD_SIZE:(n + 1) * HEAD_SIZE]
            parts.append(jnp.concatenate([part, part], axis=1) * chosen[...])
        return jnp.concatenate(parts, axis=0)

    def first(side, pair, q_ref, g_ref):
        new_q = pick_side(q_ref, q_pick)
        new_g = pick_side(g_ref, g_pick)
        q2[side] = new_q
        g2[side] = new_g
        product = dot(kcat[group_slot(pair)], new_q, ((1,), (1,)))
        top = None
        for at in range(0, keys, PIECE):
            piece = product[at:at + PIECE]
            if at >= span:
                piece = piece + bias[at - span:at - span + PIECE, :]
            scores[side, at:at + PIECE, :] = piece
            piece = fold(piece, jnp.maximum)
            top = piece if top is None else jnp.maximum(top, piece)
        tops[side] = jnp.broadcast_to(jnp.max(top, axis=0, keepdims=True), (8, columns))
        dprob[side] = dot(vcat[group_slot(pair)], new_g, ((1,), (1,)))

    def sums(side):
        top = tops[side, 0:1, :]
        total = jnp.zeros((8, columns), jnp.float32)
        delta = jnp.zeros((8, columns), jnp.float32)
        for at in range(0, keys, PIECE):
            weight = jnp.exp2((scores[side, at:at + PIECE, :] - top) * (SCALE * LOG2E))
            total = total + fold(weight, jnp.add)
            delta = delta + fold(weight * dprob[side, at:at + PIECE, :], jnp.add)
        total = jnp.sum(total, axis=0, keepdims=True)
        return top, total, jnp.sum(delta, axis=0, keepdims=True) / total

    def finish(side, top, total, delta):
        shift = jnp.log2(total)
        for at in range(0, keys, PIECE):
            power = (scores[side, at:at + PIECE, :] - top) * (SCALE * LOG2E)
            probs = jnp.exp2(power - shift)
            probs_b[slot, side, at:at + PIECE, :] = probs.astype(jnp.bfloat16)
            dscore[slot, side, at:at + PIECE, :] = (
                probs * (dprob[side, at:at + PIECE, :] - delta)
            ).astype(jnp.bfloat16)

    def work(more):
        rows(before, 1, jnp.maximum(2 * step - 3, 0))
        found = sums(0)
        first(1, 2 * step - 1, q_here, g_here)
        finish(0, *found)
        found = sums(1)
        rows(slot, 0, 2 * step - 2)
        if more:
            first(0, 2 * step, q_next, g_next)
        finish(1, *found)

    @pl.when((step >= 3) & (step <= steps))
    def _():
        for copy in copies_out(step - 2):
            copy.wait()

    @pl.when(step == 0)
    def _():
        first(0, 0, q_next, g_next)

    @pl.when((step > 0) & (step < steps))
    def _():
        work(True)

    @pl.when(step == steps)
    def _():
        work(False)

    @pl.when((step > 0) & (step <= steps))
    def _():
        for copy in copies_out(step):
            copy.start()

    @pl.when(step == steps + 1)
    def _():
        rows(before, 1, 2 * step - 3)
        for at in range(max(steps - 1, 1), steps + 1):
            for copy in copies_out(at):
                copy.wait()

    @pl.when((lax.rem(2 * step - 2, per_group) == 0) & (step > 1))
    def _():
        group = (2 * step - 2) // per_group - 1
        at = lax.rem(group, 2)
        for total_ref, cols, factor in (
            (dk_sum, key_columns(group), SCALE), (dv_sum, value_columns(group), 1.0)
        ):
            leaf = (total_ref[at, span:, :HEAD_SIZE] + total_ref[at, span:, HEAD_SIZE:]) * factor
            dleaf_ref[:, cols] = leaf.astype(jnp.bfloat16)
            for side in range(2):
                lanes = slice(side * HEAD_SIZE, (side + 1) * HEAD_SIZE)
                for j in range(per_prefix):
                    value = total_ref[at, j * block_len:(j + 1) * block_len, lanes] * factor
                    value = value.astype(jnp.bfloat16)
                    same_core, row, ahead = block_place(side, j)
                    for holder, ref in enumerate(totals):
                        @pl.when((same_core == (holder % 2 == 0)) & (row == holder // 2))
                        def _():
                            ref[ahead, :, cols] += value

            total_ref[at] = jnp.zeros((keys, 2 * HEAD_SIZE), jnp.float32)


def query_kernel(
    tokens_ref, place_ref, probs_ref, dscore_ref, vcat_t, kcat_t, *rest, prompts, chained
):
    out_ref, dq_ref = rest[2 * chained:]
    count = out_ref.shape[0]
    border = prefixes_here(tokens_ref, place_ref[0], count, prompts)[2]
    columns = PAIR * count
    token_at = lax.rem(lax.broadcasted_iota(jnp.int32, (HEAD_SIZE, columns), 1), count)
    first_side = token_at < border
    for source, cat_t, factor, target in (
        (probs_ref, vcat_t, 1.0, out_ref), (dscore_ref, kcat_t, SCALE, dq_ref)
    ):
        for pair in range(source.shape[0]):
            both = dot(cat_t[0], source[pair], ((1,), (0,)))
            mine = jnp.where(first_side, both[:HEAD_SIZE], both[HEAD_SIZE:])
            if factor != 1.0:
                mine = mine * factor
            for n in range(PAIR):
                at = (pair * PAIR + n) * HEAD_SIZE
                turned = mine[:, n * count:(n + 1) * count].T
                target[:, at:at + HEAD_SIZE] = turned.astype(jnp.bfloat16)


def full(shape):
    return pl.BlockSpec(shape, lambda i, *_: (0,) * len(shape))


def gradients(chunk, owner, tokens, place, q, g, leaf_kv, leaf, mask, sources, planes, ranks):
    count = q.shape[0]
    block_len = sources[0].shape[0] // planes
    prompts = tokens.shape[0]
    per_prefix = owner.shape[0] // prompts
    span = per_prefix * block_len
    keys = span + count
    width = sources[0].shape[1]
    groups = CHUNKS[chunk]
    skipped = sum(CHUNKS[:chunk])
    heads = groups * GQ
    pairs = heads // PAIR
    steps = pairs // 2
    per_group = GQ // PAIR
    skipped_pairs = skipped * per_group
    columns = PAIR * count
    bf16, f32 = jnp.bfloat16, jnp.float32

    def following(i):
        return jnp.minimum(2 * i, pairs - 1)

    def group_of(i):
        return following(i) // per_group

    def here(i):
        return jnp.clip(2 * i - 1, 0, pairs - 1)

    slab = (count, PAIR * HEAD_SIZE)
    ahead = pl.BlockSpec(slab, lambda i, *_: (0, skipped_pairs + following(i)))
    present = pl.BlockSpec(slab, lambda i, *_: (0, skipped_pairs + here(i)))
    leaf_k = pl.BlockSpec((count, HEAD_SIZE), lambda i, *_: (0, skipped + group_of(i)))
    leaf_v = pl.BlockSpec(
        (count, HEAD_SIZE), lambda i, *_: (0, KEY_VALUE_HEADS + skipped + group_of(i))
    )
    cat_t = pl.BlockSpec((1, 2 * HEAD_SIZE, keys), lambda i, *_: (group_of(i), 0, 0))
    anywhere = pl.BlockSpec(memory_space=pl.ANY)
    sum_shape = (planes, block_len, width)
    probs_shape = jax.ShapeDtypeStruct((pairs, keys, columns), bf16)
    cat_t_shape = jax.ShapeDtypeStruct((groups, 2 * HEAD_SIZE, keys), bf16)
    return pl.pallas_call(
        functools.partial(
            gradient_kernel, prompts=prompts, per_prefix=per_prefix, block_len=block_len,
            planes=planes, ranks=ranks, steps=steps,
        ),
        grid_spec=pltpu.PrefetchScalarGridSpec(
            num_scalar_prefetch=3,
            grid=(steps + 2,),
            in_specs=[
                ahead, ahead, present, present, leaf_k, leaf_v, full(leaf.shape), full(mask.shape),
            ] + [anywhere] * (2 * ranks),
            out_specs=[full((count, width)), anywhere, anywhere, cat_t, cat_t]
            + [full(sum_shape)] * (2 * ranks),
            scratch_shapes=[
                pltpu.VMEM((2 * span, width), bf16),
                pltpu.VMEM((2, keys, 2 * HEAD_SIZE), bf16),
                pltpu.VMEM((2, keys, 2 * HEAD_SIZE), bf16),
                pltpu.VMEM((count, columns), f32),
                pltpu.VMEM((count, 2 * HEAD_SIZE), bf16),
                pltpu.VMEM((count, 2 * HEAD_SIZE), bf16),
                pltpu.VMEM((2, columns, 2 * HEAD_SIZE), bf16),
                pltpu.VMEM((2, columns, 2 * HEAD_SIZE), bf16),
                pltpu.VMEM((2, 8, columns), f32),
                pltpu.VMEM((2, keys, columns), f32),
                pltpu.VMEM((2, keys, columns), f32),
                pltpu.VMEM((2, 2, keys, columns), bf16),
                pltpu.VMEM((2, 2, keys, columns), bf16),
                pltpu.VMEM((2, keys, 2 * HEAD_SIZE), f32),
                pltpu.VMEM((2, keys, 2 * HEAD_SIZE), f32),
                pltpu.SemaphoreType.DMA((2 * per_prefix,)),
                pltpu.SemaphoreType.DMA((2, 2)),
            ],
        ),
        out_shape=[
            jax.ShapeDtypeStruct((count, width), bf16), probs_shape, probs_shape, cat_t_shape,
            cat_t_shape,
        ] + [jax.ShapeDtypeStruct(sum_shape, bf16)] * (2 * ranks),
        compiler_params=pltpu.CompilerParams(
            vmem_limit_bytes=54 * 2**20, dimension_semantics=("arbitrary",)
        ),
        cost_estimate=pl.CostEstimate(
            flops=heads * 4 * 2 * keys * 256 * 256, bytes_accessed=groups * 8 * 2**20,
            transcendentals=2 * heads * keys * count,
        ),
    )(owner, tokens, place, q, g, q, g, leaf_kv, leaf_kv, leaf, mask, *sources)


def queries(chunk, part, tokens, place, probs, dscore, kcat_t, vcat_t, like, earlier):
    count, keys = like.shape[0], probs.shape[1]
    together = 2
    steps = GQ // (PAIR * together)
    first = (sum(CHUNKS[:chunk]) + part) * steps
    chained = len(earlier) > 0
    block = pl.BlockSpec(
        (together, keys, PAIR * count), lambda i, *_: (part * steps + i, 0, 0)
    )
    cat_t = pl.BlockSpec((1, 2 * HEAD_SIZE, keys), lambda i, *_: (part, 0, 0))
    slab = pl.BlockSpec(
        (count, together * PAIR * HEAD_SIZE), lambda i, *_: (0, first + i)
    )
    anywhere = pl.BlockSpec(memory_space=pl.ANY)
    return pl.pallas_call(
        functools.partial(
            query_kernel, prompts=tokens.shape[0], chained=chained
        ),
        grid_spec=pltpu.PrefetchScalarGridSpec(
            num_scalar_prefetch=2,
            grid=(steps,),
            in_specs=[block, block, cat_t, cat_t] + [anywhere] * len(earlier),
            out_specs=[slab, slab],
        ),
        out_shape=[jax.ShapeDtypeStruct(like.shape, jnp.bfloat16)] * 2,
        input_output_aliases={6: 0, 7: 1} if chained else {},
        compiler_params=pltpu.CompilerParams(
            vmem_limit_bytes=54 * 2**20, dimension_semantics=("arbitrary",)
        ),
        cost_estimate=pl.CostEstimate(
            flops=GQ * 2 * 2 * keys * 256 * 256, bytes_accessed=8 * 2**20, transcendentals=0,
        ),
    )(tokens, place, probs, dscore, vcat_t, kcat_t, *earlier)


def shards(
    query, leaf_key_value, prefix_key_value, d_out, block_owner, subtree_tokens, leaf_id, loss_mask
):
    devices = lax.axis_size("dp")
    ranks = 2 if devices == 16 else 1
    planes = devices // (2 * ranks)
    place = lax.axis_index("dp").astype(jnp.int32).reshape(1)
    mask = loss_mask.reshape(1, -1)
    f32 = jnp.float32

    def index(plane, rank, core):
        return (plane % planes * ranks + rank % ranks) * 2 + core % 2

    def send(array, plane_step, rank_step, core_step):
        pairs = [
            (index(p, r, c), index(p + plane_step, r + rank_step, c + core_step))
            for p in range(planes) for r in range(ranks) for c in range(2)
        ]
        return lax.ppermute(array, "dp", pairs)

    middle = KEY_VALUE_HEADS * HEAD_SIZE

    def tie(value, *others):
        return lax.optimization_barrier((value, *others))[0]

    def by_planes(chunk):
        low = sum(CHUNKS[:chunk]) * HEAD_SIZE
        high = low + CHUNKS[chunk] * HEAD_SIZE
        mine = jnp.concatenate(
            [prefix_key_value[:, low:high], prefix_key_value[:, middle + low:middle + high]], axis=1
        )
        return jnp.concatenate([mine] + [send(mine, k, 0, 0) for k in range(1, planes)], axis=0)

    def add(own, received):
        return own.astype(f32) + received.astype(f32)

    def reduce_ranks(totals, away):
        total = add(totals[0], send(totals[1], 0, 0, 1))
        return add(total, send(away, 0, 1, 0)) if ranks == 2 else total

    def for_planes(total):
        return total[0], [total[k].astype(jnp.bfloat16) for k in range(1, planes)]

    def reduce_planes(mine, away):
        for k in range(1, planes):
            mine = add(mine, send(away[k - 1], k, 0, 0))
        return mine.astype(jnp.bfloat16)

    chunks = len(CHUNKS)
    near = [by_planes(chunk) for chunk in range(chunks)]
    near_far = [send(n, 0, 0, 1) for n in near]
    other = [send(n, 0, 1, 0) for n in near] if ranks == 2 else []
    d_leaf, parts, left = [], [], []
    for chunk in range(chunks):
        first = [place] + near[chunk + 1:chunk + 2] + near_far[chunk + 1:chunk + 2]
        if chunk and ranks == 2:
            first.append(parts[-1][1])
        sources = [near[chunk], near_far[chunk]]
        if ranks == 2:
            row = tie(other[chunk], d_leaf[-1] if chunk else near[1])
            sources += [row, send(row, 0, 0, 1)]
        leaf_part, probs, dscore, kcat_t, vcat_t, *totals = gradients(
            chunk, block_owner, subtree_tokens, tie(*first), query, d_out, leaf_key_value,
            leaf_id, mask, sources, planes, ranks,
        )
        left.append((probs, dscore, kcat_t, vcat_t))
        d_leaf.append(leaf_part)
        away = add(totals[2], send(totals[3], 0, 0, 1)).astype(jnp.bfloat16) if ranks == 2 else None
        parts.append((totals, away))
    totals = [for_planes(reduce_ranks(*part)) for part in parts]
    d_prefix = [reduce_planes(*total) for total in totals]
    earlier = ()
    work = [(chunk, part) for chunk in range(chunks) for part in range(CHUNKS[chunk])]
    for at, (chunk, part) in enumerate(work):
        if at < len(work) - 2:
            begun = [away for total in totals[:-1] for away in total[1]]
            begun += [parts[-1][1]] if ranks == 2 else []
        else:
            begun = totals[-1][1]
        after = tie(place, d_leaf[-1], *begun)
        earlier = queries(chunk, part, subtree_tokens, after, *left[chunk], query, earlier)
    attended, d_query = earlier

    def join(parts):
        halves = [jnp.split(p, 2, axis=1) for p in parts]
        return jnp.concatenate([h[0] for h in halves] + [h[1] for h in halves], axis=1)

    return attended, d_query, join(d_leaf), join(d_prefix)


def solution(mesh):
    rows = P(("groups", "dp"), None)
    in_specs = (rows, rows, rows, rows, P("groups"), P("groups"), rows, P(("groups", "dp")))
    return jax.shard_map(
        shards, mesh=mesh, in_specs=in_specs, out_specs=(rows,) * 4, check_vma=False
    )
```

```python
import functools

import jax
import jax.numpy as jnp
from jax import lax
from jax.experimental import pallas as pl
from jax.experimental.pallas import tpu as pltpu
from jax.sharding import PartitionSpec as P

HEAD_SIZE = 128
KEY_VALUE_HEADS = 4
GQ = 8
SCALE = HEAD_SIZE ** (-0.5)
LOG2E = 1.4426950408889634


def dot(a, b, contract):
    return lax.dot_general(a, b, (contract, ((), ())), preferred_element_type=jnp.float32)

CHUNKS = (2, 2)
CALLS = ((0, 0, 2, 4), (1, 0, 1, 2), (1, 1, 1, 2))
PIECE = 32


def attention_kernel(
    owner_ref, tokens_ref, place_ref,
    q_ref, g_ref, leaf_k_ref, leaf_v_ref, leaf_ref, mask_ref, *rest,
    prompts, per_prefix, block_len, planes, ranks, chained, steps, step_heads,
    skipped,
):
    sources = rest[:2 * ranks]
    rest = rest[2 * ranks + 2 * chained:]
    out_ref, dq_ref, dleaf_ref = rest[:3]
    totals = rest[3:3 + 2 * ranks]
    (kv, kcat, vcat, kcat_t, vcat_t, bias, q_pick, g_pick, q2, g2, scores, late_scores, dprob, probs_b, dscore,
     dk_sum, dv_sum, sems) = rest[3 + 2 * ranks:]
    step = pl.program_id(0)
    per_group = GQ // step_heads
    count = q_ref.shape[0]
    columns = step_heads * count
    span = per_prefix * block_len
    keys = span + count
    half = sources[0].shape[1] // 2
    half_out = dleaf_ref.shape[1] // 2

    place = place_ref[0]
    first = place * count
    last = first + (count - 1)
    end = jnp.int32(0)
    pair_first = jnp.int32(0)
    pair_last = jnp.int32(0)
    border = jnp.int32(2**30)
    for p in range(prompts):
        end = end + tokens_ref[p]
        pair_first = pair_first + (end <= first).astype(jnp.int32)
        pair_last = pair_last + (end <= last).astype(jnp.int32)
        border = jnp.where(end > first, jnp.minimum(border, end), border)
    border = border - first

    def block_place(side, j):
        prefix = pair_first if side == 0 else pair_last
        owner = owner_ref[prefix * per_prefix + j]
        same_core = lax.rem(owner, 2) == lax.rem(place, 2)
        row = lax.rem(owner // 2 + place // 2, ranks)
        ahead = lax.rem(owner // (2 * ranks) + planes - place // (2 * ranks), planes)
        return same_core, row, ahead

    def head_columns(low, group):
        return pl.ds(pl.multiple_of(low + group * HEAD_SIZE, HEAD_SIZE), HEAD_SIZE)

    @pl.when(step == 0)
    def _():
        for side in range(2):
            for j in range(per_prefix):
                n = side * per_prefix + j
                same_core, row, ahead = block_place(side, j)
                slot = lax.rem(planes - ahead, planes)
                rows = pl.ds(pl.multiple_of(slot * block_len, block_len), block_len)
                target = kv.at[pl.ds(n * block_len, block_len), :]
                for at, source in enumerate(sources):
                    @pl.when((same_core == (at % 2 == 0)) & (row == at // 2))
                    def _():
                        pltpu.make_async_copy(source.at[rows, :], target, sems.at[n]).start()

        leaf_row = jnp.broadcast_to(leaf_ref[...], (count, count))
        leaf_col = leaf_row.T
        key_at = lax.broadcasted_iota(jnp.int32, (count, count), 0)
        token_at = lax.broadcasted_iota(jnp.int32, (count, count), 1)
        same = (leaf_row == leaf_col) & (key_at <= token_at)
        same = same & ((key_at < border) == (token_at < border))
        allowed_bias = jnp.where(same, 0.0, -1e30).astype(jnp.float32)
        mask_col = jnp.broadcast_to(mask_ref[...], (count, count)).T.astype(jnp.float32)
        in_first = key_at < border
        left = token_at < HEAD_SIZE
        pick = (in_first == left).astype(jnp.float32)
        q_pick[...] = pick.astype(jnp.bfloat16)
        g_pick[...] = (pick * mask_col).astype(jnp.bfloat16)
        for n in range(step_heads):
            bias[:, n * count:(n + 1) * count] = allowed_bias
        for ref in totals:
            ref[...] = jnp.zeros_like(ref)
        for ref in (dk_sum, dv_sum, probs_b, dscore):
            ref[...] = jnp.zeros_like(ref)
        for n in range(2 * per_prefix):
            target = kv.at[pl.ds(n * block_len, block_len), :]
            pltpu.make_async_copy(
                sources[0].at[pl.ds(0, block_len), :], target, sems.at[n]
            ).wait()

    new_group = lax.rem(step, per_group) == 0

    @pl.when(new_group & (step < steps))
    def _():
        group = step // per_group
        for cat, cols, leaf in (
            (kcat, head_columns(0, skipped + group), leaf_k_ref),
            (vcat, head_columns(half, skipped + group), leaf_v_ref),
        ):
            for side in range(2):
                lanes = slice(side * HEAD_SIZE, (side + 1) * HEAD_SIZE)
                cat[0:span, lanes] = kv[side * span:(side + 1) * span, cols]
                cat[span:, lanes] = leaf[...]


    def later_rows():
        dk_sum[...] += dot(dscore[...], q2[...], ((1,), (0,)))
        dv_sum[...] += dot(probs_b[...], g2[...], ((1,), (0,)))

    def later_columns():
        token_at = lax.rem(lax.broadcasted_iota(jnp.int32, (HEAD_SIZE, columns), 1), count)
        first_side = token_at < border
        for source, cat_t, factor, target in (
            (probs_b, vcat_t, 1.0, out_ref), (dscore, kcat_t, SCALE, dq_ref)
        ):
            both = dot(cat_t[...], source[...], ((1,), (0,)))
            mine = jnp.where(first_side, both[:HEAD_SIZE], both[HEAD_SIZE:])
            if factor != 1.0:
                mine = mine * factor
            for n in range(step_heads):
                lanes = slice(n * HEAD_SIZE, (n + 1) * HEAD_SIZE)
                target[:, lanes] = mine[:, n * count:(n + 1) * count].T.astype(jnp.bfloat16)


    def pick(source, chosen):
        parts = []
        for n in range(step_heads):
            part = source[:, n * HEAD_SIZE:(n + 1) * HEAD_SIZE]
            parts.append(jnp.concatenate([part, part], axis=1) * chosen[...])
        return jnp.concatenate(parts, axis=0)

    def fold(value, op):
        value = value.reshape(PIECE // 8, 8, value.shape[1])
        total = value[0]
        for n in range(1, PIECE // 8):
            total = op(total, value[n])
        return total

    def late(wide):
        return jnp.concatenate(
            [wide[:, n * count + count // 2:(n + 1) * count] for n in range(step_heads)], axis=1
        )

    def spread(value, narrow, op):
        parts = []
        for n in range(step_heads):
            low, middle, high = n * count, n * count + count // 2, (n + 1) * count
            mine = narrow[:, n * (count // 2):(n + 1) * (count // 2)]
            parts += [value[:, low:middle], op(value[:, middle:high], mine)]
        return jnp.concatenate(parts, axis=1)

    early_keys = span + count // 2

    def score(new_q):
        product = dot(kcat[...], new_q, ((1,), (1,)))
        top, late_top = None, None
        for at in range(0, keys, PIECE):
            piece = product[at:at + PIECE]
            if at < early_keys:
                if at >= span:
                    piece = piece + bias[at - span:at - span + PIECE, :]
                scores[at:at + PIECE, :] = piece
                piece = fold(piece, jnp.maximum)
                top = piece if top is None else jnp.maximum(top, piece)
            else:
                piece = late(piece) + late(bias[at - span:at - span + PIECE, :])
                late_scores[at - early_keys:at - early_keys + PIECE, :] = piece
                piece = fold(piece, jnp.maximum)
                late_top = piece if late_top is None else jnp.maximum(late_top, piece)
        top = spread(top, late_top, jnp.maximum)
        return jnp.max(top, axis=0, keepdims=True)

    def pieces():
        for at in range(0, early_keys, PIECE):
            yield scores[at:at + PIECE, :], at, False
        for at in range(early_keys, keys, PIECE):
            yield late_scores[at - early_keys:at - early_keys + PIECE, :], at, True

    def sums(top):
        total = jnp.zeros((8, columns), jnp.float32)
        delta = jnp.zeros((8, columns), jnp.float32)
        late_total = jnp.zeros((8, columns // 2), jnp.float32)
        late_delta = jnp.zeros((8, columns // 2), jnp.float32)
        late_top = late(top)
        for value, at, is_late in pieces():
            weight = jnp.exp2((value - (late_top if is_late else top)) * (SCALE * LOG2E))
            if is_late:
                late_total = late_total + fold(weight, jnp.add)
                late_delta = late_delta + fold(weight * late(dprob[at:at + PIECE, :]), jnp.add)
            else:
                total = total + fold(weight, jnp.add)
                delta = delta + fold(weight * dprob[at:at + PIECE, :], jnp.add)
        total = jnp.sum(spread(total, late_total, jnp.add), axis=0, keepdims=True)
        delta = jnp.sum(spread(delta, late_delta, jnp.add), axis=0, keepdims=True)
        return total, delta / total

    def finish(top, total, delta):
        shift = jnp.log2(total)
        late_top, late_shift, late_delta = late(top), late(shift), late(delta)
        for value, at, is_late in pieces():
            power = (value - (late_top if is_late else top)) * (SCALE * LOG2E)
            probs = jnp.exp2(power - (late_shift if is_late else shift))
            rows = slice(at, at + PIECE)
            if not is_late:
                probs_b[rows, :] = probs.astype(jnp.bfloat16)
                dscore[rows, :] = (probs * (dprob[rows, :] - delta)).astype(jnp.bfloat16)
                continue
            change = (probs * (late(dprob[rows, :]) - late_delta)).astype(jnp.bfloat16)
            probs = probs.astype(jnp.bfloat16)
            for n in range(step_heads):
                mine = slice(n * (count // 2), (n + 1) * (count // 2))
                lanes = slice(n * count + count // 2, (n + 1) * count)
                probs_b[rows, lanes] = probs[:, mine]
                dscore[rows, lanes] = change[:, mine]

    def work(later):
        new_q = pick(q_ref, q_pick)
        new_g = pick(g_ref, g_pick)
        top = score(new_q)
        if later:
            later_rows()
        dprob[...] = dot(vcat[...], new_g, ((1,), (1,)))
        total, delta = sums(top)
        if later:
            later_columns()
        finish(top, total, delta)
        q2[...] = new_q
        g2[...] = new_g

    @pl.when(step == 0)
    def _():
        work(False)

    @pl.when((step > 0) & (step < steps))
    def _():
        work(True)

    @pl.when(step == steps)
    def _():
        later_rows()
        later_columns()

    @pl.when(new_group & (step > 0))
    def _():
        group = step // per_group - 1
        for total_ref, cols, factor in (
            (dk_sum, head_columns(0, group), SCALE), (dv_sum, head_columns(half_out, group), 1.0)
        ):
            leaf = (total_ref[span:, :HEAD_SIZE] + total_ref[span:, HEAD_SIZE:]) * factor
            dleaf_ref[:, cols] = leaf.astype(jnp.bfloat16)
            for side in range(2):
                lanes = slice(side * HEAD_SIZE, (side + 1) * HEAD_SIZE)
                for j in range(per_prefix):
                    value = total_ref[j * block_len:(j + 1) * block_len, lanes] * factor
                    value = value.astype(jnp.bfloat16)
                    same_core, row, ahead = block_place(side, j)
                    for at, ref in enumerate(totals):
                        @pl.when((same_core == (at % 2 == 0)) & (row == at // 2))
                        def _():
                            ref[ahead, :, cols] += value

        dk_sum[...] = jnp.zeros_like(dk_sum)
        dv_sum[...] = jnp.zeros_like(dv_sum)

    @pl.when(new_group & (step < steps))
    def _():
        kcat_t[...] = kcat[...].T
        vcat_t[...] = vcat[...].T


def attention(
    call, owner, tokens, place, q, g, leaf_kv, leaf, mask, sources, earlier, planes, ranks
):
    chunk, chunk_skipped, groups, step_heads = call
    count = q.shape[0]
    block_len = sources[0].shape[0] // planes
    prompts = tokens.shape[0]
    per_prefix = owner.shape[0] // prompts
    span = per_prefix * block_len
    keys = span + count
    width = 2 * groups * HEAD_SIZE
    skipped = sum(CHUNKS[:chunk]) + chunk_skipped
    heads = groups * GQ
    steps = heads // step_heads
    per_group = GQ // step_heads
    skipped_steps = skipped * per_group
    bf16, f32 = jnp.bfloat16, jnp.float32

    def now(i):
        return jnp.minimum(i, steps - 1)

    ahead = pl.BlockSpec((count, step_heads * HEAD_SIZE), lambda i, *_: (0, skipped_steps + now(i)))
    behind = pl.BlockSpec(
        (count, step_heads * HEAD_SIZE), lambda i, *_: (0, skipped_steps + jnp.maximum(i - 1, 0))
    )
    leaf_k = pl.BlockSpec(
        (count, HEAD_SIZE), lambda i, *_: (0, skipped + now(i) // per_group)
    )
    leaf_v = pl.BlockSpec(
        (count, HEAD_SIZE),
        lambda i, *_: (0, KEY_VALUE_HEADS + skipped + now(i) // per_group),
    )
    anywhere = pl.BlockSpec(memory_space=pl.ANY)

    def full(shape):
        return pl.BlockSpec(shape, lambda h, *_: (0,) * len(shape))

    sum_shape = (planes, block_len, width)
    chained = len(earlier) > 0
    return pl.pallas_call(
        functools.partial(
            attention_kernel, prompts=prompts, per_prefix=per_prefix, block_len=block_len,
            planes=planes, ranks=ranks, chained=chained, steps=steps, step_heads=step_heads,
            skipped=chunk_skipped,
        ),
        grid_spec=pltpu.PrefetchScalarGridSpec(
            num_scalar_prefetch=3,
            grid=(steps + 1,),
            in_specs=[
                ahead, ahead, leaf_k, leaf_v, full(leaf.shape), full(mask.shape),
            ] + [anywhere] * (2 * ranks + len(earlier)),
            out_specs=[behind, behind, full((count, width))] + [full(sum_shape)] * (2 * ranks),
            scratch_shapes=[
                pltpu.VMEM((2 * span, sources[0].shape[1]), bf16),
                pltpu.VMEM((keys, 2 * HEAD_SIZE), bf16),
                pltpu.VMEM((keys, 2 * HEAD_SIZE), bf16),
                pltpu.VMEM((2 * HEAD_SIZE, keys), bf16),
                pltpu.VMEM((2 * HEAD_SIZE, keys), bf16),
                pltpu.VMEM((count, step_heads * count), f32),
                pltpu.VMEM((count, 2 * HEAD_SIZE), bf16),
                pltpu.VMEM((count, 2 * HEAD_SIZE), bf16),
                pltpu.VMEM((step_heads * count, 2 * HEAD_SIZE), bf16),
                pltpu.VMEM((step_heads * count, 2 * HEAD_SIZE), bf16),
                pltpu.VMEM((span + count // 2, step_heads * count), f32),
                pltpu.VMEM((count - count // 2, step_heads * count // 2), f32),
                pltpu.VMEM((keys, step_heads * count), f32),
                pltpu.VMEM((keys, step_heads * count), bf16),
                pltpu.VMEM((keys, step_heads * count), bf16),
                pltpu.VMEM((keys, 2 * HEAD_SIZE), f32),
                pltpu.VMEM((keys, 2 * HEAD_SIZE), f32),
                pltpu.SemaphoreType.DMA((2 * per_prefix,)),
            ],
        ),
        out_shape=[
            jax.ShapeDtypeStruct(q.shape, bf16),
            jax.ShapeDtypeStruct(q.shape, bf16),
            jax.ShapeDtypeStruct((count, width), bf16),
        ] + [jax.ShapeDtypeStruct(sum_shape, bf16)] * (2 * ranks),
        input_output_aliases={9 + 2 * ranks: 0, 10 + 2 * ranks: 1} if chained else {},
        compiler_params=pltpu.CompilerParams(
            vmem_limit_bytes=54 * 2**20, dimension_semantics=("arbitrary",)
        ),
        cost_estimate=pl.CostEstimate(
            flops=heads * 6 * 2 * keys * 256 * 256, bytes_accessed=groups * 4 * 2**20,
            transcendentals=heads * keys * count,
        ),
    )(owner, tokens, place, q, g, leaf_kv, leaf_kv, leaf, mask, *sources, *earlier)


def shards(
    query, leaf_key_value, prefix_key_value, d_out, block_owner, subtree_tokens, leaf_id, loss_mask
):
    devices = lax.axis_size("dp")
    ranks = 2 if devices == 16 else 1
    planes = devices // (2 * ranks)
    place = lax.axis_index("dp").astype(jnp.int32).reshape(1)
    mask = loss_mask.reshape(1, -1)
    f32 = jnp.float32

    def index(plane, rank, core):
        return (plane % planes * ranks + rank % ranks) * 2 + core % 2

    def send(array, plane_step, rank_step, core_step):
        pairs = [
            (index(p, r, c), index(p + plane_step, r + rank_step, c + core_step))
            for p in range(planes) for r in range(ranks) for c in range(2)
        ]
        return lax.ppermute(array, "dp", pairs)

    middle = KEY_VALUE_HEADS * HEAD_SIZE

    def tie(value, *others):
        return lax.optimization_barrier((value, *others))[0]

    def by_planes(chunk):
        low = sum(CHUNKS[:chunk]) * HEAD_SIZE
        high = low + CHUNKS[chunk] * HEAD_SIZE
        mine = jnp.concatenate(
            [prefix_key_value[:, low:high], prefix_key_value[:, middle + low:middle + high]], axis=1
        )
        return jnp.concatenate([mine] + [send(mine, k, 0, 0) for k in range(1, planes)], axis=0)

    def add(own, received):
        return own.astype(f32) + received.astype(f32)

    def reduce_ranks(totals, away, *last):
        total = add(totals[0], send(totals[1], 0, 0, 1))
        return add(total, tie(send(away, 0, 1, 0), *last)) if ranks == 2 else total

    def for_planes(total):
        return total[0], [total[k].astype(jnp.bfloat16) for k in range(1, planes)]

    def reduce_planes(mine, away, last):
        for k in range(1, planes):
            mine = add(mine, tie(send(away[k - 1], k, 0, 0), last))
        return mine.astype(jnp.bfloat16)

    chunks = len(CHUNKS)
    near = [by_planes(chunk) for chunk in range(chunks)]
    near_far = [send(n, 0, 0, 1) for n in near]
    other = [send(n, 0, 1, 0) for n in near] if ranks == 2 else []
    d_leaf, parts, by_ranks, earlier = [], [], [], ()
    for at, call in enumerate(CALLS):
        chunk, new_chunk = call[0], call[1] == 0
        first = [place]
        if new_chunk:
            first += near[chunk + 1:chunk + 2] + near_far[chunk + 1:chunk + 2]
            sources = [near[chunk], near_far[chunk]]
            if ranks == 2:
                row = tie(other[chunk], d_leaf[-1] if chunk else near[1])
                sources += [row, send(row, 0, 0, 1)]
        if at >= 1 and ranks == 2:
            first.append(parts[-1][1])
        if at >= 2:
            by_ranks.append(for_planes(reduce_ranks(*parts[at - 2])))
            first += by_ranks[-1][1]
        attended, d_query, leaf_part, *totals = attention(
            call, block_owner, subtree_tokens, tie(*first), query, d_out, leaf_key_value,
            leaf_id, mask, sources, earlier, planes, ranks,
        )
        earlier = (attended, d_query)
        d_leaf.append(leaf_part)
        if at == len(CALLS) - 1:
            d_prefix = [reduce_planes(*total, leaf_part) for total in by_ranks]
            totals[-1] = tie(totals[-1], *d_prefix)
        away = add(totals[2], send(totals[3], 0, 0, 1)).astype(jnp.bfloat16) if ranks == 2 else None
        parts.append((totals, away))
    for part in parts[len(d_prefix):]:
        total = for_planes(reduce_ranks(*part, d_leaf[-1]))
        d_prefix.append(reduce_planes(*total, d_leaf[-1] if ranks == 1 else parts[-1][1]))
    d_leaf = [tie(part, d_leaf[-1]) for part in d_leaf[:-1]] + d_leaf[-1:]

    def join(parts):
        halves = [jnp.split(p, 2, axis=1) for p in parts]
        return jnp.concatenate([h[0] for h in halves] + [h[1] for h in halves], axis=1)

    return attended, d_query, join(d_leaf), join(d_prefix)


def solution(mesh):
    rows = P(("groups", "dp"), None)
    in_specs = (rows, rows, rows, rows, P("groups"), P("groups"), rows, P(("groups", "dp")))
    return jax.shard_map(
        shards, mesh=mesh, in_specs=in_specs, out_specs=(rows,) * 4, check_vma=False
    )
```

```python
import functools

import jax
import jax.numpy as jnp
from jax import lax
from jax.experimental import pallas as pl
from jax.experimental.pallas import tpu as pltpu
from jax.sharding import PartitionSpec as P

HEAD_SIZE = 128
KEY_VALUE_HEADS = 4
GQ = 8
SCALE = HEAD_SIZE ** (-0.5)
LOG2E = 1.4426950408889634


def dot(a, b, contract):
    return lax.dot_general(a, b, (contract, ((), ())), preferred_element_type=jnp.float32)

CHUNKS = (2, 2)
STEP_HEADS = (4, 2)
PIECES = (32, 16)
TURNED = (True, False)


def attention_kernel(
    owner_ref, tokens_ref, place_ref,
    q_ref, g_ref, leaf_k_ref, leaf_v_ref, leaf_ref, mask_ref, *rest,
    prompts, per_prefix, block_len, planes, ranks, chained, steps, step_heads,
    piece_rows, turned,
):
    sources = rest[:2 * ranks]
    rest = rest[2 * ranks + 2 * chained:]
    out_ref, dq_ref, dleaf_ref = rest[:3]
    totals = rest[3:3 + 2 * ranks]
    (kv, kcat, vcat, kcat_t, vcat_t, bias, q_pick, g_pick, q_pick_t, g_pick_t, q2, g2, scores, dprob, probs_b, dscore,
     dk_sum, dv_sum, sems) = rest[3 + 2 * ranks:]
    step = pl.program_id(0)
    per_group = GQ // step_heads
    count = q_ref.shape[0]
    columns = step_heads * count
    span = per_prefix * block_len
    keys = span + count
    half = sources[0].shape[1] // 2

    place = place_ref[0]
    first = place * count
    last = first + (count - 1)
    end = jnp.int32(0)
    pair_first = jnp.int32(0)
    pair_last = jnp.int32(0)
    border = jnp.int32(2**30)
    for p in range(prompts):
        end = end + tokens_ref[p]
        pair_first = pair_first + (end <= first).astype(jnp.int32)
        pair_last = pair_last + (end <= last).astype(jnp.int32)
        border = jnp.where(end > first, jnp.minimum(border, end), border)
    border = border - first

    def block_place(side, j):
        prefix = pair_first if side == 0 else pair_last
        owner = owner_ref[prefix * per_prefix + j]
        same_core = lax.rem(owner, 2) == lax.rem(place, 2)
        row = lax.rem(owner // 2 + place // 2, ranks)
        ahead = lax.rem(owner // (2 * ranks) + planes - place // (2 * ranks), planes)
        return same_core, row, ahead

    def key_columns(group):
        return pl.ds(pl.multiple_of(group * HEAD_SIZE, HEAD_SIZE), HEAD_SIZE)

    def value_columns(group):
        return pl.ds(pl.multiple_of(half + group * HEAD_SIZE, HEAD_SIZE), HEAD_SIZE)

    @pl.when(step == 0)
    def _():
        for side in range(2):
            for j in range(per_prefix):
                n = side * per_prefix + j
                same_core, row, ahead = block_place(side, j)
                slot = lax.rem(planes - ahead, planes)
                rows = pl.ds(pl.multiple_of(slot * block_len, block_len), block_len)
                target = kv.at[pl.ds(n * block_len, block_len), :]
                for at, source in enumerate(sources):
                    @pl.when((same_core == (at % 2 == 0)) & (row == at // 2))
                    def _():
                        pltpu.make_async_copy(source.at[rows, :], target, sems.at[n]).start()

        leaf_row = jnp.broadcast_to(leaf_ref[...], (count, count))
        leaf_col = leaf_row.T
        key_at = lax.broadcasted_iota(jnp.int32, (count, count), 0)
        token_at = lax.broadcasted_iota(jnp.int32, (count, count), 1)
        same = (leaf_row == leaf_col) & (key_at <= token_at)
        same = same & ((key_at < border) == (token_at < border))
        allowed_bias = jnp.where(same, 0.0, -1e30).astype(jnp.float32)
        mask_col = jnp.broadcast_to(mask_ref[...], (count, count)).T.astype(jnp.float32)
        in_first = key_at < border
        left = token_at < HEAD_SIZE
        pick = (in_first == left).astype(jnp.float32)
        q_pick[...] = pick.astype(jnp.bfloat16)
        g_pick[...] = (pick * mask_col).astype(jnp.bfloat16)
        q_pick_t[...] = q_pick[...].T
        g_pick_t[...] = g_pick[...].T
        for n in range(step_heads):
            bias[:, n * count:(n + 1) * count] = allowed_bias
        for ref in totals:
            ref[...] = jnp.zeros_like(ref)
        dk_sum[...] = jnp.zeros_like(dk_sum)
        dv_sum[...] = jnp.zeros_like(dv_sum)
        for n in range(2 * per_prefix):
            target = kv.at[pl.ds(n * block_len, block_len), :]
            pltpu.make_async_copy(
                sources[0].at[pl.ds(0, block_len), :], target, sems.at[n]
            ).wait()

    new_group = lax.rem(step, per_group) == 0

    @pl.when(new_group & (step < steps))
    def _():
        group = step // per_group
        for cat, cols, leaf in (
            (kcat, key_columns(group), leaf_k_ref), (vcat, value_columns(group), leaf_v_ref)
        ):
            for side in range(2):
                lanes = slice(side * HEAD_SIZE, (side + 1) * HEAD_SIZE)
                cat[0:span, lanes] = kv[side * span:(side + 1) * span, cols]
                cat[span:, lanes] = leaf[...]


    def later_rows():
        dk_sum[...] += dot(dscore[...], q2[...], ((1,), (0,)))
        dv_sum[...] += dot(probs_b[...], g2[...], ((1,), (0,)))

    def later_columns():
        token_at = lax.rem(lax.broadcasted_iota(jnp.int32, (HEAD_SIZE, columns), 1), count)
        first_side = token_at < border
        for source, cat_t, factor, target in (
            (probs_b, vcat_t, 1.0, out_ref), (dscore, kcat_t, SCALE, dq_ref)
        ):
            both = dot(cat_t[...], source[...], ((1,), (0,)))
            mine = jnp.where(first_side, both[:HEAD_SIZE], both[HEAD_SIZE:])
            if factor != 1.0:
                mine = mine * factor
            for n in range(step_heads):
                lanes = slice(n * HEAD_SIZE, (n + 1) * HEAD_SIZE)
                target[:, lanes] = mine[:, n * count:(n + 1) * count].T.astype(jnp.bfloat16)


    def pick(source, chosen):
        parts = []
        for n in range(step_heads):
            part = source[:, n * HEAD_SIZE:(n + 1) * HEAD_SIZE]
            parts.append(jnp.concatenate([part, part], axis=1) * chosen[...])
        return jnp.concatenate(parts, axis=0)

    def times(cat, new, source, chosen_t):
        if not turned:
            return dot(cat[...], new, ((1,), (1,)))
        parts = []
        for n in range(step_heads):
            part = source[:, n * HEAD_SIZE:(n + 1) * HEAD_SIZE].T
            parts.append(jnp.concatenate([part, part], axis=0) * chosen_t[...])
        return dot(cat[...], jnp.concatenate(parts, axis=1), ((1,), (0,)))

    def fold(value, op):
        value = value.reshape(piece_rows // 8, 8, columns)
        total = value[0]
        for n in range(1, piece_rows // 8):
            total = op(total, value[n])
        return total

    def score(new_q):
        product = times(kcat, new_q, q_ref, q_pick_t)
        top = None
        for at in range(0, keys, piece_rows):
            piece = product[at:at + piece_rows]
            if at >= span:
                piece = piece + bias[at - span:at - span + piece_rows, :]
            scores[at:at + piece_rows, :] = piece
            piece = fold(piece, jnp.maximum)
            top = piece if top is None else jnp.maximum(top, piece)
        return jnp.max(top, axis=0, keepdims=True)

    def sums(top):
        total = jnp.zeros((8, columns), jnp.float32)
        delta = jnp.zeros((8, columns), jnp.float32)
        for at in range(0, keys, piece_rows):
            weight = jnp.exp2((scores[at:at + piece_rows, :] - top) * (SCALE * LOG2E))
            total = total + fold(weight, jnp.add)
            delta = delta + fold(weight * dprob[at:at + piece_rows, :], jnp.add)
        total = jnp.sum(total, axis=0, keepdims=True)
        return total, jnp.sum(delta, axis=0, keepdims=True) / total

    def finish(top, total, delta):
        shift = jnp.log2(total)
        for at in range(0, keys, piece_rows):
            power = (scores[at:at + piece_rows, :] - top) * (SCALE * LOG2E)
            probs = jnp.exp2(power - shift)
            probs_b[at:at + piece_rows, :] = probs.astype(jnp.bfloat16)
            dscore[at:at + piece_rows, :] = (probs * (dprob[at:at + piece_rows, :] - delta)).astype(jnp.bfloat16)

    def work(later):
        new_q = pick(q_ref, q_pick)
        new_g = pick(g_ref, g_pick)
        top = score(new_q)
        if later:
            later_rows()
        dprob[...] = times(vcat, new_g, g_ref, g_pick_t)
        total, delta = sums(top)
        if later:
            later_columns()
        finish(top, total, delta)
        q2[...] = new_q
        g2[...] = new_g

    @pl.when(step == 0)
    def _():
        work(False)

    @pl.when((step > 0) & (step < steps))
    def _():
        work(True)

    @pl.when(step == steps)
    def _():
        later_rows()
        later_columns()

    @pl.when(new_group & (step > 0))
    def _():
        group = step // per_group - 1
        for total_ref, cols, factor in (
            (dk_sum, key_columns(group), SCALE), (dv_sum, value_columns(group), 1.0)
        ):
            leaf = (total_ref[span:, :HEAD_SIZE] + total_ref[span:, HEAD_SIZE:]) * factor
            dleaf_ref[:, cols] = leaf.astype(jnp.bfloat16)
            for side in range(2):
                lanes = slice(side * HEAD_SIZE, (side + 1) * HEAD_SIZE)
                for j in range(per_prefix):
                    value = total_ref[j * block_len:(j + 1) * block_len, lanes] * factor
                    value = value.astype(jnp.bfloat16)
                    same_core, row, ahead = block_place(side, j)
                    for at, ref in enumerate(totals):
                        @pl.when((same_core == (at % 2 == 0)) & (row == at // 2))
                        def _():
                            ref[ahead, :, cols] += value

        dk_sum[...] = jnp.zeros_like(dk_sum)
        dv_sum[...] = jnp.zeros_like(dv_sum)

    @pl.when(new_group & (step < steps))
    def _():
        kcat_t[...] = kcat[...].T
        vcat_t[...] = vcat[...].T


def attention(
    chunk, owner, tokens, place, q, g, leaf_kv, leaf, mask, sources, earlier, planes, ranks
):
    count = q.shape[0]
    block_len = sources[0].shape[0] // planes
    prompts = tokens.shape[0]
    per_prefix = owner.shape[0] // prompts
    span = per_prefix * block_len
    keys = span + count
    width = sources[0].shape[1]
    groups = CHUNKS[chunk]
    step_heads = STEP_HEADS[chunk]
    skipped = sum(CHUNKS[:chunk])
    heads = groups * GQ
    steps = heads // step_heads
    per_group = GQ // step_heads
    skipped_steps = skipped * per_group
    bf16, f32 = jnp.bfloat16, jnp.float32

    def now(i):
        return jnp.minimum(i, steps - 1)

    ahead = pl.BlockSpec((count, step_heads * HEAD_SIZE), lambda i, *_: (0, skipped_steps + now(i)))
    behind = pl.BlockSpec(
        (count, step_heads * HEAD_SIZE), lambda i, *_: (0, skipped_steps + jnp.maximum(i - 1, 0))
    )
    leaf_k = pl.BlockSpec(
        (count, HEAD_SIZE), lambda i, *_: (0, skipped + now(i) // per_group)
    )
    leaf_v = pl.BlockSpec(
        (count, HEAD_SIZE),
        lambda i, *_: (0, KEY_VALUE_HEADS + skipped + now(i) // per_group),
    )
    anywhere = pl.BlockSpec(memory_space=pl.ANY)

    def full(shape):
        return pl.BlockSpec(shape, lambda h, *_: (0,) * len(shape))

    sum_shape = (planes, block_len, width)
    chained = len(earlier) > 0
    return pl.pallas_call(
        functools.partial(
            attention_kernel, prompts=prompts, per_prefix=per_prefix, block_len=block_len,
            planes=planes, ranks=ranks, chained=chained, steps=steps, step_heads=step_heads,
            piece_rows=PIECES[chunk], turned=TURNED[chunk],
        ),
        grid_spec=pltpu.PrefetchScalarGridSpec(
            num_scalar_prefetch=3,
            grid=(steps + 1,),
            in_specs=[
                ahead, ahead, leaf_k, leaf_v, full(leaf.shape), full(mask.shape),
            ] + [anywhere] * (2 * ranks + len(earlier)),
            out_specs=[behind, behind, full((count, width))] + [full(sum_shape)] * (2 * ranks),
            scratch_shapes=[
                pltpu.VMEM((2 * span, width), bf16),
                pltpu.VMEM((keys, 2 * HEAD_SIZE), bf16),
                pltpu.VMEM((keys, 2 * HEAD_SIZE), bf16),
                pltpu.VMEM((2 * HEAD_SIZE, keys), bf16),
                pltpu.VMEM((2 * HEAD_SIZE, keys), bf16),
                pltpu.VMEM((count, step_heads * count), f32),
                pltpu.VMEM((count, 2 * HEAD_SIZE), bf16),
                pltpu.VMEM((count, 2 * HEAD_SIZE), bf16),
                pltpu.VMEM((2 * HEAD_SIZE, count), bf16),
                pltpu.VMEM((2 * HEAD_SIZE, count), bf16),
                pltpu.VMEM((step_heads * count, 2 * HEAD_SIZE), bf16),
                pltpu.VMEM((step_heads * count, 2 * HEAD_SIZE), bf16),
                pltpu.VMEM((keys, step_heads * count), f32),
                pltpu.VMEM((keys, step_heads * count), f32),
                pltpu.VMEM((keys, step_heads * count), bf16),
                pltpu.VMEM((keys, step_heads * count), bf16),
                pltpu.VMEM((keys, 2 * HEAD_SIZE), f32),
                pltpu.VMEM((keys, 2 * HEAD_SIZE), f32),
                pltpu.SemaphoreType.DMA((2 * per_prefix,)),
            ],
        ),
        out_shape=[
            jax.ShapeDtypeStruct(q.shape, bf16),
            jax.ShapeDtypeStruct(q.shape, bf16),
            jax.ShapeDtypeStruct((count, width), bf16),
        ] + [jax.ShapeDtypeStruct(sum_shape, bf16)] * (2 * ranks),
        input_output_aliases={9 + 2 * ranks: 0, 10 + 2 * ranks: 1} if chained else {},
        compiler_params=pltpu.CompilerParams(
            vmem_limit_bytes=54 * 2**20, dimension_semantics=("arbitrary",)
        ),
        cost_estimate=pl.CostEstimate(
            flops=heads * 6 * 2 * keys * 256 * 256, bytes_accessed=groups * 4 * 2**20,
            transcendentals=heads * keys * count,
        ),
    )(owner, tokens, place, q, g, leaf_kv, leaf_kv, leaf, mask, *sources, *earlier)


def shards(
    query, leaf_key_value, prefix_key_value, d_out, block_owner, subtree_tokens, leaf_id, loss_mask
):
    devices = lax.axis_size("dp")
    ranks = 2 if devices == 16 else 1
    planes = devices // (2 * ranks)
    place = lax.axis_index("dp").astype(jnp.int32).reshape(1)
    mask = loss_mask.reshape(1, -1)
    f32 = jnp.float32

    def index(plane, rank, core):
        return (plane % planes * ranks + rank % ranks) * 2 + core % 2

    def send(array, plane_step, rank_step, core_step):
        pairs = [
            (index(p, r, c), index(p + plane_step, r + rank_step, c + core_step))
            for p in range(planes) for r in range(ranks) for c in range(2)
        ]
        return lax.ppermute(array, "dp", pairs)

    middle = KEY_VALUE_HEADS * HEAD_SIZE

    def tie(value, *others):
        return lax.optimization_barrier((value, *others))[0]

    def by_planes(chunk):
        low = sum(CHUNKS[:chunk]) * HEAD_SIZE
        high = low + CHUNKS[chunk] * HEAD_SIZE
        mine = jnp.concatenate(
            [prefix_key_value[:, low:high], prefix_key_value[:, middle + low:middle + high]], axis=1
        )
        return jnp.concatenate([mine] + [send(mine, k, 0, 0) for k in range(1, planes)], axis=0)

    def add(own, received):
        return own.astype(f32) + received.astype(f32)

    def reduce_ranks(totals, away):
        total = add(totals[0], send(totals[1], 0, 0, 1))
        return add(total, send(away, 0, 1, 0)) if ranks == 2 else total

    def reduce_planes(total, *begun):
        mine = total[0]
        for k in range(1, planes):
            away = tie(total[k].astype(jnp.bfloat16), *begun)
            mine = add(mine, send(away, k, 0, 0))
        return mine.astype(jnp.bfloat16)

    chunks = len(CHUNKS)
    near = [by_planes(chunk) for chunk in range(chunks)]
    near_far = [send(n, 0, 0, 1) for n in near]
    other = [send(n, 0, 1, 0) for n in near] if ranks == 2 else []
    d_leaf, d_prefix, earlier = [], [], ()
    parts = []
    for chunk in range(chunks):
        first = [place] + near[chunk + 1:chunk + 2] + near_far[chunk + 1:chunk + 2]
        if chunk and ranks == 2:
            first.append(parts[-1][1])
        sources = [near[chunk], near_far[chunk]]
        if ranks == 2:
            row = tie(other[chunk], d_leaf[-1] if chunk else near[1])
            sources += [row, send(row, 0, 0, 1)]
        attended, d_query, leaf_part, *totals = attention(
            chunk, block_owner, subtree_tokens, tie(*first), query, d_out, leaf_key_value,
            leaf_id, mask, sources, earlier, planes, ranks,
        )
        earlier = (attended, d_query)
        d_leaf.append(leaf_part)
        away = add(totals[2], send(totals[3], 0, 0, 1)).astype(jnp.bfloat16) if ranks == 2 else None
        parts.append((totals, away))
    begun = [parts[-1][1]] if ranks == 2 else []
    d_prefix = [reduce_planes(reduce_ranks(*part), *begun) for part in parts[:-1]]
    d_prefix.append(reduce_planes(reduce_ranks(*parts[-1])))
    d_leaf = [tie(part, d_leaf[-1]) for part in d_leaf[:-1]] + d_leaf[-1:]

    def join(parts):
        halves = [jnp.split(p, 2, axis=1) for p in parts]
        return jnp.concatenate([h[0] for h in halves] + [h[1] for h in halves], axis=1)

    return attended, d_query, join(d_leaf), join(d_prefix)


def solution(mesh):
    rows = P(("groups", "dp"), None)
    in_specs = (rows, rows, rows, rows, P("groups"), P("groups"), rows, P(("groups", "dp")))
    return jax.shard_map(
        shards, mesh=mesh, in_specs=in_specs, out_specs=(rows,) * 4, check_vma=False
    )
```

```python
import functools

import jax
import jax.numpy as jnp
from jax import lax
from jax.experimental import pallas as pl
from jax.experimental.pallas import tpu as pltpu
from jax.sharding import PartitionSpec as P

HEAD_SIZE = 128
KEY_VALUE_HEADS = 4
GQ = 8
SCALE = HEAD_SIZE ** (-0.5)
LOG2E = 1.4426950408889634


def dot(a, b, contract):
    return lax.dot_general(a, b, (contract, ((), ())), preferred_element_type=jnp.float32)

CHUNKS = (1, 3)
STEP_HEADS = (2, 4)
PIECES = (32, 32)
TURNED = (False, False)


def attention_kernel(
    owner_ref, tokens_ref, place_ref,
    q_ref, g_ref, leaf_k_ref, leaf_v_ref, leaf_ref, mask_ref, *rest,
    prompts, per_prefix, block_len, planes, ranks, chained, steps, step_heads,
    piece_rows, turned,
):
    sources = rest[:2 * ranks]
    rest = rest[2 * ranks + 2 * chained:]
    out_ref, dq_ref, dleaf_ref = rest[:3]
    totals = rest[3:3 + 2 * ranks]
    (kv, kcat, vcat, kcat_t, vcat_t, bias, q_pick, g_pick, q_pick_t, g_pick_t, q2, g2, scores, dprob, probs_b, dscore,
     dk_sum, dv_sum, sems) = rest[3 + 2 * ranks:]
    step = pl.program_id(0)
    per_group = GQ // step_heads
    count = q_ref.shape[0]
    columns = step_heads * count
    span = per_prefix * block_len
    keys = span + count
    half = sources[0].shape[1] // 2

    place = place_ref[0]
    first = place * count
    last = first + (count - 1)
    end = jnp.int32(0)
    pair_first = jnp.int32(0)
    pair_last = jnp.int32(0)
    border = jnp.int32(2**30)
    for p in range(prompts):
        end = end + tokens_ref[p]
        pair_first = pair_first + (end <= first).astype(jnp.int32)
        pair_last = pair_last + (end <= last).astype(jnp.int32)
        border = jnp.where(end > first, jnp.minimum(border, end), border)
    border = border - first

    def block_place(side, j):
        prefix = pair_first if side == 0 else pair_last
        owner = owner_ref[prefix * per_prefix + j]
        same_core = lax.rem(owner, 2) == lax.rem(place, 2)
        row = lax.rem(owner // 2 + place // 2, ranks)
        ahead = lax.rem(owner // (2 * ranks) + planes - place // (2 * ranks), planes)
        return same_core, row, ahead

    def key_columns(group):
        return pl.ds(pl.multiple_of(group * HEAD_SIZE, HEAD_SIZE), HEAD_SIZE)

    def value_columns(group):
        return pl.ds(pl.multiple_of(half + group * HEAD_SIZE, HEAD_SIZE), HEAD_SIZE)

    @pl.when(step == 0)
    def _():
        for side in range(2):
            for j in range(per_prefix):
                n = side * per_prefix + j
                same_core, row, ahead = block_place(side, j)
                slot = lax.rem(planes - ahead, planes)
                rows = pl.ds(pl.multiple_of(slot * block_len, block_len), block_len)
                target = kv.at[pl.ds(n * block_len, block_len), :]
                for at, source in enumerate(sources):
                    @pl.when((same_core == (at % 2 == 0)) & (row == at // 2))
                    def _():
                        pltpu.make_async_copy(source.at[rows, :], target, sems.at[n]).start()

        leaf_row = jnp.broadcast_to(leaf_ref[...], (count, count))
        leaf_col = leaf_row.T
        key_at = lax.broadcasted_iota(jnp.int32, (count, count), 0)
        token_at = lax.broadcasted_iota(jnp.int32, (count, count), 1)
        same = (leaf_row == leaf_col) & (key_at <= token_at)
        same = same & ((key_at < border) == (token_at < border))
        allowed_bias = jnp.where(same, 0.0, -1e30).astype(jnp.float32)
        mask_col = jnp.broadcast_to(mask_ref[...], (count, count)).T.astype(jnp.float32)
        in_first = key_at < border
        left = token_at < HEAD_SIZE
        pick = (in_first == left).astype(jnp.float32)
        q_pick[...] = pick.astype(jnp.bfloat16)
        g_pick[...] = (pick * mask_col).astype(jnp.bfloat16)
        q_pick_t[...] = q_pick[...].T
        g_pick_t[...] = g_pick[...].T
        for n in range(step_heads):
            bias[:, n * count:(n + 1) * count] = allowed_bias
        for ref in totals:
            ref[...] = jnp.zeros_like(ref)
        dk_sum[...] = jnp.zeros_like(dk_sum)
        dv_sum[...] = jnp.zeros_like(dv_sum)
        for n in range(2 * per_prefix):
            target = kv.at[pl.ds(n * block_len, block_len), :]
            pltpu.make_async_copy(
                sources[0].at[pl.ds(0, block_len), :], target, sems.at[n]
            ).wait()

    new_group = lax.rem(step, per_group) == 0

    @pl.when(new_group & (step < steps))
    def _():
        group = step // per_group
        for cat, cols, leaf in (
            (kcat, key_columns(group), leaf_k_ref), (vcat, value_columns(group), leaf_v_ref)
        ):
            for side in range(2):
                lanes = slice(side * HEAD_SIZE, (side + 1) * HEAD_SIZE)
                cat[0:span, lanes] = kv[side * span:(side + 1) * span, cols]
                cat[span:, lanes] = leaf[...]


    def later_rows():
        dk_sum[...] += dot(dscore[...], q2[...], ((1,), (0,)))
        dv_sum[...] += dot(probs_b[...], g2[...], ((1,), (0,)))

    def later_columns():
        token_at = lax.rem(lax.broadcasted_iota(jnp.int32, (HEAD_SIZE, columns), 1), count)
        first_side = token_at < border
        for source, cat_t, factor, target in (
            (probs_b, vcat_t, 1.0, out_ref), (dscore, kcat_t, SCALE, dq_ref)
        ):
            both = dot(cat_t[...], source[...], ((1,), (0,)))
            mine = jnp.where(first_side, both[:HEAD_SIZE], both[HEAD_SIZE:])
            if factor != 1.0:
                mine = mine * factor
            for n in range(step_heads):
                lanes = slice(n * HEAD_SIZE, (n + 1) * HEAD_SIZE)
                target[:, lanes] = mine[:, n * count:(n + 1) * count].T.astype(jnp.bfloat16)


    def pick(source, chosen):
        parts = []
        for n in range(step_heads):
            part = source[:, n * HEAD_SIZE:(n + 1) * HEAD_SIZE]
            parts.append(jnp.concatenate([part, part], axis=1) * chosen[...])
        return jnp.concatenate(parts, axis=0)

    def times(cat, new, source, chosen_t):
        if not turned:
            return dot(cat[...], new, ((1,), (1,)))
        parts = []
        for n in range(step_heads):
            part = source[:, n * HEAD_SIZE:(n + 1) * HEAD_SIZE].T
            parts.append(jnp.concatenate([part, part], axis=0) * chosen_t[...])
        return dot(cat[...], jnp.concatenate(parts, axis=1), ((1,), (0,)))

    def fold(value, op):
        value = value.reshape(piece_rows // 8, 8, columns)
        total = value[0]
        for n in range(1, piece_rows // 8):
            total = op(total, value[n])
        return total

    def score(new_q):
        product = times(kcat, new_q, q_ref, q_pick_t)
        top = None
        for at in range(0, keys, piece_rows):
            piece = product[at:at + piece_rows]
            if at >= span:
                piece = piece + bias[at - span:at - span + piece_rows, :]
            scores[at:at + piece_rows, :] = piece
            piece = fold(piece, jnp.maximum)
            top = piece if top is None else jnp.maximum(top, piece)
        return jnp.max(top, axis=0, keepdims=True)

    def sums(top):
        total = jnp.zeros((8, columns), jnp.float32)
        delta = jnp.zeros((8, columns), jnp.float32)
        for at in range(0, keys, piece_rows):
            weight = jnp.exp2((scores[at:at + piece_rows, :] - top) * (SCALE * LOG2E))
            total = total + fold(weight, jnp.add)
            delta = delta + fold(weight * dprob[at:at + piece_rows, :], jnp.add)
        total = jnp.sum(total, axis=0, keepdims=True)
        return total, jnp.sum(delta, axis=0, keepdims=True) / total

    def finish(top, total, delta):
        shift = jnp.log2(total)
        for at in range(0, keys, piece_rows):
            power = (scores[at:at + piece_rows, :] - top) * (SCALE * LOG2E)
            probs = jnp.exp2(power - shift)
            probs_b[at:at + piece_rows, :] = probs.astype(jnp.bfloat16)
            dscore[at:at + piece_rows, :] = (probs * (dprob[at:at + piece_rows, :] - delta)).astype(jnp.bfloat16)

    def work(later):
        new_q = pick(q_ref, q_pick)
        new_g = pick(g_ref, g_pick)
        top = score(new_q)
        if later:
            later_rows()
        dprob[...] = times(vcat, new_g, g_ref, g_pick_t)
        total, delta = sums(top)
        if later:
            later_columns()
        finish(top, total, delta)
        q2[...] = new_q
        g2[...] = new_g

    @pl.when(step == 0)
    def _():
        work(False)

    @pl.when((step > 0) & (step < steps))
    def _():
        work(True)

    @pl.when(step == steps)
    def _():
        later_rows()
        later_columns()

    @pl.when(new_group & (step > 0))
    def _():
        group = step // per_group - 1
        for total_ref, cols, factor in (
            (dk_sum, key_columns(group), SCALE), (dv_sum, value_columns(group), 1.0)
        ):
            leaf = (total_ref[span:, :HEAD_SIZE] + total_ref[span:, HEAD_SIZE:]) * factor
            dleaf_ref[:, cols] = leaf.astype(jnp.bfloat16)
            for side in range(2):
                lanes = slice(side * HEAD_SIZE, (side + 1) * HEAD_SIZE)
                for j in range(per_prefix):
                    value = total_ref[j * block_len:(j + 1) * block_len, lanes] * factor
                    value = value.astype(jnp.bfloat16)
                    same_core, row, ahead = block_place(side, j)
                    for at, ref in enumerate(totals):
                        @pl.when((same_core == (at % 2 == 0)) & (row == at // 2))
                        def _():
                            ref[ahead, :, cols] += value

        dk_sum[...] = jnp.zeros_like(dk_sum)
        dv_sum[...] = jnp.zeros_like(dv_sum)

    @pl.when(new_group & (step < steps))
    def _():
        kcat_t[...] = kcat[...].T
        vcat_t[...] = vcat[...].T


def attention(
    chunk, owner, tokens, place, q, g, leaf_kv, leaf, mask, sources, earlier, planes, ranks
):
    count = q.shape[0]
    block_len = sources[0].shape[0] // planes
    prompts = tokens.shape[0]
    per_prefix = owner.shape[0] // prompts
    span = per_prefix * block_len
    keys = span + count
    width = sources[0].shape[1]
    groups = CHUNKS[chunk]
    step_heads = STEP_HEADS[chunk]
    skipped = sum(CHUNKS[:chunk])
    heads = groups * GQ
    steps = heads // step_heads
    per_group = GQ // step_heads
    skipped_steps = skipped * per_group
    bf16, f32 = jnp.bfloat16, jnp.float32

    def now(i):
        return jnp.minimum(i, steps - 1)

    ahead = pl.BlockSpec((count, step_heads * HEAD_SIZE), lambda i, *_: (0, skipped_steps + now(i)))
    behind = pl.BlockSpec(
        (count, step_heads * HEAD_SIZE), lambda i, *_: (0, skipped_steps + jnp.maximum(i - 1, 0))
    )
    leaf_k = pl.BlockSpec(
        (count, HEAD_SIZE), lambda i, *_: (0, skipped + now(i) // per_group)
    )
    leaf_v = pl.BlockSpec(
        (count, HEAD_SIZE),
        lambda i, *_: (0, KEY_VALUE_HEADS + skipped + now(i) // per_group),
    )
    anywhere = pl.BlockSpec(memory_space=pl.ANY)

    def full(shape):
        return pl.BlockSpec(shape, lambda h, *_: (0,) * len(shape))

    sum_shape = (planes, block_len, width)
    chained = len(earlier) > 0
    return pl.pallas_call(
        functools.partial(
            attention_kernel, prompts=prompts, per_prefix=per_prefix, block_len=block_len,
            planes=planes, ranks=ranks, chained=chained, steps=steps, step_heads=step_heads,
            piece_rows=PIECES[chunk], turned=TURNED[chunk],
        ),
        grid_spec=pltpu.PrefetchScalarGridSpec(
            num_scalar_prefetch=3,
            grid=(steps + 1,),
            in_specs=[
                ahead, ahead, leaf_k, leaf_v, full(leaf.shape), full(mask.shape),
            ] + [anywhere] * (2 * ranks + len(earlier)),
            out_specs=[behind, behind, full((count, width))] + [full(sum_shape)] * (2 * ranks),
            scratch_shapes=[
                pltpu.VMEM((2 * span, width), bf16),
                pltpu.VMEM((keys, 2 * HEAD_SIZE), bf16),
                pltpu.VMEM((keys, 2 * HEAD_SIZE), bf16),
                pltpu.VMEM((2 * HEAD_SIZE, keys), bf16),
                pltpu.VMEM((2 * HEAD_SIZE, keys), bf16),
                pltpu.VMEM((count, step_heads * count), f32),
                pltpu.VMEM((count, 2 * HEAD_SIZE), bf16),
                pltpu.VMEM((count, 2 * HEAD_SIZE), bf16),
                pltpu.VMEM((2 * HEAD_SIZE, count), bf16),
                pltpu.VMEM((2 * HEAD_SIZE, count), bf16),
                pltpu.VMEM((step_heads * count, 2 * HEAD_SIZE), bf16),
                pltpu.VMEM((step_heads * count, 2 * HEAD_SIZE), bf16),
                pltpu.VMEM((keys, step_heads * count), f32),
                pltpu.VMEM((keys, step_heads * count), f32),
                pltpu.VMEM((keys, step_heads * count), bf16),
                pltpu.VMEM((keys, step_heads * count), bf16),
                pltpu.VMEM((keys, 2 * HEAD_SIZE), f32),
                pltpu.VMEM((keys, 2 * HEAD_SIZE), f32),
                pltpu.SemaphoreType.DMA((2 * per_prefix,)),
            ],
        ),
        out_shape=[
            jax.ShapeDtypeStruct(q.shape, bf16),
            jax.ShapeDtypeStruct(q.shape, bf16),
            jax.ShapeDtypeStruct((count, width), bf16),
        ] + [jax.ShapeDtypeStruct(sum_shape, bf16)] * (2 * ranks),
        input_output_aliases={9 + 2 * ranks: 0, 10 + 2 * ranks: 1} if chained else {},
        compiler_params=pltpu.CompilerParams(
            vmem_limit_bytes=54 * 2**20, dimension_semantics=("arbitrary",)
        ),
        cost_estimate=pl.CostEstimate(
            flops=heads * 6 * 2 * keys * 256 * 256, bytes_accessed=groups * 4 * 2**20,
            transcendentals=heads * keys * count,
        ),
    )(owner, tokens, place, q, g, leaf_kv, leaf_kv, leaf, mask, *sources, *earlier)


def shards(
    query, leaf_key_value, prefix_key_value, d_out, block_owner, subtree_tokens, leaf_id, loss_mask
):
    devices = lax.axis_size("dp")
    ranks = 2 if devices == 16 else 1
    planes = devices // (2 * ranks)
    place = lax.axis_index("dp").astype(jnp.int32).reshape(1)
    mask = loss_mask.reshape(1, -1)
    f32 = jnp.float32

    def index(plane, rank, core):
        return (plane % planes * ranks + rank % ranks) * 2 + core % 2

    def send(array, plane_step, rank_step, core_step):
        pairs = [
            (index(p, r, c), index(p + plane_step, r + rank_step, c + core_step))
            for p in range(planes) for r in range(ranks) for c in range(2)
        ]
        return lax.ppermute(array, "dp", pairs)

    middle = KEY_VALUE_HEADS * HEAD_SIZE

    def tie(value, *others):
        return lax.optimization_barrier((value, *others))[0]

    def by_planes(chunk):
        low = sum(CHUNKS[:chunk]) * HEAD_SIZE
        high = low + CHUNKS[chunk] * HEAD_SIZE
        mine = jnp.concatenate(
            [prefix_key_value[:, low:high], prefix_key_value[:, middle + low:middle + high]], axis=1
        )
        return [mine] + [send(mine, k, 0, 0) for k in range(1, planes)]

    def add(own, received):
        return own.astype(f32) + received.astype(f32)

    def reduce_cores(totals):
        away = add(totals[2], send(totals[3], 0, 0, 1)).astype(jnp.bfloat16) if ranks == 2 else None
        return away, add(totals[0], send(totals[1], 0, 0, 1))

    def reduce_ranks(away, keep, in_pieces, *last):
        if ranks == 1:
            sums = [keep[k] for k in range(planes)]
        elif in_pieces:
            sums, before = [None] * planes, []
            for k in sorted(range(planes), key=lambda k: -min(k, planes - k)):
                mine = tie(away[k], *before) if k == 0 else away[k]
                sums[k] = add(keep[k], tie(send(mine, 0, 1, 0), *before))
                before = [sums[k]]
        else:
            total = add(keep, tie(send(away, 0, 1, 0), *last))
            sums = [total[k] for k in range(planes)]
        return sums[:1] + [part.astype(jnp.bfloat16) for part in sums[1:]]

    def reduce_planes(sums, *last):
        mine = sums[0]
        for k in range(1, planes):
            mine = add(mine, tie(send(sums[k], k, 0, 0), *last))
        return mine.astype(jnp.bfloat16)

    chunks = len(CHUNKS)
    pieces = [by_planes(chunk) for chunk in range(chunks)]
    d_leaf, parts, earlier = [], [], ()
    for chunk in range(chunks):
        first = [place]
        own, rest = pieces[chunk][0], pieces[chunk][1:]
        if chunk:
            if ranks == 2:
                first.append(parts[-1][0])
            rest = [tie(piece, d_leaf[-1]) for piece in rest]
        rest = jnp.concatenate(rest, axis=0)
        near = jnp.concatenate([own, rest], axis=0)
        sources = [near, send(near, 0, 0, 1)]
        if ranks == 2:
            if chunk:
                row = jnp.concatenate([send(own, 0, 1, 0), send(rest, 0, 1, 0)], axis=0)
            else:
                row = tie(send(near, 0, 1, 0), pieces[1][1])
            sources += [row, send(row, 0, 0, 1)]
        attended, d_query, leaf_part, *totals = attention(
            chunk, block_owner, subtree_tokens, tie(*first), query, d_out, leaf_key_value,
            leaf_id, mask, sources, earlier, planes, ranks,
        )
        earlier = (attended, d_query)
        d_leaf.append(leaf_part)
        parts.append(reduce_cores(totals))
    last = reduce_ranks(*parts[-1], True)
    d_prefix = [
        reduce_planes(reduce_ranks(*part, False, d_leaf[-1]), last[planes // 2])
        for part in parts[:-1]
    ]
    d_prefix.append(reduce_planes(last))
    d_leaf = [tie(part, d_leaf[-1]) for part in d_leaf[:-1]] + d_leaf[-1:]

    def join(parts):
        halves = [jnp.split(p, 2, axis=1) for p in parts]
        return jnp.concatenate([h[0] for h in halves] + [h[1] for h in halves], axis=1)

    return attended, d_query, join(d_leaf), join(d_prefix)


def solution(mesh):
    rows = P(("groups", "dp"), None)
    in_specs = (rows, rows, rows, rows, P("groups"), P("groups"), rows, P(("groups", "dp")))
    return jax.shard_map(
        shards, mesh=mesh, in_specs=in_specs, out_specs=(rows,) * 4, check_vma=False
    )
```

```python
import functools

import jax
import jax.numpy as jnp
from jax import lax
from jax.experimental import pallas as pl
from jax.experimental.pallas import tpu as pltpu
from jax.sharding import PartitionSpec as P

HEAD_SIZE = 128
KEY_VALUE_HEADS = 4
GQ = 8
SCALE = HEAD_SIZE ** (-0.5)
LOG2E = 1.4426950408889634


def dot(a, b, contract):
    return lax.dot_general(a, b, (contract, ((), ())), preferred_element_type=jnp.float32)

CHUNKS = (2, 2)
STEP_HEADS = (4, 4)
PIECES = (32, 32)
BY_TOKENS = ((True, True), (True, False))


def attention_kernel(
    owner_ref, tokens_ref, place_ref,
    q_ref, g_ref, leaf_k_ref, leaf_v_ref, leaf_ref, mask_ref, *rest,
    prompts, per_prefix, block_len, planes, ranks, chained, steps, step_heads,
    piece_rows, by_tokens,
):
    sources = rest[:2 * ranks]
    rest = rest[2 * ranks + 2 * chained:]
    out_ref, dq_ref, dleaf_ref = rest[:3]
    totals = rest[3:3 + 2 * ranks]
    (kv, kcat, vcat, klast, vlast, bias, q_pick, g_pick, q2, g2, scores, dprob, probs_b, dscore,
     dk_sum, dv_sum, sems) = rest[3 + 2 * ranks:]
    step = pl.program_id(0)
    per_group = GQ // step_heads
    count = q_ref.shape[0]
    columns = step_heads * count
    span = per_prefix * block_len
    keys = span + count
    half = sources[0].shape[1] // 2

    place = place_ref[0]
    first = place * count
    last = first + (count - 1)
    end = jnp.int32(0)
    pair_first = jnp.int32(0)
    pair_last = jnp.int32(0)
    border = jnp.int32(2**30)
    for p in range(prompts):
        end = end + tokens_ref[p]
        pair_first = pair_first + (end <= first).astype(jnp.int32)
        pair_last = pair_last + (end <= last).astype(jnp.int32)
        border = jnp.where(end > first, jnp.minimum(border, end), border)
    border = border - first

    def block_place(side, j):
        prefix = pair_first if side == 0 else pair_last
        owner = owner_ref[prefix * per_prefix + j]
        same_core = lax.rem(owner, 2) == lax.rem(place, 2)
        row = lax.rem(owner // 2 + place // 2, ranks)
        ahead = lax.rem(owner // (2 * ranks) + planes - place // (2 * ranks), planes)
        return same_core, row, ahead

    def key_columns(group):
        return pl.ds(pl.multiple_of(group * HEAD_SIZE, HEAD_SIZE), HEAD_SIZE)

    def value_columns(group):
        return pl.ds(pl.multiple_of(half + group * HEAD_SIZE, HEAD_SIZE), HEAD_SIZE)

    @pl.when(step == 0)
    def _():
        for side in range(2):
            for j in range(per_prefix):
                n = side * per_prefix + j
                same_core, row, ahead = block_place(side, j)
                slot = lax.rem(planes - ahead, planes)
                rows = pl.ds(pl.multiple_of(slot * block_len, block_len), block_len)
                target = kv.at[pl.ds(n * block_len, block_len), :]
                for at, source in enumerate(sources):
                    @pl.when((same_core == (at % 2 == 0)) & (row == at // 2))
                    def _():
                        pltpu.make_async_copy(source.at[rows, :], target, sems.at[n]).start()

        leaf_row = jnp.broadcast_to(leaf_ref[...], (count, count))
        leaf_col = leaf_row.T
        key_at = lax.broadcasted_iota(jnp.int32, (count, count), 0)
        token_at = lax.broadcasted_iota(jnp.int32, (count, count), 1)
        same = (leaf_row == leaf_col) & (key_at <= token_at)
        same = same & ((key_at < border) == (token_at < border))
        allowed_bias = jnp.where(same, 0.0, -1e30).astype(jnp.float32)
        mask_col = jnp.broadcast_to(mask_ref[...], (count, count)).T.astype(jnp.float32)
        in_first = key_at < border
        left = token_at < HEAD_SIZE
        pick = (in_first == left).astype(jnp.float32)
        q_pick[...] = pick.astype(jnp.bfloat16)
        g_pick[...] = (pick * mask_col).astype(jnp.bfloat16)
        for n in range(step_heads):
            bias[:, n * count:(n + 1) * count] = allowed_bias
        for ref in totals:
            ref[...] = jnp.zeros_like(ref)
        dk_sum[...] = jnp.zeros_like(dk_sum)
        dv_sum[...] = jnp.zeros_like(dv_sum)
        for n in range(2 * per_prefix):
            target = kv.at[pl.ds(n * block_len, block_len), :]
            pltpu.make_async_copy(
                sources[0].at[pl.ds(0, block_len), :], target, sems.at[n]
            ).wait()

    new_group = lax.rem(step, per_group) == 0

    @pl.when(new_group & (step < steps))
    def _():
        group = step // per_group
        for cat, cols, leaf in (
            (kcat, key_columns(group), leaf_k_ref), (vcat, value_columns(group), leaf_v_ref)
        ):
            for side in range(2):
                lanes = slice(side * HEAD_SIZE, (side + 1) * HEAD_SIZE)
                cat[0:span, lanes] = kv[side * span:(side + 1) * span, cols]
                cat[span:, lanes] = leaf[...]


    def later_rows():
        dk_sum[...] += dot(dscore[...], q2[...], ((1,), (0,)))
        dv_sum[...] += dot(probs_b[...], g2[...], ((1,), (0,)))

    def later_columns():
        for source, cat, factor, target, rows in (
            (probs_b, vlast, 1.0, out_ref, by_tokens[0]),
            (dscore, klast, SCALE, dq_ref, by_tokens[1]),
        ):
            if rows:
                both = dot(source[...], cat[...], ((0,), (0,)))
                token_at = lax.rem(lax.broadcasted_iota(jnp.int32, (columns, HEAD_SIZE), 0), count)
                mine = jnp.where(token_at < border, both[:, :HEAD_SIZE], both[:, HEAD_SIZE:])
            else:
                both = dot(cat[...], source[...], ((1,), (0,)))
                token_at = lax.rem(lax.broadcasted_iota(jnp.int32, (HEAD_SIZE, columns), 1), count)
                mine = jnp.where(token_at < border, both[:HEAD_SIZE], both[HEAD_SIZE:])
            if factor != 1.0:
                mine = mine * factor
            for n in range(step_heads):
                lanes = slice(n * HEAD_SIZE, (n + 1) * HEAD_SIZE)
                span_n = slice(n * count, (n + 1) * count)
                part = mine[span_n] if rows else mine[:, span_n].T
                target[:, lanes] = part.astype(jnp.bfloat16)


    def pick(source, chosen):
        parts = []
        for n in range(step_heads):
            part = source[:, n * HEAD_SIZE:(n + 1) * HEAD_SIZE]
            parts.append(jnp.concatenate([part, part], axis=1) * chosen[...])
        return jnp.concatenate(parts, axis=0)

    def fold(value, op):
        value = value.reshape(piece_rows // 8, 8, columns)
        total = value[0]
        for n in range(1, piece_rows // 8):
            total = op(total, value[n])
        return total

    def score(new_q):
        product = dot(kcat[...], new_q, ((1,), (1,)))
        top = None
        for at in range(0, keys, piece_rows):
            piece = product[at:at + piece_rows]
            if at >= span:
                piece = piece + bias[at - span:at - span + piece_rows, :]
            scores[at:at + piece_rows, :] = piece
            piece = fold(piece, jnp.maximum)
            top = piece if top is None else jnp.maximum(top, piece)
        return jnp.max(top, axis=0, keepdims=True)

    def sums(top):
        total = jnp.zeros((8, columns), jnp.float32)
        delta = jnp.zeros((8, columns), jnp.float32)
        for at in range(0, keys, piece_rows):
            weight = jnp.exp2((scores[at:at + piece_rows, :] - top) * (SCALE * LOG2E))
            total = total + fold(weight, jnp.add)
            delta = delta + fold(weight * dprob[at:at + piece_rows, :], jnp.add)
        total = jnp.sum(total, axis=0, keepdims=True)
        return total, jnp.sum(delta, axis=0, keepdims=True) / total

    def finish(top, total, delta):
        shift = jnp.log2(total)
        for at in range(0, keys, piece_rows):
            power = (scores[at:at + piece_rows, :] - top) * (SCALE * LOG2E)
            probs = jnp.exp2(power - shift)
            probs_b[at:at + piece_rows, :] = probs.astype(jnp.bfloat16)
            dscore[at:at + piece_rows, :] = (probs * (dprob[at:at + piece_rows, :] - delta)).astype(jnp.bfloat16)

    def work(later):
        new_q = pick(q_ref, q_pick)
        new_g = pick(g_ref, g_pick)
        top = score(new_q)
        if later:
            later_rows()
        dprob[...] = dot(vcat[...], new_g, ((1,), (1,)))
        total, delta = sums(top)
        if later:
            later_columns()
        finish(top, total, delta)
        q2[...] = new_q
        g2[...] = new_g

    @pl.when(step == 0)
    def _():
        work(False)

    @pl.when((step > 0) & (step < steps))
    def _():
        work(True)

    @pl.when(step == steps)
    def _():
        later_rows()
        later_columns()

    @pl.when(new_group & (step > 0))
    def _():
        group = step // per_group - 1
        for total_ref, cols, factor in (
            (dk_sum, key_columns(group), SCALE), (dv_sum, value_columns(group), 1.0)
        ):
            leaf = (total_ref[span:, :HEAD_SIZE] + total_ref[span:, HEAD_SIZE:]) * factor
            dleaf_ref[:, cols] = leaf.astype(jnp.bfloat16)
            for side in range(2):
                lanes = slice(side * HEAD_SIZE, (side + 1) * HEAD_SIZE)
                for j in range(per_prefix):
                    value = total_ref[j * block_len:(j + 1) * block_len, lanes] * factor
                    value = value.astype(jnp.bfloat16)
                    same_core, row, ahead = block_place(side, j)
                    for at, ref in enumerate(totals):
                        @pl.when((same_core == (at % 2 == 0)) & (row == at // 2))
                        def _():
                            ref[ahead, :, cols] += value

        dk_sum[...] = jnp.zeros_like(dk_sum)
        dv_sum[...] = jnp.zeros_like(dv_sum)

    @pl.when(new_group & (step < steps))
    def _():
        vlast[...] = vcat[...] if by_tokens[0] else vcat[...].T
        klast[...] = kcat[...] if by_tokens[1] else kcat[...].T


def attention(
    chunk, owner, tokens, place, q, g, leaf_kv, leaf, mask, sources, earlier, planes, ranks
):
    count = q.shape[0]
    block_len = sources[0].shape[0] // planes
    prompts = tokens.shape[0]
    per_prefix = owner.shape[0] // prompts
    span = per_prefix * block_len
    keys = span + count
    width = sources[0].shape[1]
    groups = CHUNKS[chunk]
    step_heads = STEP_HEADS[chunk]
    skipped = sum(CHUNKS[:chunk])
    heads = groups * GQ
    steps = heads // step_heads
    per_group = GQ // step_heads
    skipped_steps = skipped * per_group
    bf16, f32 = jnp.bfloat16, jnp.float32

    def now(i):
        return jnp.minimum(i, steps - 1)

    ahead = pl.BlockSpec((count, step_heads * HEAD_SIZE), lambda i, *_: (0, skipped_steps + now(i)))
    behind = pl.BlockSpec(
        (count, step_heads * HEAD_SIZE), lambda i, *_: (0, skipped_steps + jnp.maximum(i - 1, 0))
    )
    leaf_k = pl.BlockSpec(
        (count, HEAD_SIZE), lambda i, *_: (0, skipped + now(i) // per_group)
    )
    leaf_v = pl.BlockSpec(
        (count, HEAD_SIZE),
        lambda i, *_: (0, KEY_VALUE_HEADS + skipped + now(i) // per_group),
    )
    anywhere = pl.BlockSpec(memory_space=pl.ANY)

    def full(shape):
        return pl.BlockSpec(shape, lambda h, *_: (0,) * len(shape))

    sum_shape = (planes, block_len, width)
    last_shape = {
        True: pltpu.VMEM((keys, 2 * HEAD_SIZE), bf16), False: pltpu.VMEM((2 * HEAD_SIZE, keys), bf16)
    }
    chained = len(earlier) > 0
    return pl.pallas_call(
        functools.partial(
            attention_kernel, prompts=prompts, per_prefix=per_prefix, block_len=block_len,
            planes=planes, ranks=ranks, chained=chained, steps=steps, step_heads=step_heads,
            piece_rows=PIECES[chunk], by_tokens=BY_TOKENS[chunk],
        ),
        grid_spec=pltpu.PrefetchScalarGridSpec(
            num_scalar_prefetch=3,
            grid=(steps + 1,),
            in_specs=[
                ahead, ahead, leaf_k, leaf_v, full(leaf.shape), full(mask.shape),
            ] + [anywhere] * (2 * ranks + len(earlier)),
            out_specs=[behind, behind, full((count, width))] + [full(sum_shape)] * (2 * ranks),
            scratch_shapes=[
                pltpu.VMEM((2 * span, width), bf16),
                pltpu.VMEM((keys, 2 * HEAD_SIZE), bf16),
                pltpu.VMEM((keys, 2 * HEAD_SIZE), bf16),
                last_shape[BY_TOKENS[chunk][1]],
                last_shape[BY_TOKENS[chunk][0]],
                pltpu.VMEM((count, step_heads * count), f32),
                pltpu.VMEM((count, 2 * HEAD_SIZE), bf16),
                pltpu.VMEM((count, 2 * HEAD_SIZE), bf16),
                pltpu.VMEM((step_heads * count, 2 * HEAD_SIZE), bf16),
                pltpu.VMEM((step_heads * count, 2 * HEAD_SIZE), bf16),
                pltpu.VMEM((keys, step_heads * count), f32),
                pltpu.VMEM((keys, step_heads * count), f32),
                pltpu.VMEM((keys, step_heads * count), bf16),
                pltpu.VMEM((keys, step_heads * count), bf16),
                pltpu.VMEM((keys, 2 * HEAD_SIZE), f32),
                pltpu.VMEM((keys, 2 * HEAD_SIZE), f32),
                pltpu.SemaphoreType.DMA((2 * per_prefix,)),
            ],
        ),
        out_shape=[
            jax.ShapeDtypeStruct(q.shape, bf16),
            jax.ShapeDtypeStruct(q.shape, bf16),
            jax.ShapeDtypeStruct((count, width), bf16),
        ] + [jax.ShapeDtypeStruct(sum_shape, bf16)] * (2 * ranks),
        input_output_aliases={9 + 2 * ranks: 0, 10 + 2 * ranks: 1} if chained else {},
        compiler_params=pltpu.CompilerParams(
            vmem_limit_bytes=54 * 2**20, dimension_semantics=("arbitrary",)
        ),
        cost_estimate=pl.CostEstimate(
            flops=heads * 6 * 2 * keys * 256 * 256, bytes_accessed=groups * 4 * 2**20,
            transcendentals=heads * keys * count,
        ),
    )(owner, tokens, place, q, g, leaf_kv, leaf_kv, leaf, mask, *sources, *earlier)


def shards(
    query, leaf_key_value, prefix_key_value, d_out, block_owner, subtree_tokens, leaf_id, loss_mask
):
    devices = lax.axis_size("dp")
    ranks = 2 if devices == 16 else 1
    planes = devices // (2 * ranks)
    place = lax.axis_index("dp").astype(jnp.int32).reshape(1)
    mask = loss_mask.reshape(1, -1)
    f32 = jnp.float32

    def index(plane, rank, core):
        return (plane % planes * ranks + rank % ranks) * 2 + core % 2

    def send(array, plane_step, rank_step, core_step):
        pairs = [
            (index(p, r, c), index(p + plane_step, r + rank_step, c + core_step))
            for p in range(planes) for r in range(ranks) for c in range(2)
        ]
        return lax.ppermute(array, "dp", pairs)

    middle = KEY_VALUE_HEADS * HEAD_SIZE

    def tie(value, *others):
        return lax.optimization_barrier((value, *others))[0]

    def by_planes(chunk):
        low = sum(CHUNKS[:chunk]) * HEAD_SIZE
        high = low + CHUNKS[chunk] * HEAD_SIZE
        mine = jnp.concatenate(
            [prefix_key_value[:, low:high], prefix_key_value[:, middle + low:middle + high]], axis=1
        )
        return jnp.concatenate([mine] + [send(mine, k, 0, 0) for k in range(1, planes)], axis=0)

    def add(own, received):
        return own.astype(f32) + received.astype(f32)

    def reduce_ranks(totals, away):
        total = add(totals[0], send(totals[1], 0, 0, 1))
        return add(total, send(away, 0, 1, 0)) if ranks == 2 else total

    def reduce_planes(total, *begun):
        mine = total[0]
        for k in range(1, planes):
            away = tie(total[k].astype(jnp.bfloat16), *begun)
            mine = add(mine, send(away, k, 0, 0))
        return mine.astype(jnp.bfloat16)

    chunks = len(CHUNKS)
    near = [by_planes(chunk) for chunk in range(chunks)]
    near_far = [send(n, 0, 0, 1) for n in near]
    other = [send(n, 0, 1, 0) for n in near] if ranks == 2 else []
    d_leaf, d_prefix, earlier = [], [], ()
    parts = []
    for chunk in range(chunks):
        first = [place] + near[chunk + 1:chunk + 2] + near_far[chunk + 1:chunk + 2]
        if chunk and ranks == 2:
            first.append(parts[-1][1])
        sources = [near[chunk], near_far[chunk]]
        if ranks == 2:
            row = tie(other[chunk], d_leaf[-1] if chunk else near[1])
            sources += [row, send(row, 0, 0, 1)]
        attended, d_query, leaf_part, *totals = attention(
            chunk, block_owner, subtree_tokens, tie(*first), query, d_out, leaf_key_value,
            leaf_id, mask, sources, earlier, planes, ranks,
        )
        earlier = (attended, d_query)
        d_leaf.append(leaf_part)
        away = add(totals[2], send(totals[3], 0, 0, 1)).astype(jnp.bfloat16) if ranks == 2 else None
        parts.append((totals, away))
    begun = [parts[-1][1]] if ranks == 2 else []
    d_prefix = [reduce_planes(reduce_ranks(*part), *begun) for part in parts[:-1]]
    d_prefix.append(reduce_planes(reduce_ranks(*parts[-1])))
    d_leaf = [tie(part, d_leaf[-1]) for part in d_leaf[:-1]] + d_leaf[-1:]

    def join(parts):
        halves = [jnp.split(p, 2, axis=1) for p in parts]
        return jnp.concatenate([h[0] for h in halves] + [h[1] for h in halves], axis=1)

    return attended, d_query, join(d_leaf), join(d_prefix)


def solution(mesh):
    rows = P(("groups", "dp"), None)
    in_specs = (rows, rows, rows, rows, P("groups"), P("groups"), rows, P(("groups", "dp")))
    return jax.shard_map(
        shards, mesh=mesh, in_specs=in_specs, out_specs=(rows,) * 4, check_vma=False
    )
```

```python
import functools

import jax
import jax.numpy as jnp
from jax import lax
from jax.experimental import pallas as pl
from jax.experimental.pallas import tpu as pltpu
from jax.sharding import PartitionSpec as P

HEAD_SIZE = 128
KEY_VALUE_HEADS = 4
GQ = 8
SCALE = HEAD_SIZE ** (-0.5)
LOG2E = 1.4426950408889634


def dot(a, b, contract):
    return lax.dot_general(a, b, (contract, ((), ())), preferred_element_type=jnp.float32)

CHUNKS = (2, 2)
STEP_HEADS = (4, 4)
PIECE = 32


def attention_kernel(
    owner_ref, tokens_ref, place_ref,
    q_ref, g_ref, leaf_k_ref, leaf_v_ref, leaf_ref, mask_ref, *rest,
    prompts, per_prefix, block_len, planes, ranks, chained, steps, step_heads,
):
    sources = rest[:2 * ranks]
    rest = rest[2 * ranks + 2 * chained:]
    out_ref, dq_ref, dleaf_ref = rest[:3]
    totals = rest[3:3 + 2 * ranks]
    (kv, held, kcat, vcat, kcat_t, vcat_t, bias, q_pick, g_pick, q2, g2, scores, dprob, probs_b, dscore,
     dk_sum, dv_sum, sems) = rest[3 + 2 * ranks:]
    step = pl.program_id(0)
    per_group = GQ // step_heads
    count = q_ref.shape[0]
    columns = step_heads * count
    span = per_prefix * block_len
    keys = span + count
    half = sources[0].shape[1] // 2

    place = place_ref[0]
    first = place * count
    last = first + (count - 1)
    end = jnp.int32(0)
    pair_first = jnp.int32(0)
    pair_last = jnp.int32(0)
    border = jnp.int32(2**30)
    for p in range(prompts):
        end = end + tokens_ref[p]
        pair_first = pair_first + (end <= first).astype(jnp.int32)
        pair_last = pair_last + (end <= last).astype(jnp.int32)
        border = jnp.where(end > first, jnp.minimum(border, end), border)
    border = border - first

    def block_place(side, j):
        prefix = pair_first if side == 0 else pair_last
        owner = owner_ref[prefix * per_prefix + j]
        core = lax.rem(owner + place, 2)
        row = lax.rem(lax.div(owner, 2) + lax.div(place, 2), ranks)
        ahead = lax.rem(lax.div(owner, 2 * ranks) + planes - lax.div(place, 2 * ranks), planes)
        return core + 2 * row, ahead

    def key_columns(group):
        return pl.ds(pl.multiple_of(group * HEAD_SIZE, HEAD_SIZE), HEAD_SIZE)

    def value_columns(group):
        return pl.ds(pl.multiple_of(half + group * HEAD_SIZE, HEAD_SIZE), HEAD_SIZE)

    @pl.when(step == 0)
    def _():
        copies = [
            pltpu.make_async_copy(source, kv.at[at], sems.at[at])
            for at, source in enumerate(sources)
        ]
        for copy in copies:
            copy.start()
        leaf_row = jnp.broadcast_to(leaf_ref[...], (count, count))
        leaf_col = leaf_row.T
        key_at = lax.broadcasted_iota(jnp.int32, (count, count), 0)
        token_at = lax.broadcasted_iota(jnp.int32, (count, count), 1)
        same = (leaf_row == leaf_col) & (key_at <= token_at)
        same = same & ((key_at < border) == (token_at < border))
        allowed_bias = jnp.where(same, 0.0, -1e30).astype(jnp.float32)
        mask_col = jnp.broadcast_to(mask_ref[...], (count, count)).T.astype(jnp.float32)
        in_first = key_at < border
        left = token_at < HEAD_SIZE
        pick = (in_first == left).astype(jnp.float32)
        q_pick[...] = pick.astype(jnp.bfloat16)
        g_pick[...] = (pick * mask_col).astype(jnp.bfloat16)
        for n in range(step_heads):
            bias[:, n * count:(n + 1) * count] = allowed_bias
        for ref in (held, dk_sum, dv_sum):
            ref[...] = jnp.zeros_like(ref)
        for copy in copies:
            copy.wait()

    new_group = lax.rem(step, per_group) == 0

    @pl.when(new_group & (step < steps))
    def _():
        group = step // per_group
        for cat, cols, leaf in (
            (kcat, key_columns(group), leaf_k_ref), (vcat, value_columns(group), leaf_v_ref)
        ):
            for side in range(2):
                lanes = slice(side * HEAD_SIZE, (side + 1) * HEAD_SIZE)
                for j in range(per_prefix):
                    holder, ahead = block_place(side, j)
                    at = lax.rem(planes - ahead, planes) * block_len
                    rows = pl.ds(pl.multiple_of(at, block_len), block_len)
                    cat[j * block_len:(j + 1) * block_len, lanes] = kv[holder, rows, cols]
                cat[span:, lanes] = leaf[...]


    def later_rows():
        dk_sum[...] += dot(dscore[...], q2[...], ((1,), (0,)))
        dv_sum[...] += dot(probs_b[...], g2[...], ((1,), (0,)))

    def later_columns():
        token_at = lax.rem(lax.broadcasted_iota(jnp.int32, (HEAD_SIZE, columns), 1), count)
        first_side = token_at < border
        for source, cat_t, factor, target in (
            (probs_b, vcat_t, 1.0, out_ref), (dscore, kcat_t, SCALE, dq_ref)
        ):
            both = dot(cat_t[...], source[...], ((1,), (0,)))
            mine = jnp.where(first_side, both[:HEAD_SIZE], both[HEAD_SIZE:])
            if factor != 1.0:
                mine = mine * factor
            for n in range(step_heads):
                lanes = slice(n * HEAD_SIZE, (n + 1) * HEAD_SIZE)
                target[:, lanes] = mine[:, n * count:(n + 1) * count].T.astype(jnp.bfloat16)


    def pick(source, chosen):
        parts = []
        for n in range(step_heads):
            part = source[:, n * HEAD_SIZE:(n + 1) * HEAD_SIZE]
            parts.append(jnp.concatenate([part, part], axis=1) * chosen[...])
        return jnp.concatenate(parts, axis=0)

    def fold(value, op):
        value = value.reshape(PIECE // 8, 8, columns)
        total = value[0]
        for n in range(1, PIECE // 8):
            total = op(total, value[n])
        return total

    def score(new_q):
        product = dot(kcat[...], new_q, ((1,), (1,)))
        top = None
        for at in range(0, keys, PIECE):
            piece = product[at:at + PIECE]
            if at >= span:
                piece = piece + bias[at - span:at - span + PIECE, :]
            scores[at:at + PIECE, :] = piece
            piece = fold(piece, jnp.maximum)
            top = piece if top is None else jnp.maximum(top, piece)
        return jnp.max(top, axis=0, keepdims=True)

    def sums(top):
        total = jnp.zeros((8, columns), jnp.float32)
        delta = jnp.zeros((8, columns), jnp.float32)
        for at in range(0, keys, PIECE):
            weight = jnp.exp2((scores[at:at + PIECE, :] - top) * (SCALE * LOG2E))
            total = total + fold(weight, jnp.add)
            delta = delta + fold(weight * dprob[at:at + PIECE, :], jnp.add)
        total = jnp.sum(total, axis=0, keepdims=True)
        return total, jnp.sum(delta, axis=0, keepdims=True) / total

    def finish(top, total, delta):
        shift = jnp.log2(total)
        for at in range(0, keys, PIECE):
            power = (scores[at:at + PIECE, :] - top) * (SCALE * LOG2E)
            probs = jnp.exp2(power - shift)
            probs_b[at:at + PIECE, :] = probs.astype(jnp.bfloat16)
            dscore[at:at + PIECE, :] = (probs * (dprob[at:at + PIECE, :] - delta)).astype(jnp.bfloat16)

    def work(later):
        new_q = pick(q_ref, q_pick)
        new_g = pick(g_ref, g_pick)
        top = score(new_q)
        if later:
            later_rows()
        dprob[...] = dot(vcat[...], new_g, ((1,), (1,)))
        total, delta = sums(top)
        if later:
            later_columns()
        finish(top, total, delta)
        q2[...] = new_q
        g2[...] = new_g

    @pl.when(step == 0)
    def _():
        work(False)

    @pl.when((step > 0) & (step < steps))
    def _():
        work(True)

    @pl.when(step == steps)
    def _():
        later_rows()
        later_columns()

    @pl.when(new_group & (step > 0))
    def _():
        group = step // per_group - 1
        for total_ref, cols, factor in (
            (dk_sum, key_columns(group), SCALE), (dv_sum, value_columns(group), 1.0)
        ):
            leaf = (total_ref[span:, :HEAD_SIZE] + total_ref[span:, HEAD_SIZE:]) * factor
            dleaf_ref[:, cols] = leaf.astype(jnp.bfloat16)
            for side in range(2):
                lanes = slice(side * HEAD_SIZE, (side + 1) * HEAD_SIZE)
                for j in range(per_prefix):
                    value = total_ref[j * block_len:(j + 1) * block_len, lanes] * factor
                    value = value.astype(jnp.bfloat16)
                    holder, ahead = block_place(side, j)
                    held[holder, ahead, :, cols] += value

        dk_sum[...] = jnp.zeros_like(dk_sum)
        dv_sum[...] = jnp.zeros_like(dv_sum)

    @pl.when(new_group & (step < steps))
    def _():
        kcat_t[...] = kcat[...].T
        vcat_t[...] = vcat[...].T

    @pl.when(step == steps)
    def _():
        copies = [
            pltpu.make_async_copy(held.at[at], total, sems.at[at])
            for at, total in enumerate(totals)
        ]
        for copy in copies:
            copy.start()
        for copy in copies:
            copy.wait()


def attention(
    chunk, owner, tokens, place, q, g, leaf_kv, leaf, mask, sources, earlier, planes, ranks
):
    count = q.shape[0]
    block_len = sources[0].shape[0] // planes
    prompts = tokens.shape[0]
    per_prefix = owner.shape[0] // prompts
    span = per_prefix * block_len
    keys = span + count
    width = sources[0].shape[1]
    groups = CHUNKS[chunk]
    step_heads = STEP_HEADS[chunk]
    skipped = sum(CHUNKS[:chunk])
    heads = groups * GQ
    steps = heads // step_heads
    per_group = GQ // step_heads
    skipped_steps = skipped * per_group
    bf16, f32 = jnp.bfloat16, jnp.float32

    def now(i):
        return jnp.minimum(i, steps - 1)

    ahead = pl.BlockSpec((count, step_heads * HEAD_SIZE), lambda i, *_: (0, skipped_steps + now(i)))
    behind = pl.BlockSpec(
        (count, step_heads * HEAD_SIZE), lambda i, *_: (0, skipped_steps + jnp.maximum(i - 1, 0))
    )
    leaf_k = pl.BlockSpec(
        (count, HEAD_SIZE), lambda i, *_: (0, skipped + now(i) // per_group)
    )
    leaf_v = pl.BlockSpec(
        (count, HEAD_SIZE),
        lambda i, *_: (0, KEY_VALUE_HEADS + skipped + now(i) // per_group),
    )
    anywhere = pl.BlockSpec(memory_space=pl.ANY)

    def full(shape):
        return pl.BlockSpec(shape, lambda h, *_: (0,) * len(shape))

    sum_shape = (planes, block_len, width)
    chained = len(earlier) > 0
    return pl.pallas_call(
        functools.partial(
            attention_kernel, prompts=prompts, per_prefix=per_prefix, block_len=block_len,
            planes=planes, ranks=ranks, chained=chained, steps=steps, step_heads=step_heads,
        ),
        grid_spec=pltpu.PrefetchScalarGridSpec(
            num_scalar_prefetch=3,
            grid=(steps + 1,),
            in_specs=[
                ahead, ahead, leaf_k, leaf_v, full(leaf.shape), full(mask.shape),
            ] + [anywhere] * (2 * ranks + len(earlier)),
            out_specs=[behind, behind, full((count, width))] + [anywhere] * (2 * ranks),
            scratch_shapes=[
                pltpu.VMEM((2 * ranks, planes * block_len, width), bf16),
                pltpu.VMEM((2 * ranks, *sum_shape), bf16),
                pltpu.VMEM((keys, 2 * HEAD_SIZE), bf16),
                pltpu.VMEM((keys, 2 * HEAD_SIZE), bf16),
                pltpu.VMEM((2 * HEAD_SIZE, keys), bf16),
                pltpu.VMEM((2 * HEAD_SIZE, keys), bf16),
                pltpu.VMEM((count, step_heads * count), f32),
                pltpu.VMEM((count, 2 * HEAD_SIZE), bf16),
                pltpu.VMEM((count, 2 * HEAD_SIZE), bf16),
                pltpu.VMEM((step_heads * count, 2 * HEAD_SIZE), bf16),
                pltpu.VMEM((step_heads * count, 2 * HEAD_SIZE), bf16),
                pltpu.VMEM((keys, step_heads * count), f32),
                pltpu.VMEM((keys, step_heads * count), f32),
                pltpu.VMEM((keys, step_heads * count), bf16),
                pltpu.VMEM((keys, step_heads * count), bf16),
                pltpu.VMEM((keys, 2 * HEAD_SIZE), f32),
                pltpu.VMEM((keys, 2 * HEAD_SIZE), f32),
                pltpu.SemaphoreType.DMA((2 * ranks,)),
            ],
        ),
        out_shape=[
            jax.ShapeDtypeStruct(q.shape, bf16),
            jax.ShapeDtypeStruct(q.shape, bf16),
            jax.ShapeDtypeStruct((count, width), bf16),
        ] + [jax.ShapeDtypeStruct(sum_shape, bf16)] * (2 * ranks),
        input_output_aliases={9 + 2 * ranks: 0, 10 + 2 * ranks: 1} if chained else {},
        compiler_params=pltpu.CompilerParams(
            vmem_limit_bytes=54 * 2**20, dimension_semantics=("arbitrary",)
        ),
        cost_estimate=pl.CostEstimate(
            flops=heads * 6 * 2 * keys * 256 * 256, bytes_accessed=groups * 4 * 2**20,
            transcendentals=heads * keys * count,
        ),
    )(owner, tokens, place, q, g, leaf_kv, leaf_kv, leaf, mask, *sources, *earlier)


def shards(
    query, leaf_key_value, prefix_key_value, d_out, block_owner, subtree_tokens, leaf_id, loss_mask
):
    devices = lax.axis_size("dp")
    ranks = 2 if devices == 16 else 1
    planes = devices // (2 * ranks)
    place = lax.axis_index("dp").astype(jnp.int32).reshape(1)
    mask = loss_mask.reshape(1, -1)
    f32 = jnp.float32

    def index(plane, rank, core):
        return (plane % planes * ranks + rank % ranks) * 2 + core % 2

    def send(array, plane_step, rank_step, core_step):
        pairs = [
            (index(p, r, c), index(p + plane_step, r + rank_step, c + core_step))
            for p in range(planes) for r in range(ranks) for c in range(2)
        ]
        return lax.ppermute(array, "dp", pairs)

    middle = KEY_VALUE_HEADS * HEAD_SIZE

    def tie(value, *others):
        return lax.optimization_barrier((value, *others))[0]

    def by_planes(chunk):
        low = sum(CHUNKS[:chunk]) * HEAD_SIZE
        high = low + CHUNKS[chunk] * HEAD_SIZE
        mine = jnp.concatenate(
            [prefix_key_value[:, low:high], prefix_key_value[:, middle + low:middle + high]], axis=1
        )
        return jnp.concatenate([mine] + [send(mine, k, 0, 0) for k in range(1, planes)], axis=0)

    def add(own, received):
        return own.astype(f32) + received.astype(f32)

    def reduce_ranks(totals, away):
        total = add(totals[0], send(totals[1], 0, 0, 1))
        return add(total, send(away, 0, 1, 0)) if ranks == 2 else total

    def reduce_planes(total, *begun):
        mine = total[0]
        for k in range(1, planes):
            away = tie(total[k].astype(jnp.bfloat16), *begun)
            mine = add(mine, send(away, k, 0, 0))
        return mine.astype(jnp.bfloat16)

    chunks = len(CHUNKS)
    near = [by_planes(chunk) for chunk in range(chunks)]
    near_far = [send(n, 0, 0, 1) for n in near]
    other = [send(n, 0, 1, 0) for n in near] if ranks == 2 else []
    d_leaf, d_prefix, earlier = [], [], ()
    parts = []
    for chunk in range(chunks):
        first = [place] + near[chunk + 1:chunk + 2] + near_far[chunk + 1:chunk + 2]
        if chunk and ranks == 2:
            first.append(parts[-1][1])
        sources = [near[chunk], near_far[chunk]]
        if ranks == 2:
            row = tie(other[chunk], d_leaf[-1] if chunk else near[1])
            sources += [row, send(row, 0, 0, 1)]
        attended, d_query, leaf_part, *totals = attention(
            chunk, block_owner, subtree_tokens, tie(*first), query, d_out, leaf_key_value,
            leaf_id, mask, sources, earlier, planes, ranks,
        )
        earlier = (attended, d_query)
        d_leaf.append(leaf_part)
        away = add(totals[2], send(totals[3], 0, 0, 1)).astype(jnp.bfloat16) if ranks == 2 else None
        parts.append((totals, away))
    begun = [parts[-1][1]] if ranks == 2 else []
    d_prefix = [reduce_planes(reduce_ranks(*part), *begun) for part in parts[:-1]]
    d_prefix.append(reduce_planes(reduce_ranks(*parts[-1])))
    d_leaf = [tie(part, d_leaf[-1]) for part in d_leaf[:-1]] + d_leaf[-1:]

    def join(parts):
        halves = [jnp.split(p, 2, axis=1) for p in parts]
        return jnp.concatenate([h[0] for h in halves] + [h[1] for h in halves], axis=1)

    return attended, d_query, join(d_leaf), join(d_prefix)


def solution(mesh):
    rows = P(("groups", "dp"), None)
    in_specs = (rows, rows, rows, rows, P("groups"), P("groups"), rows, P(("groups", "dp")))
    return jax.shard_map(
        shards, mesh=mesh, in_specs=in_specs, out_specs=(rows,) * 4, check_vma=False
    )
```

```python
import functools

import jax
import jax.numpy as jnp
from jax import lax
from jax.experimental import pallas as pl
from jax.experimental.pallas import tpu as pltpu
from jax.sharding import PartitionSpec as P

HEAD_SIZE = 128
KEY_VALUE_HEADS = 4
GQ = 8
SCALE = HEAD_SIZE ** (-0.5)
LOG2E = 1.4426950408889634


def dot(a, b, contract):
    return lax.dot_general(a, b, (contract, ((), ())), preferred_element_type=jnp.float32)

CHUNKS = (2, 2)
STEP_HEADS = (4, 4)
PIECE = 32


def attention_kernel(
    owner_ref, tokens_ref, place_ref,
    q_ref, g_ref, leaf_k_ref, leaf_v_ref, leaf_ref, mask_ref, *rest,
    prompts, per_prefix, block_len, planes, ranks, chained, steps, step_heads,
    first_column,
):
    blocks = 2 * ranks * planes
    sources = rest[:blocks]
    rest = rest[blocks + 2 * chained:]
    out_ref, dq_ref, dleaf_ref = rest[:3]
    totals = rest[3:3 + 2 * ranks]
    (kv, held, kcat, vcat, kcat_t, vcat_t, bias, q_pick, g_pick, q2, g2, scores, dprob, probs_b, dscore,
     dk_sum, dv_sum, sems) = rest[3 + 2 * ranks:]
    step = pl.program_id(0)
    per_group = GQ // step_heads
    count = q_ref.shape[0]
    columns = step_heads * count
    span = per_prefix * block_len
    keys = span + count
    half = kv.shape[2] // 2

    place = place_ref[0]
    first = place * count
    last = first + (count - 1)
    end = jnp.int32(0)
    pair_first = jnp.int32(0)
    pair_last = jnp.int32(0)
    border = jnp.int32(2**30)
    for p in range(prompts):
        end = end + tokens_ref[p]
        pair_first = pair_first + (end <= first).astype(jnp.int32)
        pair_last = pair_last + (end <= last).astype(jnp.int32)
        border = jnp.where(end > first, jnp.minimum(border, end), border)
    border = border - first

    def block_place(side, j):
        prefix = pair_first if side == 0 else pair_last
        owner = owner_ref[prefix * per_prefix + j]
        core = lax.rem(owner + place, 2)
        row = lax.rem(lax.div(owner, 2) + lax.div(place, 2), ranks)
        ahead = lax.rem(lax.div(owner, 2 * ranks) + planes - lax.div(place, 2 * ranks), planes)
        return core + 2 * row, ahead

    def key_columns(group):
        return pl.ds(pl.multiple_of(group * HEAD_SIZE, HEAD_SIZE), HEAD_SIZE)

    def value_columns(group):
        return pl.ds(pl.multiple_of(half + group * HEAD_SIZE, HEAD_SIZE), HEAD_SIZE)

    @pl.when(step == 0)
    def _():
        copies = []
        for at, source in enumerate(sources):
            rows = pl.ds(at % planes * block_len, block_len)
            for side in range(2):
                columns_in = pl.ds(first_column + side * (source.shape[1] // 2), half)
                columns_to = pl.ds(side * half, half)
                copies.append(pltpu.make_async_copy(
                    source.at[:, columns_in], kv.at[at // planes, rows, columns_to], sems.at[at, side]
                ))
        for copy in copies:
            copy.start()
        leaf_row = jnp.broadcast_to(leaf_ref[...], (count, count))
        leaf_col = leaf_row.T
        key_at = lax.broadcasted_iota(jnp.int32, (count, count), 0)
        token_at = lax.broadcasted_iota(jnp.int32, (count, count), 1)
        same = (leaf_row == leaf_col) & (key_at <= token_at)
        same = same & ((key_at < border) == (token_at < border))
        allowed_bias = jnp.where(same, 0.0, -1e30).astype(jnp.float32)
        mask_col = jnp.broadcast_to(mask_ref[...], (count, count)).T.astype(jnp.float32)
        in_first = key_at < border
        left = token_at < HEAD_SIZE
        pick = (in_first == left).astype(jnp.float32)
        q_pick[...] = pick.astype(jnp.bfloat16)
        g_pick[...] = (pick * mask_col).astype(jnp.bfloat16)
        for n in range(step_heads):
            bias[:, n * count:(n + 1) * count] = allowed_bias
        for ref in (held, dk_sum, dv_sum):
            ref[...] = jnp.zeros_like(ref)
        for copy in copies:
            copy.wait()

    new_group = lax.rem(step, per_group) == 0

    @pl.when(new_group & (step < steps))
    def _():
        group = step // per_group
        for cat, cols, leaf in (
            (kcat, key_columns(group), leaf_k_ref), (vcat, value_columns(group), leaf_v_ref)
        ):
            for side in range(2):
                lanes = slice(side * HEAD_SIZE, (side + 1) * HEAD_SIZE)
                for j in range(per_prefix):
                    holder, ahead = block_place(side, j)
                    at = lax.rem(planes - ahead, planes) * block_len
                    rows = pl.ds(pl.multiple_of(at, block_len), block_len)
                    cat[j * block_len:(j + 1) * block_len, lanes] = kv[holder, rows, cols]
                cat[span:, lanes] = leaf[...]


    def later_rows():
        dk_sum[...] += dot(dscore[...], q2[...], ((1,), (0,)))
        dv_sum[...] += dot(probs_b[...], g2[...], ((1,), (0,)))

    def later_columns():
        token_at = lax.rem(lax.broadcasted_iota(jnp.int32, (HEAD_SIZE, columns), 1), count)
        first_side = token_at < border
        for source, cat_t, factor, target in (
            (probs_b, vcat_t, 1.0, out_ref), (dscore, kcat_t, SCALE, dq_ref)
        ):
            both = dot(cat_t[...], source[...], ((1,), (0,)))
            mine = jnp.where(first_side, both[:HEAD_SIZE], both[HEAD_SIZE:])
            if factor != 1.0:
                mine = mine * factor
            for n in range(step_heads):
                lanes = slice(n * HEAD_SIZE, (n + 1) * HEAD_SIZE)
                target[:, lanes] = mine[:, n * count:(n + 1) * count].T.astype(jnp.bfloat16)


    def pick(source, chosen):
        parts = []
        for n in range(step_heads):
            part = source[:, n * HEAD_SIZE:(n + 1) * HEAD_SIZE]
            parts.append(jnp.concatenate([part, part], axis=1) * chosen[...])
        return jnp.concatenate(parts, axis=0)

    def fold(value, op):
        value = value.reshape(PIECE // 8, 8, columns)
        total = value[0]
        for n in range(1, PIECE // 8):
            total = op(total, value[n])
        return total

    def score(new_q):
        product = dot(kcat[...], new_q, ((1,), (1,)))
        top = None
        for at in range(0, keys, PIECE):
            piece = product[at:at + PIECE]
            if at >= span:
                piece = piece + bias[at - span:at - span + PIECE, :]
            scores[at:at + PIECE, :] = piece
            piece = fold(piece, jnp.maximum)
            top = piece if top is None else jnp.maximum(top, piece)
        return jnp.max(top, axis=0, keepdims=True)

    def sums(top):
        total = jnp.zeros((8, columns), jnp.float32)
        delta = jnp.zeros((8, columns), jnp.float32)
        for at in range(0, keys, PIECE):
            weight = jnp.exp2((scores[at:at + PIECE, :] - top) * (SCALE * LOG2E))
            total = total + fold(weight, jnp.add)
            delta = delta + fold(weight * dprob[at:at + PIECE, :], jnp.add)
        total = jnp.sum(total, axis=0, keepdims=True)
        return total, jnp.sum(delta, axis=0, keepdims=True) / total

    def finish(top, total, delta):
        shift = jnp.log2(total)
        for at in range(0, keys, PIECE):
            power = (scores[at:at + PIECE, :] - top) * (SCALE * LOG2E)
            probs = jnp.exp2(power - shift)
            probs_b[at:at + PIECE, :] = probs.astype(jnp.bfloat16)
            dscore[at:at + PIECE, :] = (probs * (dprob[at:at + PIECE, :] - delta)).astype(jnp.bfloat16)

    def work(later):
        new_q = pick(q_ref, q_pick)
        new_g = pick(g_ref, g_pick)
        top = score(new_q)
        if later:
            later_rows()
        dprob[...] = dot(vcat[...], new_g, ((1,), (1,)))
        total, delta = sums(top)
        if later:
            later_columns()
        finish(top, total, delta)
        q2[...] = new_q
        g2[...] = new_g

    @pl.when(step == 0)
    def _():
        work(False)

    @pl.when((step > 0) & (step < steps))
    def _():
        work(True)

    @pl.when(step == steps)
    def _():
        later_rows()
        later_columns()

    @pl.when(new_group & (step > 0))
    def _():
        group = step // per_group - 1
        for total_ref, cols, factor in (
            (dk_sum, key_columns(group), SCALE), (dv_sum, value_columns(group), 1.0)
        ):
            leaf = (total_ref[span:, :HEAD_SIZE] + total_ref[span:, HEAD_SIZE:]) * factor
            dleaf_ref[:, cols] = leaf.astype(jnp.bfloat16)
            for side in range(2):
                lanes = slice(side * HEAD_SIZE, (side + 1) * HEAD_SIZE)
                for j in range(per_prefix):
                    value = total_ref[j * block_len:(j + 1) * block_len, lanes] * factor
                    value = value.astype(jnp.bfloat16)
                    holder, ahead = block_place(side, j)
                    held[holder, ahead, :, cols] += value

        dk_sum[...] = jnp.zeros_like(dk_sum)
        dv_sum[...] = jnp.zeros_like(dv_sum)

    @pl.when(new_group & (step < steps))
    def _():
        kcat_t[...] = kcat[...].T
        vcat_t[...] = vcat[...].T

    @pl.when(step == steps)
    def _():
        copies = [
            pltpu.make_async_copy(held.at[at], total, sems.at[at, 0])
            for at, total in enumerate(totals)
        ]
        for copy in copies:
            copy.start()
        for copy in copies:
            copy.wait()


def attention(
    chunk, owner, tokens, place, q, g, leaf_kv, leaf, mask, sources, earlier, planes, ranks
):
    count = q.shape[0]
    block_len = sources[0].shape[0]
    prompts = tokens.shape[0]
    per_prefix = owner.shape[0] // prompts
    span = per_prefix * block_len
    keys = span + count
    groups = CHUNKS[chunk]
    width = 2 * groups * HEAD_SIZE
    step_heads = STEP_HEADS[chunk]
    skipped = sum(CHUNKS[:chunk])
    heads = groups * GQ
    steps = heads // step_heads
    per_group = GQ // step_heads
    skipped_steps = skipped * per_group
    bf16, f32 = jnp.bfloat16, jnp.float32

    def now(i):
        return jnp.minimum(i, steps - 1)

    ahead = pl.BlockSpec((count, step_heads * HEAD_SIZE), lambda i, *_: (0, skipped_steps + now(i)))
    behind = pl.BlockSpec(
        (count, step_heads * HEAD_SIZE), lambda i, *_: (0, skipped_steps + jnp.maximum(i - 1, 0))
    )
    leaf_k = pl.BlockSpec(
        (count, HEAD_SIZE), lambda i, *_: (0, skipped + now(i) // per_group)
    )
    leaf_v = pl.BlockSpec(
        (count, HEAD_SIZE),
        lambda i, *_: (0, KEY_VALUE_HEADS + skipped + now(i) // per_group),
    )
    anywhere = pl.BlockSpec(memory_space=pl.ANY)

    def full(shape):
        return pl.BlockSpec(shape, lambda h, *_: (0,) * len(shape))

    sum_shape = (planes, block_len, width)
    chained = len(earlier) > 0
    return pl.pallas_call(
        functools.partial(
            attention_kernel, prompts=prompts, per_prefix=per_prefix, block_len=block_len,
            planes=planes, ranks=ranks, chained=chained, steps=steps, step_heads=step_heads,
            first_column=skipped * HEAD_SIZE,
        ),
        grid_spec=pltpu.PrefetchScalarGridSpec(
            num_scalar_prefetch=3,
            grid=(steps + 1,),
            in_specs=[
                ahead, ahead, leaf_k, leaf_v, full(leaf.shape), full(mask.shape),
            ] + [anywhere] * (len(sources) + len(earlier)),
            out_specs=[behind, behind, full((count, width))] + [anywhere] * (2 * ranks),
            scratch_shapes=[
                pltpu.VMEM((2 * ranks, planes * block_len, width), bf16),
                pltpu.VMEM((2 * ranks, *sum_shape), bf16),
                pltpu.VMEM((keys, 2 * HEAD_SIZE), bf16),
                pltpu.VMEM((keys, 2 * HEAD_SIZE), bf16),
                pltpu.VMEM((2 * HEAD_SIZE, keys), bf16),
                pltpu.VMEM((2 * HEAD_SIZE, keys), bf16),
                pltpu.VMEM((count, step_heads * count), f32),
                pltpu.VMEM((count, 2 * HEAD_SIZE), bf16),
                pltpu.VMEM((count, 2 * HEAD_SIZE), bf16),
                pltpu.VMEM((step_heads * count, 2 * HEAD_SIZE), bf16),
                pltpu.VMEM((step_heads * count, 2 * HEAD_SIZE), bf16),
                pltpu.VMEM((keys, step_heads * count), f32),
                pltpu.VMEM((keys, step_heads * count), f32),
                pltpu.VMEM((keys, step_heads * count), bf16),
                pltpu.VMEM((keys, step_heads * count), bf16),
                pltpu.VMEM((keys, 2 * HEAD_SIZE), f32),
                pltpu.VMEM((keys, 2 * HEAD_SIZE), f32),
                pltpu.SemaphoreType.DMA((2 * ranks * planes, 2)),
            ],
        ),
        out_shape=[
            jax.ShapeDtypeStruct(q.shape, bf16),
            jax.ShapeDtypeStruct(q.shape, bf16),
            jax.ShapeDtypeStruct((count, width), bf16),
        ] + [jax.ShapeDtypeStruct(sum_shape, bf16)] * (2 * ranks),
        input_output_aliases={9 + len(sources): 0, 10 + len(sources): 1} if chained else {},
        compiler_params=pltpu.CompilerParams(
            vmem_limit_bytes=54 * 2**20, dimension_semantics=("arbitrary",)
        ),
        cost_estimate=pl.CostEstimate(
            flops=heads * 6 * 2 * keys * 256 * 256, bytes_accessed=groups * 4 * 2**20,
            transcendentals=heads * keys * count,
        ),
    )(owner, tokens, place, q, g, leaf_kv, leaf_kv, leaf, mask, *sources, *earlier)


def shards(
    query, leaf_key_value, prefix_key_value, d_out, block_owner, subtree_tokens, leaf_id, loss_mask
):
    devices = lax.axis_size("dp")
    ranks = 2 if devices == 16 else 1
    planes = devices // (2 * ranks)
    place = lax.axis_index("dp").astype(jnp.int32).reshape(1)
    mask = loss_mask.reshape(1, -1)
    f32 = jnp.float32

    def index(plane, rank, core):
        return (plane % planes * ranks + rank % ranks) * 2 + core % 2

    def send(array, plane_step, rank_step, core_step):
        pairs = [
            (index(p, r, c), index(p + plane_step, r + rank_step, c + core_step))
            for p in range(planes) for r in range(ranks) for c in range(2)
        ]
        return lax.ppermute(array, "dp", pairs)

    def tie(value, *others):
        return lax.optimization_barrier((value, *others))[0]

    def add(own, received):
        return own.astype(f32) + received.astype(f32)

    def reduce_ranks(totals, away):
        total = add(totals[0], send(totals[1], 0, 0, 1))
        return add(total, send(away, 0, 1, 0)) if ranks == 2 else total

    def reduce_planes(total, *begun):
        mine = total[0]
        for k in range(1, planes):
            away = tie(total[k].astype(jnp.bfloat16), *begun)
            mine = add(mine, send(away, k, 0, 0))
        return mine.astype(jnp.bfloat16)

    chunks = len(CHUNKS)
    near, rows = [], []
    for plane in range(planes):
        near.append(send(tie(near[-1], *rows[-2:-1]), 1, 0, 0) if plane else prefix_key_value)
        if ranks == 2:
            rows.append(send(near[-1], 0, 1, 0))
    sources = []
    for held in (near, rows):
        sources += held + [send(piece, 0, 0, 1) for piece in held]
    d_leaf, parts, earlier = [], [], ()
    for chunk in range(chunks):
        first = [place]
        if chunk and ranks == 2:
            first.append(parts[-1][1])
        attended, d_query, leaf_part, *totals = attention(
            chunk, block_owner, subtree_tokens, tie(*first), query, d_out, leaf_key_value,
            leaf_id, mask, sources, earlier, planes, ranks,
        )
        earlier = (attended, d_query)
        d_leaf.append(leaf_part)
        away = add(totals[2], send(totals[3], 0, 0, 1)).astype(jnp.bfloat16) if ranks == 2 else None
        parts.append((totals, away))
    begun = [parts[-1][1]] if ranks == 2 else []
    d_prefix = [reduce_planes(reduce_ranks(*part), *begun) for part in parts[:-1]]
    d_prefix.append(reduce_planes(reduce_ranks(*parts[-1])))
    d_leaf = [tie(part, d_leaf[-1]) for part in d_leaf[:-1]] + d_leaf[-1:]

    def join(parts):
        halves = [jnp.split(p, 2, axis=1) for p in parts]
        return jnp.concatenate([h[0] for h in halves] + [h[1] for h in halves], axis=1)

    return attended, d_query, join(d_leaf), join(d_prefix)


def solution(mesh):
    rows = P(("groups", "dp"), None)
    in_specs = (rows, rows, rows, rows, P("groups"), P("groups"), rows, P(("groups", "dp")))
    return jax.shard_map(
        shards, mesh=mesh, in_specs=in_specs, out_specs=(rows,) * 4, check_vma=False
    )
```

```python
import functools

import jax
import jax.numpy as jnp
from jax import lax
from jax.experimental import pallas as pl
from jax.experimental.pallas import tpu as pltpu
from jax.sharding import PartitionSpec as P

HEAD_SIZE = 128
KEY_VALUE_HEADS = 4
GQ = 8
SCALE = HEAD_SIZE ** (-0.5)
LOG2E = 1.4426950408889634


def dot(a, b, contract):
    return lax.dot_general(a, b, (contract, ((), ())), preferred_element_type=jnp.float32)

CHUNKS = (2, 2)
STEP_HEADS = (4, 4)
PIECE = 32


def attention_kernel(
    owner_ref, tokens_ref, place_ref,
    q_ref, g_ref, leaf_k_ref, leaf_v_ref, leaf_ref, mask_ref, *rest,
    prompts, per_prefix, block_len, planes, ranks, chained, steps, step_heads,
    first_column,
):
    blocks = 2 * ranks * planes
    sources = rest[:blocks]
    rest = rest[blocks + 2 * chained:]
    out_ref, dq_ref, dleaf_ref = rest[:3]
    totals = rest[3:3 + 2 * ranks]
    (kv, held, kcat, vcat, kcat_t, vcat_t, bias, q_pick, g_pick, q2, g2, scores, dprob, probs_b, dscore,
     dk_sum, dv_sum, sems) = rest[3 + 2 * ranks:]
    step = pl.program_id(0)
    per_group = GQ // step_heads
    count = q_ref.shape[0]
    columns = step_heads * count
    span = per_prefix * block_len
    keys = span + count
    half = kv.shape[2] // 2

    place = place_ref[0]
    first = place * count
    last = first + (count - 1)
    end = jnp.int32(0)
    pair_first = jnp.int32(0)
    pair_last = jnp.int32(0)
    border = jnp.int32(2**30)
    for p in range(prompts):
        end = end + tokens_ref[p]
        pair_first = pair_first + (end <= first).astype(jnp.int32)
        pair_last = pair_last + (end <= last).astype(jnp.int32)
        border = jnp.where(end > first, jnp.minimum(border, end), border)
    border = border - first

    def block_place(side, j):
        prefix = pair_first if side == 0 else pair_last
        owner = owner_ref[prefix * per_prefix + j]
        core = lax.rem(owner + place, 2)
        row = lax.rem(lax.div(owner, 2) + lax.div(place, 2), ranks)
        ahead = lax.rem(lax.div(owner, 2 * ranks) + planes - lax.div(place, 2 * ranks), planes)
        return core + 2 * row, ahead

    def key_columns(group):
        return pl.ds(pl.multiple_of(group * HEAD_SIZE, HEAD_SIZE), HEAD_SIZE)

    def value_columns(group):
        return pl.ds(pl.multiple_of(half + group * HEAD_SIZE, HEAD_SIZE), HEAD_SIZE)

    @pl.when(step == 0)
    def _():
        copies = []
        for at, source in enumerate(sources):
            rows = pl.ds(at % planes * block_len, block_len)
            for side in range(2):
                columns_in = pl.ds(first_column + side * (source.shape[1] // 2), half)
                columns_to = pl.ds(side * half, half)
                copies.append(pltpu.make_async_copy(
                    source.at[:, columns_in], kv.at[at // planes, rows, columns_to], sems.at[at, side]
                ))
        for copy in copies:
            copy.start()
        leaf_row = jnp.broadcast_to(leaf_ref[...], (count, count))
        leaf_col = leaf_row.T
        key_at = lax.broadcasted_iota(jnp.int32, (count, count), 0)
        token_at = lax.broadcasted_iota(jnp.int32, (count, count), 1)
        same = (leaf_row == leaf_col) & (key_at <= token_at)
        same = same & ((key_at < border) == (token_at < border))
        allowed_bias = jnp.where(same, 0.0, -1e30).astype(jnp.float32)
        mask_col = jnp.broadcast_to(mask_ref[...], (count, count)).T.astype(jnp.float32)
        in_first = key_at < border
        left = token_at < HEAD_SIZE
        pick = (in_first == left).astype(jnp.float32)
        q_pick[...] = pick.astype(jnp.bfloat16)
        g_pick[...] = (pick * mask_col).astype(jnp.bfloat16)
        for n in range(step_heads):
            bias[:, n * count:(n + 1) * count] = allowed_bias
        for ref in (held, dk_sum, dv_sum):
            ref[...] = jnp.zeros_like(ref)
        for copy in copies:
            copy.wait()

    new_group = lax.rem(step, per_group) == 0

    @pl.when(new_group & (step < steps))
    def _():
        group = step // per_group
        for cat, cols, leaf in (
            (kcat, key_columns(group), leaf_k_ref), (vcat, value_columns(group), leaf_v_ref)
        ):
            for side in range(2):
                lanes = slice(side * HEAD_SIZE, (side + 1) * HEAD_SIZE)
                for j in range(per_prefix):
                    holder, ahead = block_place(side, j)
                    at = lax.rem(planes - ahead, planes) * block_len
                    rows = pl.ds(pl.multiple_of(at, block_len), block_len)
                    cat[j * block_len:(j + 1) * block_len, lanes] = kv[holder, rows, cols]
                cat[span:, lanes] = leaf[...]


    def later_rows():
        dk_sum[...] += dot(dscore[...], q2[...], ((1,), (0,)))
        dv_sum[...] += dot(probs_b[...], g2[...], ((1,), (0,)))

    def later_columns():
        token_at = lax.rem(lax.broadcasted_iota(jnp.int32, (HEAD_SIZE, columns), 1), count)
        first_side = token_at < border
        for source, cat_t, factor, target in (
            (probs_b, vcat_t, 1.0, out_ref), (dscore, kcat_t, SCALE, dq_ref)
        ):
            both = dot(cat_t[...], source[...], ((1,), (0,)))
            mine = jnp.where(first_side, both[:HEAD_SIZE], both[HEAD_SIZE:])
            if factor != 1.0:
                mine = mine * factor
            for n in range(step_heads):
                lanes = slice(n * HEAD_SIZE, (n + 1) * HEAD_SIZE)
                target[:, lanes] = mine[:, n * count:(n + 1) * count].T.astype(jnp.bfloat16)


    def pick(source, chosen):
        parts = []
        for n in range(step_heads):
            part = source[:, n * HEAD_SIZE:(n + 1) * HEAD_SIZE]
            parts.append(jnp.concatenate([part, part], axis=1) * chosen[...])
        return jnp.concatenate(parts, axis=0)

    def fold(value, op):
        value = value.reshape(PIECE // 8, 8, columns)
        total = value[0]
        for n in range(1, PIECE // 8):
            total = op(total, value[n])
        return total

    def score(new_q):
        product = dot(kcat[...], new_q, ((1,), (1,)))
        top = None
        for at in range(0, keys, PIECE):
            piece = product[at:at + PIECE]
            if at >= span:
                piece = piece + bias[at - span:at - span + PIECE, :]
            scores[at:at + PIECE, :] = piece
            piece = fold(piece, jnp.maximum)
            top = piece if top is None else jnp.maximum(top, piece)
        return jnp.max(top, axis=0, keepdims=True)

    def sums(top):
        total = jnp.zeros((8, columns), jnp.float32)
        delta = jnp.zeros((8, columns), jnp.float32)
        for at in range(0, keys, PIECE):
            weight = jnp.exp2((scores[at:at + PIECE, :] - top) * (SCALE * LOG2E))
            total = total + fold(weight, jnp.add)
            delta = delta + fold(weight * dprob[at:at + PIECE, :], jnp.add)
        total = jnp.sum(total, axis=0, keepdims=True)
        return total, jnp.sum(delta, axis=0, keepdims=True) / total

    def finish(top, total, delta):
        shift = jnp.log2(total)
        for at in range(0, keys, PIECE):
            power = (scores[at:at + PIECE, :] - top) * (SCALE * LOG2E)
            probs = jnp.exp2(power - shift)
            probs_b[at:at + PIECE, :] = probs.astype(jnp.bfloat16)
            dscore[at:at + PIECE, :] = (probs * (dprob[at:at + PIECE, :] - delta)).astype(jnp.bfloat16)

    def work(later):
        new_q = pick(q_ref, q_pick)
        new_g = pick(g_ref, g_pick)
        top = score(new_q)
        if later:
            later_rows()
        dprob[...] = dot(vcat[...], new_g, ((1,), (1,)))
        total, delta = sums(top)
        if later:
            later_columns()
        finish(top, total, delta)
        q2[...] = new_q
        g2[...] = new_g

    @pl.when(step == 0)
    def _():
        work(False)

    @pl.when((step > 0) & (step < steps))
    def _():
        work(True)

    @pl.when(step == steps)
    def _():
        later_rows()
        later_columns()

    @pl.when(new_group & (step > 0))
    def _():
        group = step // per_group - 1
        for total_ref, cols, factor in (
            (dk_sum, key_columns(group), SCALE), (dv_sum, value_columns(group), 1.0)
        ):
            leaf = (total_ref[span:, :HEAD_SIZE] + total_ref[span:, HEAD_SIZE:]) * factor
            dleaf_ref[:, cols] = leaf.astype(jnp.bfloat16)
            for side in range(2):
                lanes = slice(side * HEAD_SIZE, (side + 1) * HEAD_SIZE)
                for j in range(per_prefix):
                    value = total_ref[j * block_len:(j + 1) * block_len, lanes] * factor
                    value = value.astype(jnp.bfloat16)
                    holder, ahead = block_place(side, j)
                    held[holder, ahead, :, cols] += value

        dk_sum[...] = jnp.zeros_like(dk_sum)
        dv_sum[...] = jnp.zeros_like(dv_sum)

    @pl.when(new_group & (step < steps))
    def _():
        kcat_t[...] = kcat[...].T
        vcat_t[...] = vcat[...].T

    @pl.when(step == steps)
    def _():
        copies = [
            pltpu.make_async_copy(held.at[at], total, sems.at[at, 0])
            for at, total in enumerate(totals)
        ]
        for copy in copies:
            copy.start()
        for copy in copies:
            copy.wait()


def attention(
    chunk, owner, tokens, place, q, g, leaf_kv, leaf, mask, sources, earlier, planes, ranks
):
    count = q.shape[0]
    block_len = sources[0].shape[0]
    prompts = tokens.shape[0]
    per_prefix = owner.shape[0] // prompts
    span = per_prefix * block_len
    keys = span + count
    groups = CHUNKS[chunk]
    width = 2 * groups * HEAD_SIZE
    step_heads = STEP_HEADS[chunk]
    skipped = sum(CHUNKS[:chunk])
    heads = groups * GQ
    steps = heads // step_heads
    per_group = GQ // step_heads
    skipped_steps = skipped * per_group
    bf16, f32 = jnp.bfloat16, jnp.float32

    def now(i):
        return jnp.minimum(i, steps - 1)

    ahead = pl.BlockSpec((count, step_heads * HEAD_SIZE), lambda i, *_: (0, skipped_steps + now(i)))
    behind = pl.BlockSpec(
        (count, step_heads * HEAD_SIZE), lambda i, *_: (0, skipped_steps + jnp.maximum(i - 1, 0))
    )
    leaf_k = pl.BlockSpec(
        (count, HEAD_SIZE), lambda i, *_: (0, skipped + now(i) // per_group)
    )
    leaf_v = pl.BlockSpec(
        (count, HEAD_SIZE),
        lambda i, *_: (0, KEY_VALUE_HEADS + skipped + now(i) // per_group),
    )
    anywhere = pl.BlockSpec(memory_space=pl.ANY)

    def full(shape):
        return pl.BlockSpec(shape, lambda h, *_: (0,) * len(shape))

    sum_shape = (planes, block_len, width)
    chained = len(earlier) > 0
    return pl.pallas_call(
        functools.partial(
            attention_kernel, prompts=prompts, per_prefix=per_prefix, block_len=block_len,
            planes=planes, ranks=ranks, chained=chained, steps=steps, step_heads=step_heads,
            first_column=skipped * HEAD_SIZE,
        ),
        grid_spec=pltpu.PrefetchScalarGridSpec(
            num_scalar_prefetch=3,
            grid=(steps + 1,),
            in_specs=[
                ahead, ahead, leaf_k, leaf_v, full(leaf.shape), full(mask.shape),
            ] + [anywhere] * (len(sources) + len(earlier)),
            out_specs=[behind, behind, full((count, width))] + [anywhere] * (2 * ranks),
            scratch_shapes=[
                pltpu.VMEM((2 * ranks, planes * block_len, width), bf16),
                pltpu.VMEM((2 * ranks, *sum_shape), bf16),
                pltpu.VMEM((keys, 2 * HEAD_SIZE), bf16),
                pltpu.VMEM((keys, 2 * HEAD_SIZE), bf16),
                pltpu.VMEM((2 * HEAD_SIZE, keys), bf16),
                pltpu.VMEM((2 * HEAD_SIZE, keys), bf16),
                pltpu.VMEM((count, step_heads * count), f32),
                pltpu.VMEM((count, 2 * HEAD_SIZE), bf16),
                pltpu.VMEM((count, 2 * HEAD_SIZE), bf16),
                pltpu.VMEM((step_heads * count, 2 * HEAD_SIZE), bf16),
                pltpu.VMEM((step_heads * count, 2 * HEAD_SIZE), bf16),
                pltpu.VMEM((keys, step_heads * count), f32),
                pltpu.VMEM((keys, step_heads * count), f32),
                pltpu.VMEM((keys, step_heads * count), bf16),
                pltpu.VMEM((keys, step_heads * count), bf16),
                pltpu.VMEM((keys, 2 * HEAD_SIZE), f32),
                pltpu.VMEM((keys, 2 * HEAD_SIZE), f32),
                pltpu.SemaphoreType.DMA((2 * ranks * planes, 2)),
            ],
        ),
        out_shape=[
            jax.ShapeDtypeStruct(q.shape, bf16),
            jax.ShapeDtypeStruct(q.shape, bf16),
            jax.ShapeDtypeStruct((count, width), bf16),
        ] + [jax.ShapeDtypeStruct(sum_shape, bf16)] * (2 * ranks),
        input_output_aliases={9 + len(sources): 0, 10 + len(sources): 1} if chained else {},
        compiler_params=pltpu.CompilerParams(
            vmem_limit_bytes=54 * 2**20, dimension_semantics=("arbitrary",)
        ),
        cost_estimate=pl.CostEstimate(
            flops=heads * 6 * 2 * keys * 256 * 256, bytes_accessed=groups * 4 * 2**20,
            transcendentals=heads * keys * count,
        ),
    )(owner, tokens, place, q, g, leaf_kv, leaf_kv, leaf, mask, *sources, *earlier)


def shards(
    query, leaf_key_value, prefix_key_value, d_out, block_owner, subtree_tokens, leaf_id, loss_mask
):
    devices = lax.axis_size("dp")
    ranks = 2 if devices == 16 else 1
    planes = devices // (2 * ranks)
    place = lax.axis_index("dp").astype(jnp.int32).reshape(1)
    mask = loss_mask.reshape(1, -1)
    f32 = jnp.float32

    def index(plane, rank, core):
        return (plane % planes * ranks + rank % ranks) * 2 + core % 2

    def send(array, plane_step, rank_step, core_step):
        pairs = [
            (index(p, r, c), index(p + plane_step, r + rank_step, c + core_step))
            for p in range(planes) for r in range(ranks) for c in range(2)
        ]
        return lax.ppermute(array, "dp", pairs)

    def tie(value, *others):
        return lax.optimization_barrier((value, *others))[0]

    def add(own, received):
        return own.astype(f32) + received.astype(f32)

    def reduce_ranks(totals, away):
        total = add(totals[0], send(totals[1], 0, 0, 1))
        return add(total, send(away, 0, 1, 0)) if ranks == 2 else total

    def reduce_planes(total, *begun):
        mine = total[0]
        for k in range(1, planes):
            away = tie(total[k].astype(jnp.bfloat16), *begun)
            mine = add(mine, send(away, k, 0, 0))
        return mine.astype(jnp.bfloat16)

    chunks = len(CHUNKS)
    near, rows = [], []
    for plane in range(planes):
        near.append(send(tie(near[-1], *rows[-2:-1]), 1, 0, 0) if plane else prefix_key_value)
        if ranks == 2:
            rows.append(send(tie(near[-1], *rows[-1:]), 0, 1, 0))
    sources = []
    for held in (near, rows):
        sources += held + [send(piece, 0, 0, 1) for piece in held]
    d_leaf, parts, earlier = [], [], ()
    for chunk in range(chunks):
        first = [place]
        if chunk and ranks == 2:
            first.append(parts[-1][1])
        attended, d_query, leaf_part, *totals = attention(
            chunk, block_owner, subtree_tokens, tie(*first), query, d_out, leaf_key_value,
            leaf_id, mask, sources, earlier, planes, ranks,
        )
        earlier = (attended, d_query)
        d_leaf.append(leaf_part)
        away = add(totals[2], send(totals[3], 0, 0, 1)).astype(jnp.bfloat16) if ranks == 2 else None
        parts.append((totals, away))
    begun = [parts[-1][1]] if ranks == 2 else []
    d_prefix = [reduce_planes(reduce_ranks(*part), *begun) for part in parts[:-1]]
    d_prefix.append(reduce_planes(reduce_ranks(*parts[-1])))
    d_leaf = [tie(part, d_leaf[-1]) for part in d_leaf[:-1]] + d_leaf[-1:]

    def join(parts):
        halves = [jnp.split(p, 2, axis=1) for p in parts]
        return jnp.concatenate([h[0] for h in halves] + [h[1] for h in halves], axis=1)

    return attended, d_query, join(d_leaf), join(d_prefix)


def solution(mesh):
    rows = P(("groups", "dp"), None)
    in_specs = (rows, rows, rows, rows, P("groups"), P("groups"), rows, P(("groups", "dp")))
    return jax.shard_map(
        shards, mesh=mesh, in_specs=in_specs, out_specs=(rows,) * 4, check_vma=False
    )
```

```python
import functools

import jax
import jax.numpy as jnp
from jax import lax
from jax.experimental import pallas as pl
from jax.experimental.pallas import tpu as pltpu
from jax.sharding import PartitionSpec as P

HEAD_SIZE = 128
KEY_VALUE_HEADS = 4
GQ = 8
SCALE = HEAD_SIZE ** (-0.5)
LOG2E = 1.4426950408889634


def dot(a, b, contract):
    return lax.dot_general(a, b, (contract, ((), ())), preferred_element_type=jnp.float32)

CHUNKS = (2, 2)
STEP_HEADS = (4, 4)
PIECE = 32


def attention_kernel(
    owner_ref, tokens_ref, place_ref,
    q_ref, g_ref, leaf_k_ref, leaf_v_ref, leaf_ref, mask_ref, *rest,
    prompts, per_prefix, block_len, planes, ranks, chained, steps, step_heads,
):
    sources = rest[:2 * ranks]
    rest = rest[2 * ranks + 2 * chained:]
    out_ref, dq_ref, dleaf_ref = rest[:3]
    totals = rest[3:3 + 2 * ranks]
    (kv, held, kcat, vcat, kcat_t, vcat_t, bias, q_pick, g_pick, q2, g2, scores, dprob, probs_b, dscore,
     dk_sum, dv_sum, sems) = rest[3 + 2 * ranks:]
    step = pl.program_id(0)
    per_group = GQ // step_heads
    count = q_ref.shape[0]
    columns = step_heads * count
    span = per_prefix * block_len
    keys = span + count
    half = sources[0].shape[1] // 2

    place = place_ref[0]
    first = place * count
    last = first + (count - 1)
    end = jnp.int32(0)
    pair_first = jnp.int32(0)
    pair_last = jnp.int32(0)
    border = jnp.int32(2**30)
    for p in range(prompts):
        end = end + tokens_ref[p]
        pair_first = pair_first + (end <= first).astype(jnp.int32)
        pair_last = pair_last + (end <= last).astype(jnp.int32)
        border = jnp.where(end > first, jnp.minimum(border, end), border)
    border = border - first

    def block_place(side, j):
        prefix = pair_first if side == 0 else pair_last
        owner = owner_ref[prefix * per_prefix + j]
        core = lax.rem(owner + place, 2)
        row = lax.rem(lax.div(owner, 2) + lax.div(place, 2), ranks)
        ahead = lax.rem(lax.div(owner, 2 * ranks) + planes - lax.div(place, 2 * ranks), planes)
        return core + 2 * row, ahead

    def key_columns(group):
        return pl.ds(pl.multiple_of(group * HEAD_SIZE, HEAD_SIZE), HEAD_SIZE)

    def value_columns(group):
        return pl.ds(pl.multiple_of(half + group * HEAD_SIZE, HEAD_SIZE), HEAD_SIZE)

    @pl.when(step == 0)
    def _():
        copies = [
            pltpu.make_async_copy(source, kv.at[at], sems.at[at])
            for at, source in enumerate(sources)
        ]
        for copy in copies:
            copy.start()
        leaf_row = jnp.broadcast_to(leaf_ref[...], (count, count))
        leaf_col = leaf_row.T
        key_at = lax.broadcasted_iota(jnp.int32, (count, count), 0)
        token_at = lax.broadcasted_iota(jnp.int32, (count, count), 1)
        same = (leaf_row == leaf_col) & (key_at <= token_at)
        same = same & ((key_at < border) == (token_at < border))
        allowed_bias = jnp.where(same, 0.0, -1e30).astype(jnp.float32)
        mask_col = jnp.broadcast_to(mask_ref[...], (count, count)).T.astype(jnp.float32)
        in_first = key_at < border
        left = token_at < HEAD_SIZE
        pick = (in_first == left).astype(jnp.float32)
        q_pick[...] = pick.astype(jnp.bfloat16)
        g_pick[...] = (pick * mask_col).astype(jnp.bfloat16)
        for n in range(step_heads):
            bias[:, n * count:(n + 1) * count] = allowed_bias
        for ref in (held, dk_sum, dv_sum):
            ref[...] = jnp.zeros_like(ref)
        for copy in copies:
            copy.wait()

    new_group = lax.rem(step, per_group) == 0

    @pl.when(new_group & (step < steps))
    def _():
        group = step // per_group
        for cat, cols, leaf in (
            (kcat, key_columns(group), leaf_k_ref), (vcat, value_columns(group), leaf_v_ref)
        ):
            for side in range(2):
                lanes = slice(side * HEAD_SIZE, (side + 1) * HEAD_SIZE)
                for j in range(per_prefix):
                    holder, ahead = block_place(side, j)
                    at = lax.rem(planes - ahead, planes) * block_len
                    rows = pl.ds(pl.multiple_of(at, block_len), block_len)
                    cat[j * block_len:(j + 1) * block_len, lanes] = kv[holder, rows, cols]
                cat[span:, lanes] = leaf[...]


    def later_rows():
        dk_sum[...] += dot(dscore[...], q2[...], ((1,), (0,)))
        dv_sum[...] += dot(probs_b[...], g2[...], ((1,), (0,)))

    def later_columns():
        token_at = lax.rem(lax.broadcasted_iota(jnp.int32, (HEAD_SIZE, columns), 1), count)
        first_side = token_at < border
        for source, cat_t, factor, target in (
            (probs_b, vcat_t, 1.0, out_ref), (dscore, kcat_t, SCALE, dq_ref)
        ):
            both = dot(cat_t[...], source[...], ((1,), (0,)))
            mine = jnp.where(first_side, both[:HEAD_SIZE], both[HEAD_SIZE:])
            if factor != 1.0:
                mine = mine * factor
            for n in range(step_heads):
                lanes = slice(n * HEAD_SIZE, (n + 1) * HEAD_SIZE)
                target[:, lanes] = mine[:, n * count:(n + 1) * count].T.astype(jnp.bfloat16)


    def pick(source, chosen):
        parts = []
        for n in range(step_heads):
            part = source[:, n * HEAD_SIZE:(n + 1) * HEAD_SIZE]
            parts.append(jnp.concatenate([part, part], axis=1) * chosen[...])
        return jnp.concatenate(parts, axis=0)

    def fold(value, op):
        value = value.reshape(PIECE // 8, 8, columns)
        total = value[0]
        for n in range(1, PIECE // 8):
            total = op(total, value[n])
        return total

    def score(new_q):
        product = dot(kcat[...], new_q, ((1,), (1,)))
        top = None
        for at in range(0, keys, PIECE):
            piece = product[at:at + PIECE]
            if at >= span:
                piece = piece + bias[at - span:at - span + PIECE, :]
            scores[at:at + PIECE, :] = piece
            piece = fold(piece, jnp.maximum)
            top = piece if top is None else jnp.maximum(top, piece)
        return jnp.max(top, axis=0, keepdims=True)

    def sums(top):
        total = jnp.zeros((8, columns), jnp.float32)
        delta = jnp.zeros((8, columns), jnp.float32)
        for at in range(0, keys, PIECE):
            weight = jnp.exp2((scores[at:at + PIECE, :] - top) * (SCALE * LOG2E))
            total = total + fold(weight, jnp.add)
            delta = delta + fold(weight * dprob[at:at + PIECE, :], jnp.add)
        total = jnp.sum(total, axis=0, keepdims=True)
        return total, jnp.sum(delta, axis=0, keepdims=True) / total

    def finish(top, total, delta):
        shift = jnp.log2(total)
        for at in range(0, keys, PIECE):
            power = (scores[at:at + PIECE, :] - top) * (SCALE * LOG2E)
            probs = jnp.exp2(power - shift)
            probs_b[at:at + PIECE, :] = probs.astype(jnp.bfloat16)
            dscore[at:at + PIECE, :] = (probs * (dprob[at:at + PIECE, :] - delta)).astype(jnp.bfloat16)

    def work(later):
        new_q = pick(q_ref, q_pick)
        new_g = pick(g_ref, g_pick)
        top = score(new_q)
        if later:
            later_rows()
        dprob[...] = dot(vcat[...], new_g, ((1,), (1,)))
        total, delta = sums(top)
        if later:
            later_columns()
        finish(top, total, delta)
        q2[...] = new_q
        g2[...] = new_g

    @pl.when(step == 0)
    def _():
        work(False)

    @pl.when((step > 0) & (step < steps))
    def _():
        work(True)

    @pl.when(step == steps)
    def _():
        later_rows()
        later_columns()

    @pl.when(new_group & (step > 0))
    def _():
        group = step // per_group - 1
        for total_ref, cols, factor in (
            (dk_sum, key_columns(group), SCALE), (dv_sum, value_columns(group), 1.0)
        ):
            leaf = (total_ref[span:, :HEAD_SIZE] + total_ref[span:, HEAD_SIZE:]) * factor
            dleaf_ref[:, cols] = leaf.astype(jnp.bfloat16)
            for side in range(2):
                lanes = slice(side * HEAD_SIZE, (side + 1) * HEAD_SIZE)
                for j in range(per_prefix):
                    value = total_ref[j * block_len:(j + 1) * block_len, lanes] * factor
                    value = value.astype(jnp.bfloat16)
                    holder, ahead = block_place(side, j)
                    held[holder, ahead, :, cols] += value

        dk_sum[...] = jnp.zeros_like(dk_sum)
        dv_sum[...] = jnp.zeros_like(dv_sum)

    @pl.when(new_group & (step < steps))
    def _():
        kcat_t[...] = kcat[...].T
        vcat_t[...] = vcat[...].T

    @pl.when(step == steps)
    def _():
        copies = [
            pltpu.make_async_copy(held.at[at], total, sems.at[at])
            for at, total in enumerate(totals)
        ]
        for copy in copies:
            copy.start()
        for copy in copies:
            copy.wait()


def attention(
    chunk, owner, tokens, place, q, g, leaf_kv, leaf, mask, sources, earlier, planes, ranks
):
    count = q.shape[0]
    block_len = sources[0].shape[0] // planes
    prompts = tokens.shape[0]
    per_prefix = owner.shape[0] // prompts
    span = per_prefix * block_len
    keys = span + count
    width = sources[0].shape[1]
    groups = CHUNKS[chunk]
    step_heads = STEP_HEADS[chunk]
    skipped = sum(CHUNKS[:chunk])
    heads = groups * GQ
    steps = heads // step_heads
    per_group = GQ // step_heads
    skipped_steps = skipped * per_group
    bf16, f32 = jnp.bfloat16, jnp.float32

    def now(i):
        return jnp.minimum(i, steps - 1)

    ahead = pl.BlockSpec((count, step_heads * HEAD_SIZE), lambda i, *_: (0, skipped_steps + now(i)))
    behind = pl.BlockSpec(
        (count, step_heads * HEAD_SIZE), lambda i, *_: (0, skipped_steps + jnp.maximum(i - 1, 0))
    )
    leaf_k = pl.BlockSpec(
        (count, HEAD_SIZE), lambda i, *_: (0, skipped + now(i) // per_group)
    )
    leaf_v = pl.BlockSpec(
        (count, HEAD_SIZE),
        lambda i, *_: (0, KEY_VALUE_HEADS + skipped + now(i) // per_group),
    )
    anywhere = pl.BlockSpec(memory_space=pl.ANY)

    def full(shape):
        return pl.BlockSpec(shape, lambda h, *_: (0,) * len(shape))

    sum_shape = (planes, block_len, width)
    chained = len(earlier) > 0
    return pl.pallas_call(
        functools.partial(
            attention_kernel, prompts=prompts, per_prefix=per_prefix, block_len=block_len,
            planes=planes, ranks=ranks, chained=chained, steps=steps, step_heads=step_heads,
        ),
        grid_spec=pltpu.PrefetchScalarGridSpec(
            num_scalar_prefetch=3,
            grid=(steps + 1,),
            in_specs=[
                ahead, ahead, leaf_k, leaf_v, full(leaf.shape), full(mask.shape),
            ] + [anywhere] * (2 * ranks + len(earlier)),
            out_specs=[behind, behind, full((count, width))] + [anywhere] * (2 * ranks),
            scratch_shapes=[
                pltpu.VMEM((2 * ranks, planes * block_len, width), bf16),
                pltpu.VMEM((2 * ranks, *sum_shape), bf16),
                pltpu.VMEM((keys, 2 * HEAD_SIZE), bf16),
                pltpu.VMEM((keys, 2 * HEAD_SIZE), bf16),
                pltpu.VMEM((2 * HEAD_SIZE, keys), bf16),
                pltpu.VMEM((2 * HEAD_SIZE, keys), bf16),
                pltpu.VMEM((count, step_heads * count), f32),
                pltpu.VMEM((count, 2 * HEAD_SIZE), bf16),
                pltpu.VMEM((count, 2 * HEAD_SIZE), bf16),
                pltpu.VMEM((step_heads * count, 2 * HEAD_SIZE), bf16),
                pltpu.VMEM((step_heads * count, 2 * HEAD_SIZE), bf16),
                pltpu.VMEM((keys, step_heads * count), f32),
                pltpu.VMEM((keys, step_heads * count), f32),
                pltpu.VMEM((keys, step_heads * count), bf16),
                pltpu.VMEM((keys, step_heads * count), bf16),
                pltpu.VMEM((keys, 2 * HEAD_SIZE), f32),
                pltpu.VMEM((keys, 2 * HEAD_SIZE), f32),
                pltpu.SemaphoreType.DMA((2 * ranks,)),
            ],
        ),
        out_shape=[
            jax.ShapeDtypeStruct(q.shape, bf16),
            jax.ShapeDtypeStruct(q.shape, bf16),
            jax.ShapeDtypeStruct((count, width), bf16),
        ] + [jax.ShapeDtypeStruct(sum_shape, bf16)] * (2 * ranks),
        input_output_aliases={9 + 2 * ranks: 0, 10 + 2 * ranks: 1} if chained else {},
        compiler_params=pltpu.CompilerParams(
            vmem_limit_bytes=54 * 2**20, dimension_semantics=("arbitrary",)
        ),
        cost_estimate=pl.CostEstimate(
            flops=heads * 6 * 2 * keys * 256 * 256, bytes_accessed=groups * 4 * 2**20,
            transcendentals=heads * keys * count,
        ),
    )(owner, tokens, place, q, g, leaf_kv, leaf_kv, leaf, mask, *sources, *earlier)


def shards(
    query, leaf_key_value, prefix_key_value, d_out, block_owner, subtree_tokens, leaf_id, loss_mask
):
    devices = lax.axis_size("dp")
    ranks = 2 if devices == 16 else 1
    planes = devices // (2 * ranks)
    place = lax.axis_index("dp").astype(jnp.int32).reshape(1)
    mask = loss_mask.reshape(1, -1)
    f32 = jnp.float32

    def index(plane, rank, core):
        return (plane % planes * ranks + rank % ranks) * 2 + core % 2

    def send(array, plane_step, rank_step, core_step):
        pairs = [
            (index(p, r, c), index(p + plane_step, r + rank_step, c + core_step))
            for p in range(planes) for r in range(ranks) for c in range(2)
        ]
        return lax.ppermute(array, "dp", pairs)

    middle = KEY_VALUE_HEADS * HEAD_SIZE

    def tie(value, *others):
        return lax.optimization_barrier((value, *others))[0]

    def by_planes(chunk):
        low = sum(CHUNKS[:chunk]) * HEAD_SIZE
        high = low + CHUNKS[chunk] * HEAD_SIZE
        mine = jnp.concatenate(
            [prefix_key_value[:, low:high], prefix_key_value[:, middle + low:middle + high]], axis=1
        )
        return jnp.concatenate([mine] + [send(mine, k, 0, 0) for k in range(1, planes)], axis=0)

    def add(own, received):
        return own.astype(f32) + received.astype(f32)

    def reduce_planes(totals, away):
        total = add(totals[0], send(totals[1], 0, 0, 1))
        total = add(total, send(away, 0, 1, 0)) if ranks == 2 else total
        mine = total[0]
        for k in range(1, planes):
            mine = add(mine, send(total[k].astype(jnp.bfloat16), k, 0, 0))
        return mine.astype(jnp.bfloat16)


    def reduce_ranks(totals, away, in_pieces):
        total = add(totals[0], send(totals[1], 0, 0, 1))
        if not in_pieces:
            total = add(total, send(away, 0, 1, 0))
            return total[1::2].astype(jnp.bfloat16), total[0::2]
        odd = add(total[1::2], send(away[1::2], 0, 1, 0)).astype(jnp.bfloat16)
        return odd, add(total[0::2], tie(send(away[0::2], 0, 1, 0), odd))

    def reduce_halves(odd, even, first, second):
        pairs = [
            (index(p, r, c), index(p ^ 1, r, c))
            for p in range(planes) for r in range(ranks) for c in range(2)
        ]
        received = tie(lax.ppermute(odd, "dp", pairs), *first).astype(f32)
        is_odd = lax.bitwise_and(place[0], jnp.int32(2 * ranks)) != 0
        mine = even[0] + jnp.where(is_odd, received[0], received[1])
        rest = even[1] + jnp.where(is_odd, received[1], received[0])
        received = tie(send(rest.astype(jnp.bfloat16), 2, 0, 0), *second)
        return add(mine, received).astype(jnp.bfloat16)

    chunks = len(CHUNKS)
    near = [by_planes(chunk) for chunk in range(chunks)]
    near_far = [send(n, 0, 0, 1) for n in near]
    other = [send(n, 0, 1, 0) for n in near] if ranks == 2 else []
    d_leaf, d_prefix, earlier = [], [], ()
    parts = []
    for chunk in range(chunks):
        first = [place] + near[chunk + 1:chunk + 2] + near_far[chunk + 1:chunk + 2]
        if chunk and ranks == 2:
            first.append(parts[-1][1])
        sources = [near[chunk], near_far[chunk]]
        if ranks == 2:
            row = tie(other[chunk], d_leaf[-1] if chunk else near[1])
            sources += [row, send(row, 0, 0, 1)]
        attended, d_query, leaf_part, *totals = attention(
            chunk, block_owner, subtree_tokens, tie(*first), query, d_out, leaf_key_value,
            leaf_id, mask, sources, earlier, planes, ranks,
        )
        earlier = (attended, d_query)
        d_leaf.append(leaf_part)
        away = add(totals[2], send(totals[3], 0, 0, 1)).astype(jnp.bfloat16) if ranks == 2 else None
        parts.append((totals, away))
    if planes == 4 and ranks == 2:
        away = parts[-1][1]
        odd, even = reduce_ranks(*parts[-1], True)
        d_prefix = [reduce_halves(*reduce_ranks(*part, False), [away], [odd]) for part in parts[:-1]]
        d_prefix.append(reduce_halves(odd, even, [], []))
        d_leaf = [tie(part, odd) for part in d_leaf]
    else:
        d_prefix = [reduce_planes(*part) for part in parts]

    def join(parts):
        halves = [jnp.split(p, 2, axis=1) for p in parts]
        return jnp.concatenate([h[0] for h in halves] + [h[1] for h in halves], axis=1)

    return attended, d_query, join(d_leaf), join(d_prefix)


def solution(mesh):
    rows = P(("groups", "dp"), None)
    in_specs = (rows, rows, rows, rows, P("groups"), P("groups"), rows, P(("groups", "dp")))
    return jax.shard_map(
        shards, mesh=mesh, in_specs=in_specs, out_specs=(rows,) * 4, check_vma=False
    )
```

```python
import functools

import jax
import jax.numpy as jnp
from jax import lax
from jax.experimental import pallas as pl
from jax.experimental.pallas import tpu as pltpu
from jax.sharding import PartitionSpec as P

HEAD_SIZE = 128
KEY_VALUE_HEADS = 4
GQ = 8
SCALE = HEAD_SIZE ** (-0.5)
LOG2E = 1.4426950408889634


def dot(a, b, contract):
    return lax.dot_general(a, b, (contract, ((), ())), preferred_element_type=jnp.float32)

CHUNKS = (2, 2)
STEP_HEADS = (4, 4)
PIECE = 32


def attention_kernel(
    owner_ref, tokens_ref, place_ref,
    q_ref, g_ref, leaf_k_ref, leaf_v_ref, leaf_ref, mask_ref, *rest,
    prompts, per_prefix, block_len, planes, ranks, chained, steps, step_heads,
):
    sources = rest[:2 * ranks]
    rest = rest[2 * ranks + 2 * chained:]
    out_ref, dq_ref, dleaf_ref = rest[:3]
    totals = rest[3:3 + 2 * ranks]
    (kv, held, kcat, vcat, kcat_t, vcat_t, bias, q_pick, g_pick, q2, g2, scores, dprob, probs_b, dscore,
     dk_sum, dv_sum, sems) = rest[3 + 2 * ranks:]
    step = pl.program_id(0)
    per_group = GQ // step_heads
    count = q_ref.shape[0]
    columns = step_heads * count
    span = per_prefix * block_len
    keys = span + count
    half = sources[0].shape[1] // 2

    place = place_ref[0]
    first = place * count
    last = first + (count - 1)
    end = jnp.int32(0)
    pair_first = jnp.int32(0)
    pair_last = jnp.int32(0)
    border = jnp.int32(2**30)
    for p in range(prompts):
        end = end + tokens_ref[p]
        pair_first = pair_first + (end <= first).astype(jnp.int32)
        pair_last = pair_last + (end <= last).astype(jnp.int32)
        border = jnp.where(end > first, jnp.minimum(border, end), border)
    border = border - first

    def block_place(side, j):
        prefix = pair_first if side == 0 else pair_last
        owner = owner_ref[prefix * per_prefix + j]
        core = lax.rem(owner + place, 2)
        row = lax.rem(lax.div(owner, 2) + lax.div(place, 2), ranks)
        ahead = lax.rem(lax.div(owner, 2 * ranks) + planes - lax.div(place, 2 * ranks), planes)
        return core + 2 * row, ahead

    def block_slot(ahead):
        back = lax.rem(planes - ahead, planes)
        if not (planes == 4 and ranks == 2):
            return back
        is_odd = lax.bitwise_and(place, jnp.int32(2 * ranks)) != 0
        last = jnp.where(is_odd, 3, 1)
        near = 2 + (back == last).astype(jnp.int32)
        return jnp.where(lax.rem(back, 2) == 0, lax.div(back, 2), near)

    def key_columns(group):
        return pl.ds(pl.multiple_of(group * HEAD_SIZE, HEAD_SIZE), HEAD_SIZE)

    def value_columns(group):
        return pl.ds(pl.multiple_of(half + group * HEAD_SIZE, HEAD_SIZE), HEAD_SIZE)

    @pl.when(step == 0)
    def _():
        copies = [
            pltpu.make_async_copy(source, kv.at[at], sems.at[at])
            for at, source in enumerate(sources)
        ]
        for copy in copies:
            copy.start()
        leaf_row = jnp.broadcast_to(leaf_ref[...], (count, count))
        leaf_col = leaf_row.T
        key_at = lax.broadcasted_iota(jnp.int32, (count, count), 0)
        token_at = lax.broadcasted_iota(jnp.int32, (count, count), 1)
        same = (leaf_row == leaf_col) & (key_at <= token_at)
        same = same & ((key_at < border) == (token_at < border))
        allowed_bias = jnp.where(same, 0.0, -1e30).astype(jnp.float32)
        mask_col = jnp.broadcast_to(mask_ref[...], (count, count)).T.astype(jnp.float32)
        in_first = key_at < border
        left = token_at < HEAD_SIZE
        pick = (in_first == left).astype(jnp.float32)
        q_pick[...] = pick.astype(jnp.bfloat16)
        g_pick[...] = (pick * mask_col).astype(jnp.bfloat16)
        for n in range(step_heads):
            bias[:, n * count:(n + 1) * count] = allowed_bias
        for ref in (held, dk_sum, dv_sum):
            ref[...] = jnp.zeros_like(ref)
        for copy in copies:
            copy.wait()

    new_group = lax.rem(step, per_group) == 0

    @pl.when(new_group & (step < steps))
    def _():
        group = step // per_group
        for cat, cols, leaf in (
            (kcat, key_columns(group), leaf_k_ref), (vcat, value_columns(group), leaf_v_ref)
        ):
            for side in range(2):
                lanes = slice(side * HEAD_SIZE, (side + 1) * HEAD_SIZE)
                for j in range(per_prefix):
                    holder, ahead = block_place(side, j)
                    at = block_slot(ahead) * block_len
                    rows = pl.ds(pl.multiple_of(at, block_len), block_len)
                    cat[j * block_len:(j + 1) * block_len, lanes] = kv[holder, rows, cols]
                cat[span:, lanes] = leaf[...]


    def later_rows():
        dk_sum[...] += dot(dscore[...], q2[...], ((1,), (0,)))
        dv_sum[...] += dot(probs_b[...], g2[...], ((1,), (0,)))

    def later_columns():
        token_at = lax.rem(lax.broadcasted_iota(jnp.int32, (HEAD_SIZE, columns), 1), count)
        first_side = token_at < border
        for source, cat_t, factor, target in (
            (probs_b, vcat_t, 1.0, out_ref), (dscore, kcat_t, SCALE, dq_ref)
        ):
            both = dot(cat_t[...], source[...], ((1,), (0,)))
            mine = jnp.where(first_side, both[:HEAD_SIZE], both[HEAD_SIZE:])
            if factor != 1.0:
                mine = mine * factor
            for n in range(step_heads):
                lanes = slice(n * HEAD_SIZE, (n + 1) * HEAD_SIZE)
                target[:, lanes] = mine[:, n * count:(n + 1) * count].T.astype(jnp.bfloat16)


    def pick(source, chosen):
        parts = []
        for n in range(step_heads):
            part = source[:, n * HEAD_SIZE:(n + 1) * HEAD_SIZE]
            parts.append(jnp.concatenate([part, part], axis=1) * chosen[...])
        return jnp.concatenate(parts, axis=0)

    def fold(value, op):
        value = value.reshape(PIECE // 8, 8, columns)
        total = value[0]
        for n in range(1, PIECE // 8):
            total = op(total, value[n])
        return total

    def score(new_q):
        product = dot(kcat[...], new_q, ((1,), (1,)))
        top = None
        for at in range(0, keys, PIECE):
            piece = product[at:at + PIECE]
            if at >= span:
                piece = piece + bias[at - span:at - span + PIECE, :]
            scores[at:at + PIECE, :] = piece
            piece = fold(piece, jnp.maximum)
            top = piece if top is None else jnp.maximum(top, piece)
        return jnp.max(top, axis=0, keepdims=True)

    def sums(top):
        total = jnp.zeros((8, columns), jnp.float32)
        delta = jnp.zeros((8, columns), jnp.float32)
        for at in range(0, keys, PIECE):
            weight = jnp.exp2((scores[at:at + PIECE, :] - top) * (SCALE * LOG2E))
            total = total + fold(weight, jnp.add)
            delta = delta + fold(weight * dprob[at:at + PIECE, :], jnp.add)
        total = jnp.sum(total, axis=0, keepdims=True)
        return total, jnp.sum(delta, axis=0, keepdims=True) / total

    def finish(top, total, delta):
        shift = jnp.log2(total)
        for at in range(0, keys, PIECE):
            power = (scores[at:at + PIECE, :] - top) * (SCALE * LOG2E)
            probs = jnp.exp2(power - shift)
            probs_b[at:at + PIECE, :] = probs.astype(jnp.bfloat16)
            dscore[at:at + PIECE, :] = (probs * (dprob[at:at + PIECE, :] - delta)).astype(jnp.bfloat16)

    def work(later):
        new_q = pick(q_ref, q_pick)
        new_g = pick(g_ref, g_pick)
        top = score(new_q)
        if later:
            later_rows()
        dprob[...] = dot(vcat[...], new_g, ((1,), (1,)))
        total, delta = sums(top)
        if later:
            later_columns()
        finish(top, total, delta)
        q2[...] = new_q
        g2[...] = new_g

    @pl.when(step == 0)
    def _():
        work(False)

    @pl.when((step > 0) & (step < steps))
    def _():
        work(True)

    @pl.when(step == steps)
    def _():
        later_rows()
        later_columns()

    @pl.when(new_group & (step > 0))
    def _():
        group = step // per_group - 1
        for total_ref, cols, factor in (
            (dk_sum, key_columns(group), SCALE), (dv_sum, value_columns(group), 1.0)
        ):
            leaf = (total_ref[span:, :HEAD_SIZE] + total_ref[span:, HEAD_SIZE:]) * factor
            dleaf_ref[:, cols] = leaf.astype(jnp.bfloat16)
            for side in range(2):
                lanes = slice(side * HEAD_SIZE, (side + 1) * HEAD_SIZE)
                for j in range(per_prefix):
                    value = total_ref[j * block_len:(j + 1) * block_len, lanes] * factor
                    value = value.astype(jnp.bfloat16)
                    holder, ahead = block_place(side, j)
                    held[holder, ahead, :, cols] += value

        dk_sum[...] = jnp.zeros_like(dk_sum)
        dv_sum[...] = jnp.zeros_like(dv_sum)

    @pl.when(new_group & (step < steps))
    def _():
        kcat_t[...] = kcat[...].T
        vcat_t[...] = vcat[...].T

    @pl.when(step == steps)
    def _():
        copies = [
            pltpu.make_async_copy(held.at[at], total, sems.at[at])
            for at, total in enumerate(totals)
        ]
        for copy in copies:
            copy.start()
        for copy in copies:
            copy.wait()


def attention(
    chunk, owner, tokens, place, q, g, leaf_kv, leaf, mask, sources, earlier, planes, ranks
):
    count = q.shape[0]
    block_len = sources[0].shape[0] // planes
    prompts = tokens.shape[0]
    per_prefix = owner.shape[0] // prompts
    span = per_prefix * block_len
    keys = span + count
    width = sources[0].shape[1]
    groups = CHUNKS[chunk]
    step_heads = STEP_HEADS[chunk]
    skipped = sum(CHUNKS[:chunk])
    heads = groups * GQ
    steps = heads // step_heads
    per_group = GQ // step_heads
    skipped_steps = skipped * per_group
    bf16, f32 = jnp.bfloat16, jnp.float32

    def now(i):
        return jnp.minimum(i, steps - 1)

    ahead = pl.BlockSpec((count, step_heads * HEAD_SIZE), lambda i, *_: (0, skipped_steps + now(i)))
    behind = pl.BlockSpec(
        (count, step_heads * HEAD_SIZE), lambda i, *_: (0, skipped_steps + jnp.maximum(i - 1, 0))
    )
    leaf_k = pl.BlockSpec(
        (count, HEAD_SIZE), lambda i, *_: (0, skipped + now(i) // per_group)
    )
    leaf_v = pl.BlockSpec(
        (count, HEAD_SIZE),
        lambda i, *_: (0, KEY_VALUE_HEADS + skipped + now(i) // per_group),
    )
    anywhere = pl.BlockSpec(memory_space=pl.ANY)

    def full(shape):
        return pl.BlockSpec(shape, lambda h, *_: (0,) * len(shape))

    sum_shape = (planes, block_len, width)
    chained = len(earlier) > 0
    return pl.pallas_call(
        functools.partial(
            attention_kernel, prompts=prompts, per_prefix=per_prefix, block_len=block_len,
            planes=planes, ranks=ranks, chained=chained, steps=steps, step_heads=step_heads,
        ),
        grid_spec=pltpu.PrefetchScalarGridSpec(
            num_scalar_prefetch=3,
            grid=(steps + 1,),
            in_specs=[
                ahead, ahead, leaf_k, leaf_v, full(leaf.shape), full(mask.shape),
            ] + [anywhere] * (2 * ranks + len(earlier)),
            out_specs=[behind, behind, full((count, width))] + [anywhere] * (2 * ranks),
            scratch_shapes=[
                pltpu.VMEM((2 * ranks, planes * block_len, width), bf16),
                pltpu.VMEM((2 * ranks, *sum_shape), bf16),
                pltpu.VMEM((keys, 2 * HEAD_SIZE), bf16),
                pltpu.VMEM((keys, 2 * HEAD_SIZE), bf16),
                pltpu.VMEM((2 * HEAD_SIZE, keys), bf16),
                pltpu.VMEM((2 * HEAD_SIZE, keys), bf16),
                pltpu.VMEM((count, step_heads * count), f32),
                pltpu.VMEM((count, 2 * HEAD_SIZE), bf16),
                pltpu.VMEM((count, 2 * HEAD_SIZE), bf16),
                pltpu.VMEM((step_heads * count, 2 * HEAD_SIZE), bf16),
                pltpu.VMEM((step_heads * count, 2 * HEAD_SIZE), bf16),
                pltpu.VMEM((keys, step_heads * count), f32),
                pltpu.VMEM((keys, step_heads * count), f32),
                pltpu.VMEM((keys, step_heads * count), bf16),
                pltpu.VMEM((keys, step_heads * count), bf16),
                pltpu.VMEM((keys, 2 * HEAD_SIZE), f32),
                pltpu.VMEM((keys, 2 * HEAD_SIZE), f32),
                pltpu.SemaphoreType.DMA((2 * ranks,)),
            ],
        ),
        out_shape=[
            jax.ShapeDtypeStruct(q.shape, bf16),
            jax.ShapeDtypeStruct(q.shape, bf16),
            jax.ShapeDtypeStruct((count, width), bf16),
        ] + [jax.ShapeDtypeStruct(sum_shape, bf16)] * (2 * ranks),
        input_output_aliases={9 + 2 * ranks: 0, 10 + 2 * ranks: 1} if chained else {},
        compiler_params=pltpu.CompilerParams(
            vmem_limit_bytes=54 * 2**20, dimension_semantics=("arbitrary",)
        ),
        cost_estimate=pl.CostEstimate(
            flops=heads * 6 * 2 * keys * 256 * 256, bytes_accessed=groups * 4 * 2**20,
            transcendentals=heads * keys * count,
        ),
    )(owner, tokens, place, q, g, leaf_kv, leaf_kv, leaf, mask, *sources, *earlier)


def shards(
    query, leaf_key_value, prefix_key_value, d_out, block_owner, subtree_tokens, leaf_id, loss_mask
):
    devices = lax.axis_size("dp")
    ranks = 2 if devices == 16 else 1
    planes = devices // (2 * ranks)
    place = lax.axis_index("dp").astype(jnp.int32).reshape(1)
    mask = loss_mask.reshape(1, -1)
    f32 = jnp.float32

    def index(plane, rank, core):
        return (plane % planes * ranks + rank % ranks) * 2 + core % 2

    def send(array, plane_step, rank_step, core_step):
        pairs = [
            (index(p, r, c), index(p + plane_step, r + rank_step, c + core_step))
            for p in range(planes) for r in range(ranks) for c in range(2)
        ]
        return lax.ppermute(array, "dp", pairs)

    neighbours = [
        (index(p, r, c), index(p ^ 1, r, c))
        for p in range(planes) for r in range(ranks) for c in range(2)
    ]
    middle = KEY_VALUE_HEADS * HEAD_SIZE

    def tie(value, *others):
        return lax.optimization_barrier((value, *others))[0]

    def by_planes(chunk):
        low = sum(CHUNKS[:chunk]) * HEAD_SIZE
        high = low + CHUNKS[chunk] * HEAD_SIZE
        mine = jnp.concatenate(
            [prefix_key_value[:, low:high], prefix_key_value[:, middle + low:middle + high]], axis=1
        )
        if planes == 4 and ranks == 2:
            both = jnp.concatenate([mine, send(mine, 2, 0, 0)], axis=0)
            return jnp.concatenate([both, lax.ppermute(both, "dp", neighbours)], axis=0)
        return jnp.concatenate([mine] + [send(mine, k, 0, 0) for k in range(1, planes)], axis=0)

    def add(own, received):
        return own.astype(f32) + received.astype(f32)

    def reduce_planes(totals, away):
        total = add(totals[0], send(totals[1], 0, 0, 1))
        total = add(total, send(away, 0, 1, 0)) if ranks == 2 else total
        mine = total[0]
        for k in range(1, planes):
            mine = add(mine, send(total[k].astype(jnp.bfloat16), k, 0, 0))
        return mine.astype(jnp.bfloat16)


    def reduce_ranks(totals, away, in_pieces):
        total = add(totals[0], send(totals[1], 0, 0, 1))
        if not in_pieces:
            total = add(total, send(away, 0, 1, 0))
            return total[1::2].astype(jnp.bfloat16), total[0::2]
        odd = add(total[1::2], send(away[1::2], 0, 1, 0)).astype(jnp.bfloat16)
        return odd, add(total[0::2], tie(send(away[0::2], 0, 1, 0), odd))

    def reduce_halves(odd, even, first, second):
        received = tie(lax.ppermute(odd, "dp", neighbours), *first).astype(f32)
        is_odd = lax.bitwise_and(place[0], jnp.int32(2 * ranks)) != 0
        mine = even[0] + jnp.where(is_odd, received[0], received[1])
        rest = even[1] + jnp.where(is_odd, received[1], received[0])
        received = tie(send(rest.astype(jnp.bfloat16), 2, 0, 0), *second)
        return add(mine, received).astype(jnp.bfloat16)

    chunks = len(CHUNKS)
    near = [by_planes(chunk) for chunk in range(chunks)]
    near_far = [send(n, 0, 0, 1) for n in near]
    other = [send(n, 0, 1, 0) for n in near] if ranks == 2 else []
    d_leaf, d_prefix, earlier = [], [], ()
    parts = []
    for chunk in range(chunks):
        first = [place] + near[chunk + 1:chunk + 2] + near_far[chunk + 1:chunk + 2]
        if chunk and ranks == 2:
            first.append(parts[-1][1])
        sources = [near[chunk], near_far[chunk]]
        if ranks == 2:
            row = tie(other[chunk], d_leaf[-1] if chunk else near[1])
            sources += [row, send(row, 0, 0, 1)]
        attended, d_query, leaf_part, *totals = attention(
            chunk, block_owner, subtree_tokens, tie(*first), query, d_out, leaf_key_value,
            leaf_id, mask, sources, earlier, planes, ranks,
        )
        earlier = (attended, d_query)
        d_leaf.append(leaf_part)
        away = add(totals[2], send(totals[3], 0, 0, 1)).astype(jnp.bfloat16) if ranks == 2 else None
        parts.append((totals, away))
    if planes == 4 and ranks == 2:
        away = parts[-1][1]
        odd, even = reduce_ranks(*parts[-1], True)
        d_prefix = [reduce_halves(*reduce_ranks(*part, False), [away], [odd]) for part in parts[:-1]]
        d_prefix.append(reduce_halves(odd, even, [], []))
        d_leaf = [tie(part, odd) for part in d_leaf]
    else:
        d_prefix = [reduce_planes(*part) for part in parts]

    def join(parts):
        halves = [jnp.split(p, 2, axis=1) for p in parts]
        return jnp.concatenate([h[0] for h in halves] + [h[1] for h in halves], axis=1)

    return attended, d_query, join(d_leaf), join(d_prefix)


def solution(mesh):
    rows = P(("groups", "dp"), None)
    in_specs = (rows, rows, rows, rows, P("groups"), P("groups"), rows, P(("groups", "dp")))
    return jax.shard_map(
        shards, mesh=mesh, in_specs=in_specs, out_specs=(rows,) * 4, check_vma=False
    )
```

```python
import functools

import jax
import jax.numpy as jnp
from jax import lax
from jax.experimental import pallas as pl
from jax.experimental.pallas import tpu as pltpu
from jax.sharding import PartitionSpec as P

HEAD_SIZE = 128
KEY_VALUE_HEADS = 4
GQ = 8
SCALE = HEAD_SIZE ** (-0.5)
LOG2E = 1.4426950408889634


def dot(a, b, contract):
    return lax.dot_general(a, b, (contract, ((), ())), preferred_element_type=jnp.float32)

CHUNKS = (2, 2)
STEP_HEADS = (4, 4)
PIECE = 32


def attention_kernel(
    owner_ref, tokens_ref, place_ref,
    q_ref, g_ref, leaf_k_ref, leaf_v_ref, leaf_ref, mask_ref, *rest,
    prompts, per_prefix, block_len, planes, ranks, chained, steps, step_heads,
    first_column,
):
    blocks = 2 * ranks * planes
    sources = rest[:blocks]
    rest = rest[blocks + 2 * chained:]
    out_ref, dq_ref, dleaf_ref = rest[:3]
    totals = rest[3:3 + 2 * ranks]
    (kv, held, kcat, vcat, kcat_t, vcat_t, bias, q_pick, g_pick, q2, g2, scores, dprob, probs_b, dscore,
     dk_sum, dv_sum, sems) = rest[3 + 2 * ranks:]
    step = pl.program_id(0)
    per_group = GQ // step_heads
    count = q_ref.shape[0]
    columns = step_heads * count
    span = per_prefix * block_len
    keys = span + count
    half = kv.shape[2] // 2

    place = place_ref[0]
    first = place * count
    last = first + (count - 1)
    end = jnp.int32(0)
    pair_first = jnp.int32(0)
    pair_last = jnp.int32(0)
    border = jnp.int32(2**30)
    for p in range(prompts):
        end = end + tokens_ref[p]
        pair_first = pair_first + (end <= first).astype(jnp.int32)
        pair_last = pair_last + (end <= last).astype(jnp.int32)
        border = jnp.where(end > first, jnp.minimum(border, end), border)
    border = border - first

    def block_place(side, j):
        prefix = pair_first if side == 0 else pair_last
        owner = owner_ref[prefix * per_prefix + j]
        core = lax.rem(owner + place, 2)
        row = lax.rem(lax.div(owner, 2) + lax.div(place, 2), ranks)
        ahead = lax.rem(lax.div(owner, 2 * ranks) + planes - lax.div(place, 2 * ranks), planes)
        return core + 2 * row, ahead

    def key_columns(group):
        return pl.ds(pl.multiple_of(group * HEAD_SIZE, HEAD_SIZE), HEAD_SIZE)

    def value_columns(group):
        return pl.ds(pl.multiple_of(half + group * HEAD_SIZE, HEAD_SIZE), HEAD_SIZE)

    @pl.when(step == 0)
    def _():
        copies = []
        for at, source in enumerate(sources):
            rows = pl.ds(at % planes * block_len, block_len)
            for side in range(2):
                columns_in = pl.ds(first_column + side * (source.shape[1] // 2), half)
                columns_to = pl.ds(side * half, half)
                copies.append(pltpu.make_async_copy(
                    source.at[:, columns_in], kv.at[at // planes, rows, columns_to], sems.at[at, side]
                ))
        for copy in copies:
            copy.start()
        leaf_row = jnp.broadcast_to(leaf_ref[...], (count, count))
        leaf_col = leaf_row.T
        key_at = lax.broadcasted_iota(jnp.int32, (count, count), 0)
        token_at = lax.broadcasted_iota(jnp.int32, (count, count), 1)
        same = (leaf_row == leaf_col) & (key_at <= token_at)
        same = same & ((key_at < border) == (token_at < border))
        allowed_bias = jnp.where(same, 0.0, -1e30).astype(jnp.float32)
        mask_col = jnp.broadcast_to(mask_ref[...], (count, count)).T.astype(jnp.float32)
        in_first = key_at < border
        left = token_at < HEAD_SIZE
        pick = (in_first == left).astype(jnp.float32)
        q_pick[...] = pick.astype(jnp.bfloat16)
        g_pick[...] = (pick * mask_col).astype(jnp.bfloat16)
        for n in range(step_heads):
            bias[:, n * count:(n + 1) * count] = allowed_bias
        for ref in (held, dk_sum, dv_sum):
            ref[...] = jnp.zeros_like(ref)
        for copy in copies:
            copy.wait()

    new_group = lax.rem(step, per_group) == 0

    @pl.when(new_group & (step < steps))
    def _():
        group = step // per_group
        for cat, cols, leaf in (
            (kcat, key_columns(group), leaf_k_ref), (vcat, value_columns(group), leaf_v_ref)
        ):
            for side in range(2):
                lanes = slice(side * HEAD_SIZE, (side + 1) * HEAD_SIZE)
                for j in range(per_prefix):
                    holder, ahead = block_place(side, j)
                    at = lax.rem(planes - ahead, planes) * block_len
                    rows = pl.ds(pl.multiple_of(at, block_len), block_len)
                    cat[j * block_len:(j + 1) * block_len, lanes] = kv[holder, rows, cols]
                cat[span:, lanes] = leaf[...]


    def later_rows():
        dk_sum[...] += dot(dscore[...], q2[...], ((1,), (0,)))
        dv_sum[...] += dot(probs_b[...], g2[...], ((1,), (0,)))

    def later_columns():
        token_at = lax.rem(lax.broadcasted_iota(jnp.int32, (HEAD_SIZE, columns), 1), count)
        first_side = token_at < border
        for source, cat_t, factor, target in (
            (probs_b, vcat_t, 1.0, out_ref), (dscore, kcat_t, SCALE, dq_ref)
        ):
            both = dot(cat_t[...], source[...], ((1,), (0,)))
            mine = jnp.where(first_side, both[:HEAD_SIZE], both[HEAD_SIZE:])
            if factor != 1.0:
                mine = mine * factor
            for n in range(step_heads):
                lanes = slice(n * HEAD_SIZE, (n + 1) * HEAD_SIZE)
                target[:, lanes] = mine[:, n * count:(n + 1) * count].T.astype(jnp.bfloat16)


    def pick(source, chosen):
        parts = []
        for n in range(step_heads):
            part = source[:, n * HEAD_SIZE:(n + 1) * HEAD_SIZE]
            parts.append(jnp.concatenate([part, part], axis=1) * chosen[...])
        return jnp.concatenate(parts, axis=0)

    def fold(value, op):
        value = value.reshape(PIECE // 8, 8, columns)
        total = value[0]
        for n in range(1, PIECE // 8):
            total = op(total, value[n])
        return total

    def score(new_q):
        product = dot(kcat[...], new_q, ((1,), (1,)))
        top = None
        for at in range(0, keys, PIECE):
            piece = product[at:at + PIECE]
            if at >= span:
                piece = piece + bias[at - span:at - span + PIECE, :]
            scores[at:at + PIECE, :] = piece
            piece = fold(piece, jnp.maximum)
            top = piece if top is None else jnp.maximum(top, piece)
        return jnp.max(top, axis=0, keepdims=True)

    def sums(top):
        total = jnp.zeros((8, columns), jnp.float32)
        delta = jnp.zeros((8, columns), jnp.float32)
        for at in range(0, keys, PIECE):
            weight = jnp.exp2((scores[at:at + PIECE, :] - top) * (SCALE * LOG2E))
            total = total + fold(weight, jnp.add)
            delta = delta + fold(weight * dprob[at:at + PIECE, :], jnp.add)
        total = jnp.sum(total, axis=0, keepdims=True)
        return total, jnp.sum(delta, axis=0, keepdims=True) / total

    def finish(top, total, delta):
        shift = jnp.log2(total)
        for at in range(0, keys, PIECE):
            power = (scores[at:at + PIECE, :] - top) * (SCALE * LOG2E)
            probs = jnp.exp2(power - shift)
            probs_b[at:at + PIECE, :] = probs.astype(jnp.bfloat16)
            dscore[at:at + PIECE, :] = (probs * (dprob[at:at + PIECE, :] - delta)).astype(jnp.bfloat16)

    def work(later):
        new_q = pick(q_ref, q_pick)
        new_g = pick(g_ref, g_pick)
        top = score(new_q)
        if later:
            later_rows()
        dprob[...] = dot(vcat[...], new_g, ((1,), (1,)))
        total, delta = sums(top)
        if later:
            later_columns()
        finish(top, total, delta)
        q2[...] = new_q
        g2[...] = new_g

    @pl.when(step == 0)
    def _():
        work(False)

    @pl.when((step > 0) & (step < steps))
    def _():
        work(True)

    @pl.when(step == steps)
    def _():
        later_rows()
        later_columns()

    @pl.when(new_group & (step > 0))
    def _():
        group = step // per_group - 1
        for total_ref, cols, factor in (
            (dk_sum, key_columns(group), SCALE), (dv_sum, value_columns(group), 1.0)
        ):
            leaf = (total_ref[span:, :HEAD_SIZE] + total_ref[span:, HEAD_SIZE:]) * factor
            dleaf_ref[:, cols] = leaf.astype(jnp.bfloat16)
            for side in range(2):
                lanes = slice(side * HEAD_SIZE, (side + 1) * HEAD_SIZE)
                for j in range(per_prefix):
                    value = total_ref[j * block_len:(j + 1) * block_len, lanes] * factor
                    value = value.astype(jnp.bfloat16)
                    holder, ahead = block_place(side, j)
                    held[holder, ahead, :, cols] += value

        dk_sum[...] = jnp.zeros_like(dk_sum)
        dv_sum[...] = jnp.zeros_like(dv_sum)

    @pl.when(new_group & (step < steps))
    def _():
        kcat_t[...] = kcat[...].T
        vcat_t[...] = vcat[...].T

    @pl.when(step == steps)
    def _():
        copies = [
            pltpu.make_async_copy(held.at[at], total, sems.at[at, 0])
            for at, total in enumerate(totals)
        ]
        for copy in copies:
            copy.start()
        for copy in copies:
            copy.wait()


def attention(
    chunk, owner, tokens, place, q, g, leaf_kv, leaf, mask, sources, earlier, planes, ranks
):
    count = q.shape[0]
    block_len = sources[0].shape[0]
    prompts = tokens.shape[0]
    per_prefix = owner.shape[0] // prompts
    span = per_prefix * block_len
    keys = span + count
    groups = CHUNKS[chunk]
    width = 2 * groups * HEAD_SIZE
    step_heads = STEP_HEADS[chunk]
    skipped = sum(CHUNKS[:chunk])
    heads = groups * GQ
    steps = heads // step_heads
    per_group = GQ // step_heads
    skipped_steps = skipped * per_group
    bf16, f32 = jnp.bfloat16, jnp.float32

    def now(i):
        return jnp.minimum(i, steps - 1)

    ahead = pl.BlockSpec((count, step_heads * HEAD_SIZE), lambda i, *_: (0, skipped_steps + now(i)))
    behind = pl.BlockSpec(
        (count, step_heads * HEAD_SIZE), lambda i, *_: (0, skipped_steps + jnp.maximum(i - 1, 0))
    )
    leaf_k = pl.BlockSpec(
        (count, HEAD_SIZE), lambda i, *_: (0, skipped + now(i) // per_group)
    )
    leaf_v = pl.BlockSpec(
        (count, HEAD_SIZE),
        lambda i, *_: (0, KEY_VALUE_HEADS + skipped + now(i) // per_group),
    )
    anywhere = pl.BlockSpec(memory_space=pl.ANY)

    def full(shape):
        return pl.BlockSpec(shape, lambda h, *_: (0,) * len(shape))

    sum_shape = (planes, block_len, width)
    chained = len(earlier) > 0
    return pl.pallas_call(
        functools.partial(
            attention_kernel, prompts=prompts, per_prefix=per_prefix, block_len=block_len,
            planes=planes, ranks=ranks, chained=chained, steps=steps, step_heads=step_heads,
            first_column=skipped * HEAD_SIZE,
        ),
        grid_spec=pltpu.PrefetchScalarGridSpec(
            num_scalar_prefetch=3,
            grid=(steps + 1,),
            in_specs=[
                ahead, ahead, leaf_k, leaf_v, full(leaf.shape), full(mask.shape),
            ] + [anywhere] * (len(sources) + len(earlier)),
            out_specs=[behind, behind, full((count, width))] + [anywhere] * (2 * ranks),
            scratch_shapes=[
                pltpu.VMEM((2 * ranks, planes * block_len, width), bf16),
                pltpu.VMEM((2 * ranks, *sum_shape), bf16),
                pltpu.VMEM((keys, 2 * HEAD_SIZE), bf16),
                pltpu.VMEM((keys, 2 * HEAD_SIZE), bf16),
                pltpu.VMEM((2 * HEAD_SIZE, keys), bf16),
                pltpu.VMEM((2 * HEAD_SIZE, keys), bf16),
                pltpu.VMEM((count, step_heads * count), f32),
                pltpu.VMEM((count, 2 * HEAD_SIZE), bf16),
                pltpu.VMEM((count, 2 * HEAD_SIZE), bf16),
                pltpu.VMEM((step_heads * count, 2 * HEAD_SIZE), bf16),
                pltpu.VMEM((step_heads * count, 2 * HEAD_SIZE), bf16),
                pltpu.VMEM((keys, step_heads * count), f32),
                pltpu.VMEM((keys, step_heads * count), f32),
                pltpu.VMEM((keys, step_heads * count), bf16),
                pltpu.VMEM((keys, step_heads * count), bf16),
                pltpu.VMEM((keys, 2 * HEAD_SIZE), f32),
                pltpu.VMEM((keys, 2 * HEAD_SIZE), f32),
                pltpu.SemaphoreType.DMA((2 * ranks * planes, 2)),
            ],
        ),
        out_shape=[
            jax.ShapeDtypeStruct(q.shape, bf16),
            jax.ShapeDtypeStruct(q.shape, bf16),
            jax.ShapeDtypeStruct((count, width), bf16),
        ] + [jax.ShapeDtypeStruct(sum_shape, bf16)] * (2 * ranks),
        input_output_aliases={9 + len(sources): 0, 10 + len(sources): 1} if chained else {},
        compiler_params=pltpu.CompilerParams(
            vmem_limit_bytes=54 * 2**20, dimension_semantics=("arbitrary",)
        ),
        cost_estimate=pl.CostEstimate(
            flops=heads * 6 * 2 * keys * 256 * 256, bytes_accessed=groups * 4 * 2**20,
            transcendentals=heads * keys * count,
        ),
    )(owner, tokens, place, q, g, leaf_kv, leaf_kv, leaf, mask, *sources, *earlier)


def shards(
    query, leaf_key_value, prefix_key_value, d_out, block_owner, subtree_tokens, leaf_id, loss_mask
):
    devices = lax.axis_size("dp")
    ranks = 2 if devices == 16 else 1
    planes = devices // (2 * ranks)
    place = lax.axis_index("dp").astype(jnp.int32).reshape(1)
    mask = loss_mask.reshape(1, -1)
    f32 = jnp.float32

    def index(plane, rank, core):
        return (plane % planes * ranks + rank % ranks) * 2 + core % 2

    def send(array, plane_step, rank_step, core_step):
        pairs = [
            (index(p, r, c), index(p + plane_step, r + rank_step, c + core_step))
            for p in range(planes) for r in range(ranks) for c in range(2)
        ]
        return lax.ppermute(array, "dp", pairs)

    def tie(value, *others):
        return lax.optimization_barrier((value, *others))[0]

    def add(own, received):
        return own.astype(f32) + received.astype(f32)

    def reduce_planes(totals, away):
        total = add(totals[0], send(totals[1], 0, 0, 1))
        total = add(total, send(away, 0, 1, 0)) if ranks == 2 else total
        mine = total[0]
        for k in range(1, planes):
            mine = add(mine, send(total[k].astype(jnp.bfloat16), k, 0, 0))
        return mine.astype(jnp.bfloat16)


    def reduce_ranks(totals, away, in_pieces):
        total = add(totals[0], send(totals[1], 0, 0, 1))
        if not in_pieces:
            total = add(total, send(away, 0, 1, 0))
            return total[1::2].astype(jnp.bfloat16), total[0::2]
        odd = add(total[1::2], send(away[1::2], 0, 1, 0)).astype(jnp.bfloat16)
        return odd, add(total[0::2], tie(send(away[0::2], 0, 1, 0), odd))

    def reduce_halves(odd, even, first, second):
        pairs = [
            (index(p, r, c), index(p ^ 1, r, c))
            for p in range(planes) for r in range(ranks) for c in range(2)
        ]
        received = tie(lax.ppermute(odd, "dp", pairs), *first).astype(f32)
        is_odd = lax.bitwise_and(place[0], jnp.int32(2 * ranks)) != 0
        mine = even[0] + jnp.where(is_odd, received[0], received[1])
        rest = even[1] + jnp.where(is_odd, received[1], received[0])
        received = tie(send(rest.astype(jnp.bfloat16), 2, 0, 0), *second)
        return add(mine, received).astype(jnp.bfloat16)

    chunks = len(CHUNKS)
    near, rows = [], []
    for plane in range(planes):
        near.append(send(tie(near[-1], *rows[-2:-1]), 1, 0, 0) if plane else prefix_key_value)
        if ranks == 2:
            rows.append(send(tie(near[-1], *rows[-1:]), 0, 1, 0))
    sources = []
    for held in (near, rows):
        sources += held + [send(piece, 0, 0, 1) for piece in held]
    d_leaf, parts, earlier = [], [], ()
    for chunk in range(chunks):
        first = [place]
        if chunk and ranks == 2:
            first.append(parts[-1][1])
        attended, d_query, leaf_part, *totals = attention(
            chunk, block_owner, subtree_tokens, tie(*first), query, d_out, leaf_key_value,
            leaf_id, mask, sources, earlier, planes, ranks,
        )
        earlier = (attended, d_query)
        d_leaf.append(leaf_part)
        away = add(totals[2], send(totals[3], 0, 0, 1)).astype(jnp.bfloat16) if ranks == 2 else None
        parts.append((totals, away))
    if planes == 4 and ranks == 2:
        odd, even = reduce_ranks(*parts[-1], True)
        d_prefix = [reduce_halves(*reduce_ranks(*part, False), [odd], [odd]) for part in parts[:-1]]
        d_prefix.append(reduce_halves(odd, even, [], []))
        d_leaf = [tie(part, odd) for part in d_leaf]
    else:
        d_prefix = [reduce_planes(*part) for part in parts]

    def join(parts):
        halves = [jnp.split(p, 2, axis=1) for p in parts]
        return jnp.concatenate([h[0] for h in halves] + [h[1] for h in halves], axis=1)

    return attended, d_query, join(d_leaf), join(d_prefix)


def solution(mesh):
    rows = P(("groups", "dp"), None)
    in_specs = (rows, rows, rows, rows, P("groups"), P("groups"), rows, P(("groups", "dp")))
    return jax.shard_map(
        shards, mesh=mesh, in_specs=in_specs, out_specs=(rows,) * 4, check_vma=False
    )
```
